32 devices in a mesh: groups: 2 (over y), tensor: 4 (over z), dp: 4 (over x, core).
Axes of the slice: x: 2, y: 2, z: 4, core: 2. Of those that a mesh axis runs over, the one named last changes fastest.
Arguments:
- attention_result: bfloat16 [4096, 8192], P(('groups', 'dp'), 'tensor'), parts along dimension 0, may hold values from -6 to 6
- output_weight: bfloat16 [8192, 8192], P(None, 'tensor'), may hold values from -0.0625 to 0.0625
- adapter_down_weight: bfloat16 [16, 128, 8192], P('dp', 'tensor'), may hold values from -0.0625 to 0.0625
- adapter_up_weight: bfloat16 [16, 128, 8192], P('dp', None, 'tensor'), may hold values from -0.5 to 0.5
- adapter_page_row: int32 [32], P('groups'), parts along dimension 0, may hold values from 0 to 15, as said below
- requests: int32 [8, 6], P(('groups', 'dp')), parts along dimension 0, may hold values from 0 to 15, as said below
- row_request_entry: int32 [4096], P(('groups', 'dp')), parts along dimension 0, may hold values from 0 to 5
- ranks: int32 [16], replicated, may hold values from 16 to 128, as said below
Outputs:
- projected: bfloat16 [4096, 8192], P(('groups', 'dp'), 'tensor'), parts along dimension 0
The draws below stay inside these ranges and needn't reach their ends.
There are 2 independent parts, one for each index of `groups`. The reference program is written for one: setup_inputs(seed, part) draws one part's arguments, and reference() takes and returns one part's arrays. A program takes and returns all parts, laid end to end along the dimension named above; an argument that names none is the same for every part. Nothing has to cross between parts.
Inputs may be any that keep to these rules, and one draw needn't show every extreme that they name: `adapter_page_row`: A permutation of the page rows. `requests`: each list holds 6 different adapters; among them at most 2 have their page with one holder, the holder of adapter a being adapter_page_row[a] // 4, and every list reaches 2 with some holder. `ranks`: some adapter has rank 128.
All inputs are finite; a program needn't handle non-finite values.
Results may differ from the reference program's by a relative error of at most 0.0037.
Values may be sent and summed in bfloat16 or wider, within the bound.
No kernel may reach another device: no remote copies, remote signals or barrier semaphores. Data moves between devices by JAX's collectives and lax.ppermute only.
A program may use at most 192 MiB of HBM per device.

```python
import jax
import jax.numpy as jnp
from jax import lax

MODEL_WIDTH = 8192
ROWS_DEV = 512
PADDED_RANK = 128
ADP = 4
CAP = 2
REQ = 6
ADAPTER_TOTAL = 16
ROWS = 2048
N_DP = 4


def shared_home(key):
    return jax.random.permutation(jax.random.fold_in(key, 11), ADAPTER_TOTAL).astype(jnp.int32)


def draw_adapter_page_row(key, part):
    return shared_home(key)


def draw_requests(key, part):
    home_rows = shared_home(key)
    at_page = jnp.argsort(home_rows, stable=True).astype(jnp.int32)
    key = jax.random.fold_in(key, 2)
    key_list = jax.random.split(key, N_DP)

    def draw_device(dev_key):
        key_pick, key_score, key_favour = jax.random.split(dev_key, 3)
        chosen = jax.vmap(lambda sub_key: jax.random.permutation(sub_key, ADP)[:CAP])(jax.random.split(key_pick, N_DP))
        page_rows = (jnp.arange(N_DP, dtype=jnp.int32)[:, None] * ADP + chosen.astype(jnp.int32)).reshape(-1)
        holder_row = jnp.repeat(jnp.arange(N_DP, dtype=jnp.int32), CAP)
        scores = jax.random.permutation(key_score, N_DP * CAP).astype(jnp.int32)
        favour = jax.random.randint(key_favour, (), 0, N_DP)
        scores = jnp.where(holder_row == favour, scores - 2 * N_DP * CAP, scores)
        ranking = jnp.argsort(scores, stable=True)[:REQ]
        return at_page[page_rows[ranking]]
    return jax.vmap(draw_device)(key_list).astype(jnp.int32)


def draw_ranks(key, part):
    key = jax.random.fold_in(key, 5)
    key_rank, key_full, key_spot = jax.random.split(key, 3)
    drawn = jax.random.randint(key_rank, (ADAPTER_TOTAL,), 16, PADDED_RANK + 1)
    padded = jax.random.randint(key_full, (ADAPTER_TOTAL,), 0, 2)
    drawn = jnp.where(padded == 1, PADDED_RANK, drawn)
    spot = jax.random.randint(key_spot, (), 0, ADAPTER_TOTAL)
    drawn = jnp.where(jnp.arange(ADAPTER_TOTAL) == spot, PADDED_RANK, drawn)
    return drawn.astype(jnp.int32)


def set_ends(values, rng, least, largest):
    dims = values.shape
    place = [jax.random.randint(jax.random.fold_in(rng, axis), (), 0, dims[axis]) for axis in range(len(dims))]
    values = values.at[tuple(place)].set(least)
    longest = dims.index(max(dims))
    place[longest] = (place[longest] + 1) % dims[longest]
    return values.at[tuple(place)].set(largest)


def block_levels(stream_key, extent, cuts, smallest, high):
    gain, own = 1.0, jax.random.fold_in(stream_key, 6)
    for dim, shards_of in cuts:
        steps = jnp.exp(jax.random.uniform(jax.random.fold_in(own, dim), (shards_of,), jnp.float32, smallest / len(cuts), high / len(cuts)))
        gain = gain * jnp.repeat(steps, extent[dim] // shards_of).reshape([-1 if axis == dim else 1 for axis in range(len(extent))])
    return gain


def noise(key, dims, spread, reach, cuts=(), kind=jnp.bfloat16):
    gain = block_levels(key, dims, cuts, -0.22, 0.18) if cuts else 1.0
    values = jax.random.normal(key, dims, jnp.float32) * spread * gain
    return jnp.minimum(jnp.maximum(values, -reach), reach).astype(kind)


def setup_inputs(seed: int = 0, part: int = 0) -> dict:
    keys = jax.random.split(jax.random.key(seed), 9)
    part_keys = jax.random.split(jax.random.fold_in(keys[8], part), 9)
    attention_result = noise(part_keys[0], (ROWS, MODEL_WIDTH), 1.0, 6.0, ((0, 4), (1, 4)))
    output_weight = noise(keys[1], (MODEL_WIDTH, MODEL_WIDTH), MODEL_WIDTH ** -0.5, 0.0625, ((1, 4),))
    adapter_down_weight = noise(keys[2], (ADAPTER_TOTAL, PADDED_RANK, MODEL_WIDTH), MODEL_WIDTH ** -0.5, 0.0625, ((0, 4), (1, 4)))
    adapter_up_weight = noise(keys[3], (ADAPTER_TOTAL, PADDED_RANK, MODEL_WIDTH), PADDED_RANK ** -0.5, 0.5, ((0, 4), (2, 4)))
    adapter_page_row = draw_adapter_page_row(jax.random.fold_in(jax.random.fold_in(keys[8], part), 71), part)
    requests = draw_requests(jax.random.fold_in(jax.random.fold_in(keys[8], part), 71), part)
    row_request_entry = set_ends(jax.random.randint(part_keys[6], (ROWS,), 0, REQ), jax.random.fold_in(part_keys[6], 1), 0, REQ - 1).astype(jnp.int32)
    ranks = draw_ranks(jax.random.fold_in(keys[8], 71), part)
    return dict(attention_result=attention_result, output_weight=output_weight, adapter_down_weight=adapter_down_weight, adapter_up_weight=adapter_up_weight, adapter_page_row=adapter_page_row, requests=requests, row_request_entry=row_request_entry, ranks=ranks)


def reference(attention_result, output_weight, adapter_down_weight, adapter_up_weight, adapter_page_row, requests, row_request_entry, ranks):
    row_owner = jnp.arange(ROWS, dtype=jnp.int32) // ROWS_DEV
    adapter = requests[row_owner, row_request_entry]
    page_of_row = adapter_page_row[adapter]
    base_term = jnp.dot(attention_result, output_weight, preferred_element_type=jnp.float32)

    def add_down(totals, current_page_row):
        down_page_rows = adapter_down_weight[current_page_row]
        projected = jnp.dot(attention_result, down_page_rows.T, preferred_element_type=jnp.float32)
        return totals + jnp.where((page_of_row == current_page_row)[:, None], projected, jnp.zeros_like(projected)), None

    low_sum, _ = lax.scan(add_down, jnp.zeros((ROWS, PADDED_RANK), jnp.float32), jnp.arange(ADAPTER_TOTAL, dtype=jnp.int32))
    low_rank = low_sum.astype(jnp.bfloat16)
    live_mask = jnp.arange(PADDED_RANK, dtype=jnp.int32)[None, :] < ranks[adapter][:, None]
    masked = jnp.where(live_mask, low_rank, jnp.zeros_like(low_rank))

    def add_up(totals, current_page_row):
        up_page_rows = adapter_up_weight[current_page_row]
        term = jnp.dot(masked, up_page_rows, preferred_element_type=jnp.float32)
        return totals + jnp.where((page_of_row == current_page_row)[:, None], term, jnp.zeros_like(term)), None

    low_term, _ = lax.scan(add_up, jnp.zeros((ROWS, MODEL_WIDTH), jnp.float32), jnp.arange(ADAPTER_TOTAL, dtype=jnp.int32))
    return (base_term + low_term).astype(jnp.bfloat16)
```

```python
import jax
import jax.numpy as jnp
from jax import lax
from jax.sharding import PartitionSpec as P

ROW_CHUNKS = 2


def gather_pages(block, n_dp):
    held = block[None]
    step = n_dp // 2
    while step:
        pairs = [(i, i ^ step) for i in range(n_dp)]
        held = jnp.stack([held, lax.ppermute(held, "dp", pairs)], axis=1)
        held = held.reshape((-1,) + block.shape)
        step //= 2
    return held


def local(
    attention_result,
    output_weight,
    adapter_down_weight,
    adapter_up_weight,
    adapter_page_row,
    requests,
    row_request_entry,
    ranks,
):
    n_dp = lax.axis_size("dp")
    n_tensor = lax.axis_size("tensor")
    dp = lax.axis_index("dp")
    me = lax.axis_index("tensor")
    row_count, width = attention_result.shape
    holder_length, rank_part, _ = adapter_down_weight.shape
    rank_complete, output_columns = adapter_up_weight.shape[1:]
    own_list = requests[0]
    entries = own_list.shape[0]
    chunk_rows = row_count // ROW_CHUNKS

    pages = adapter_page_row[own_list]
    places = ((pages // holder_length) ^ dp) * holder_length + pages % holder_length

    def requested(block):
        every = gather_pages(block, n_dp).reshape((-1,) + block.shape[1:])
        return jnp.concatenate(
            [lax.dynamic_slice_in_dim(every, places[e], 1, 0) for e in range(entries)], axis=0
        )

    down = requested(adapter_down_weight).reshape(entries * rank_part, -1)
    up = requested(adapter_up_weight).reshape(entries * rank_complete, output_columns)

    base = [jnp.zeros((chunk_rows, output_columns), jnp.float32)] * ROW_CHUNKS
    low = [jnp.zeros((chunk_rows, entries * rank_part), jnp.float32)] * ROW_CHUNKS

    def add(c, features, source):
        start = jnp.clip(source, 0, n_tensor - 1) * width
        weight = lax.dynamic_slice_in_dim(output_weight, start, width, 0)
        down_part = lax.dynamic_slice_in_dim(down, start, width, 1)
        base[c] = base[c] + jnp.dot(features, weight, preferred_element_type=jnp.float32)
        low[c] = low[c] + lax.dot_general(
            features, down_part, (((1,), (1,)), ((), ())), preferred_element_type=jnp.float32
        )

    own = [attention_result[c * chunk_rows:(c + 1) * chunk_rows] for c in range(ROW_CHUNKS)]
    from_left, from_right = list(own), list(own)
    for c in range(ROW_CHUNKS):
        add(c, own[c], me)
    for s in range(1, n_tensor):
        right = [(i, i + 1) for i in range(s - 1, n_tensor - 1)]
        left = [(i, i - 1) for i in range(1, n_tensor - s + 1)]
        for c in range(ROW_CHUNKS):
            if s > n_tensor // 2:
                merged = jnp.where(me >= s - 1, from_left[c], from_right[c])
                merged = lax.ppermute(merged, "tensor", right + left)
                from_left[c] = from_right[c] = merged
                add(c, merged, jnp.where(me >= s, me - s, me + s))
            else:
                from_left[c] = lax.ppermute(from_left[c], "tensor", right)
                from_right[c] = lax.ppermute(from_right[c], "tensor", left)
                add(c, from_left[c], me - s)
                add(c, from_right[c], me + s)

    outs = []
    for c in range(ROW_CHUNKS):
        entry = row_request_entry[c * chunk_rows:(c + 1) * chunk_rows]
        one_hot = entry[:, None] == jnp.arange(entries)[None, :]
        row_rank = jnp.sum(jnp.where(one_hot, ranks[own_list][None, :], 0), axis=1)
        low_mine = jnp.sum(
            jnp.where(one_hot[:, :, None], low[c].reshape(chunk_rows, entries, rank_part), 0.0), axis=1
        ).astype(jnp.bfloat16)
        low_full = lax.all_gather(low_mine, "tensor", axis=1, tiled=True)
        live = jnp.arange(rank_complete)[None, :] < row_rank[:, None]
        masked = jnp.where(live, low_full, jnp.zeros_like(low_full))
        spread = jnp.where(one_hot[:, :, None], masked[:, None, :], jnp.zeros((), jnp.bfloat16))
        low_term = jnp.dot(
            spread.reshape(chunk_rows, entries * rank_complete), up, preferred_element_type=jnp.float32
        )
        outs.append((base[c] + low_term).astype(jnp.bfloat16))
    return jnp.concatenate(outs, axis=0)


def solution(mesh):
    in_specs = (
        P(("groups", "dp"), "tensor"),
        P(None, "tensor"),
        P("dp", "tensor", None),
        P("dp", None, "tensor"),
        P("groups"),
        P(("groups", "dp"), None),
        P(("groups", "dp")),
        P(),
    )
    out_specs = P(("groups", "dp"), "tensor")
    return jax.shard_map(local, mesh=mesh, in_specs=in_specs, out_specs=out_specs, check_vma=False)
```

```python
import functools

import jax
import jax.numpy as jnp
from jax import lax
from jax.experimental import pallas as pl
from jax.experimental.pallas import tpu as pltpu
from jax.sharding import PartitionSpec as P

PARAMS = pltpu.CompilerParams(vmem_limit_bytes=40 * 2**20)
F32 = jnp.float32
BF16 = jnp.bfloat16


def gather_pages(block, n_dp):
    held = {0: block}
    step = n_dp // 2
    while step:
        pairs = [(i, i ^ step) for i in range(n_dp)]
        held.update({j | step: lax.ppermute(b, "dp", pairs) for j, b in held.items()})
        step //= 2
    return [held[j] for j in range(n_dp)]


def pick_kernel(length, places, *refs):
    *blocks, out, sems = refs
    entries = out.shape[0]
    for e in range(entries):
        for j, block in enumerate(blocks):

            @pl.when(places[e] // length == j)
            def _():
                pltpu.make_async_copy(block.at[places[e] % length], out.at[e], sems.at[e]).start()

    for e in range(entries):
        pltpu.make_async_copy(blocks[0].at[0], out.at[e], sems.at[e]).wait()


def pick_pages(places, blocks):
    entries = places.shape[0]
    length, rows, columns = blocks[0].shape
    return pl.pallas_call(
        functools.partial(pick_kernel, length),
        out_shape=jax.ShapeDtypeStruct((entries, rows, columns), BF16),
        in_specs=[pl.BlockSpec(memory_space=pltpu.SMEM)] + [pl.BlockSpec(memory_space=pl.ANY)] * len(blocks),
        out_specs=pl.BlockSpec(memory_space=pl.ANY),
        scratch_shapes=[pltpu.SemaphoreType.DMA((entries,))],
        cost_estimate=pl.CostEstimate(flops=0, bytes_accessed=4 * entries * rows * columns, transcendentals=0),
    )(places, *blocks)


def base_kernel(has_total, x, weight, *refs):
    out = refs[-1]
    columns = out.shape[1]
    part = min(columns, 512)

    @pl.when(pl.program_id(0) == 0)
    def _():
        out[...] = refs[0][...] if has_total else jnp.zeros_like(out)

    for n in range(0, columns, part):
        out[:, n:n + part] += jnp.dot(x[0], weight[0, :, n:n + part], preferred_element_type=F32)


def add_base(total, x, weight, k):
    shards, rows, features = x.shape
    columns = weight.shape[-1]
    held = [] if total is None else [total]
    whole = pl.BlockSpec((rows, columns), lambda t: (0, 0))
    return pl.pallas_call(
        functools.partial(base_kernel, bool(held)),
        grid=(shards,),
        out_shape=jax.ShapeDtypeStruct((rows, columns), F32),
        in_specs=[
            pl.BlockSpec((1, rows, features), lambda t: (t, 0, 0)),
            pl.BlockSpec((1, features, columns), lambda t: (t, k, 0)),
        ] + [whole] * len(held),
        out_specs=whole,
        compiler_params=PARAMS,
        cost_estimate=pl.CostEstimate(
            flops=2 * shards * rows * features * columns,
            bytes_accessed=2 * shards * features * (rows + columns) + 8 * rows * columns,
            transcendentals=0,
        ),
    )(x, weight, *held)


def low_kernel(has_total, last, rank_part, x, down, *refs):
    refs = list(refs)
    total = refs.pop(0) if has_total else None
    step = pl.program_id(0)
    out = refs[-1]
    acc = out if not last else refs.pop()
    if last:
        out = refs[-1]

    @pl.when(step == 0)
    def _():
        acc[...] = total[...] if has_total else jnp.zeros_like(acc)

    acc[...] += lax.dot_general(x[0], down[...], (((1,), (1,)), ((), ())), preferred_element_type=F32)
    if last:
        entry, live = refs[0], refs[1]

        @pl.when(step == pl.num_programs(0) - 1)
        def _():
            mine = jnp.zeros((acc.shape[0], rank_part), F32)
            for e in range(acc.shape[1] // rank_part):
                mine += jnp.where(entry[...] == e, acc[:, e * rank_part:(e + 1) * rank_part], 0.0)
            k = lax.broadcasted_iota(jnp.int32, mine.shape, 1)
            out[...] = jnp.where(k < live[...], mine.astype(BF16).astype(F32), 0.0).astype(BF16)


def add_low(total, x, down, k, chunks, rank_part, entry=None, live=None):
    shards, rows, features = x.shape
    ranks = down.shape[0]
    last = entry is not None
    held = [] if total is None else [total]
    whole = pl.BlockSpec((rows, ranks), lambda t: (0, 0))
    column = pl.BlockSpec((rows, 1), lambda t: (0, 0))
    return pl.pallas_call(
        functools.partial(low_kernel, bool(held), last, rank_part),
        grid=(shards,),
        out_shape=jax.ShapeDtypeStruct((rows, rank_part), BF16) if last else jax.ShapeDtypeStruct((rows, ranks), F32),
        in_specs=[
            pl.BlockSpec((1, rows, features), lambda t: (t, 0, 0)),
            pl.BlockSpec((ranks, features), lambda t: (0, t * chunks + k)),
        ] + [whole] * len(held) + ([column, column] if last else []),
        out_specs=pl.BlockSpec((rows, rank_part), lambda t: (0, 0)) if last else whole,
        scratch_shapes=[pltpu.VMEM((rows, ranks), F32)] if last else [],
        compiler_params=PARAMS,
        cost_estimate=pl.CostEstimate(
            flops=2 * shards * rows * features * ranks,
            bytes_accessed=2 * shards * features * (rows + ranks) + 8 * rows * ranks,
            transcendentals=0,
        ),
    )(x, down, *held, *([entry, live] if last else []))


def finish_kernel(parts, me, entry, total, up, *refs):
    lows, (out, spread) = refs[:parts], refs[parts:]
    rank_part = lows[0].shape[1]
    rank = parts * rank_part

    @pl.when(pl.program_id(0) == 0)
    def _():
        low = jnp.concatenate([part[...].astype(F32) for part in lows], axis=1)
        low = pltpu.roll(low, me[0] * rank_part, 1)
        for e in range(up.shape[0] // rank):
            spread[:, e * rank:(e + 1) * rank] = jnp.where(entry[...] == e, low, 0.0).astype(BF16)

    term = jnp.dot(spread[...], up[...], preferred_element_type=F32)
    out[...] = (total[...] + term).astype(BF16)


def finish(me, entry, total, up, lows):
    rows, columns = total.shape
    depth = up.shape[0]
    rank_part = lows[0].shape[1]
    part = min(columns, 512)
    return pl.pallas_call(
        functools.partial(finish_kernel, len(lows)),
        grid=(columns // part,),
        out_shape=jax.ShapeDtypeStruct((rows, columns), BF16),
        in_specs=[
            pl.BlockSpec(memory_space=pltpu.SMEM),
            pl.BlockSpec((rows, 1), lambda n: (0, 0)),
            pl.BlockSpec((rows, part), lambda n: (0, n)),
            pl.BlockSpec((depth, part), lambda n: (0, n)),
        ] + [pl.BlockSpec((rows, rank_part), lambda n: (0, 0))] * len(lows),
        out_specs=pl.BlockSpec((rows, part), lambda n: (0, n)),
        scratch_shapes=[pltpu.VMEM((rows, depth), BF16)],
        compiler_params=PARAMS,
        cost_estimate=pl.CostEstimate(
            flops=2 * rows * depth * columns,
            bytes_accessed=6 * rows * columns + 2 * depth * columns,
            transcendentals=0,
        ),
    )(me, entry, total, up, *lows)


def local(
    attention_result,
    output_weight,
    adapter_down_weight,
    adapter_up_weight,
    adapter_page_row,
    requests,
    row_request_entry,
    ranks,
):
    n_dp = lax.axis_size("dp")
    n_tensor = lax.axis_size("tensor")
    dp = lax.axis_index("dp")
    me = lax.axis_index("tensor")
    rows, width = attention_result.shape
    holder_length, rank_part, _ = adapter_down_weight.shape
    rank, columns = adapter_up_weight.shape[1:]
    own_list = requests[0]
    entries = own_list.shape[0]
    pages = adapter_page_row[own_list]
    places = ((pages // holder_length) ^ dp) * holder_length + pages % holder_length
    one_hot = row_request_entry[:, None] == jnp.arange(entries)[None, :]
    row_rank = jnp.sum(jnp.where(one_hot, ranks[own_list][None, :], 0), axis=1)

    if width % 512 or rank_part % 16:
        return plain(
            attention_result, output_weight, adapter_down_weight, adapter_up_weight, places, one_hot, row_rank
        )

    chunks = 4
    features = width // chunks
    gathered = [
        lax.all_gather(attention_result[:, k * features:(k + 1) * features], "tensor", axis=0)
        for k in range(chunks)
    ]
    weight = output_weight.reshape(n_tensor, width, columns)
    down_blocks = gather_pages(adapter_down_weight, n_dp)
    up_own = lax.optimization_barrier((adapter_up_weight, down_blocks[n_dp // 2]))[0]
    up_blocks = gather_pages(up_own, n_dp)
    down = pick_pages(places, down_blocks).reshape(entries * rank_part, -1)
    up = pick_pages(places, up_blocks).reshape(entries * rank, columns)

    entry = row_request_entry[:, None]
    live = row_rank[:, None] - me * rank_part
    base = low = None
    for k in range(chunks):
        ends = dict(entry=entry, live=live) if k == chunks - 1 else {}
        low = add_low(low, gathered[k], down, k, chunks, rank_part, **ends)
        base = add_base(base, gathered[k], weight, k)
    lows = [low] + [
        lax.ppermute(low, "tensor", [(i, (i - j) % n_tensor) for i in range(n_tensor)])
        for j in range(1, n_tensor)
    ]
    return finish(me[None], entry, base, up, lows)


def plain(attention_result, output_weight, adapter_down_weight, adapter_up_weight, places, one_hot, row_rank):
    n_dp = lax.axis_size("dp")
    rows = attention_result.shape[0]
    rank, columns = adapter_up_weight.shape[1:]
    entries = one_hot.shape[1]

    def requested(block):
        every = jnp.concatenate(gather_pages(block, n_dp), axis=0)
        return jnp.concatenate(
            [lax.dynamic_slice_in_dim(every, places[e], 1, 0) for e in range(entries)], axis=0
        )

    down, up = requested(adapter_down_weight), requested(adapter_up_weight)
    x = lax.all_gather(attention_result, "tensor", axis=1, tiled=True)
    base = jnp.dot(x, output_weight, preferred_element_type=F32)
    low = jnp.einsum("rd,ekd->rek", x, down, preferred_element_type=F32)
    low = jnp.sum(jnp.where(one_hot[:, :, None], low, 0.0), axis=1).astype(BF16)
    low = lax.all_gather(low, "tensor", axis=1, tiled=True)
    low = jnp.where(jnp.arange(rank)[None, :] < row_rank[:, None], low, jnp.zeros_like(low))
    spread = jnp.where(one_hot[:, :, None], low[:, None, :], jnp.zeros((), BF16))
    term = jnp.dot(
        spread.reshape(rows, entries * rank), up.reshape(entries * rank, columns), preferred_element_type=F32
    )
    return (base + term).astype(BF16)


def solution(mesh):
    in_specs = (
        P(("groups", "dp"), "tensor"),
        P(None, "tensor"),
        P("dp", "tensor", None),
        P("dp", None, "tensor"),
        P("groups"),
        P(("groups", "dp"), None),
        P(("groups", "dp")),
        P(),
    )
    out_specs = P(("groups", "dp"), "tensor")
    return jax.shard_map(local, mesh=mesh, in_specs=in_specs, out_specs=out_specs, check_vma=False)
```

```python
import functools

import jax
import jax.numpy as jnp
from jax import lax
from jax.experimental import pallas as pl
from jax.experimental.pallas import tpu as pltpu
from jax.sharding import PartitionSpec as P

CAP = 2
UNIT = 256
LINE = 512
GATHERED = (768, 768)
PARAMS = pltpu.CompilerParams(vmem_limit_bytes=60 * 2**20)
F32 = jnp.float32
BF16 = jnp.bfloat16


def pick_kernel(places, down, up, down_out, up_out):
    down_out[...] = down[...]
    up_out[...] = up[...]


def pick_pages(places, down, up):
    count = places.shape[0]
    blocks = [(1,) + a.shape[1:] for a in (down, up)]
    return pl.pallas_call(
        pick_kernel,
        out_shape=[jax.ShapeDtypeStruct((count,) + a.shape[1:], BF16) for a in (down, up)],
        grid_spec=pltpu.PrefetchScalarGridSpec(
            num_scalar_prefetch=1,
            grid=(count,),
            in_specs=[pl.BlockSpec(b, lambda i, places: (places[i], 0, 0)) for b in blocks],
            out_specs=[pl.BlockSpec(b, lambda i, places: (i, 0, 0)) for b in blocks],
        ),
        compiler_params=PARAMS,
    )(places, down, up)


def steps_of(xs):
    return sum(x.shape[0] for x in xs)


def x_specs(xs):
    specs, first = [], 0
    for x in xs:
        units = x.shape[2] // UNIT

        def index(s, j, *_, first=first, count=x.shape[0], units=units):
            shard = jnp.clip(s - first, 0, count - 1)
            return shard, 0, jnp.where(s < first, 0, jnp.where(s >= first + count, units - 1, j))

        specs.append(pl.BlockSpec((1, x.shape[1], UNIT), index))
        first += x.shape[0]
    return specs


def for_block(xs, counts, valid, body):
    s, first = pl.program_id(0), 0
    for x, count in zip(xs, counts):

        @pl.when((s >= first) & (s < first + count) & (valid[s] != 0))
        def _():
            body(x[0])

        first += count


def start_total(out, total):
    @pl.when((pl.program_id(0) == 0) & (pl.program_id(1) == 0))
    def _():
        out[...] = jnp.zeros_like(out) if total is None else total[...]


def base_kernel(counts, has_total, source, valid, *refs):
    xs, weight, out = refs[:len(counts)], refs[len(counts)], refs[-1]
    start_total(out, refs[-2] if has_total else None)
    columns = out.shape[1]
    part = min(columns, 512)

    def body(x):
        for n in range(0, columns, part):
            out[:, n:n + part] += jnp.dot(x, weight[0, :, n:n + part], preferred_element_type=F32)

    for_block(xs, counts, valid, body)


def add_base(total, xs, source, valid, offset, weight):
    rows, features = xs[0].shape[1:]
    columns = weight.shape[-1]
    held = [] if total is None else [total]
    whole = pl.BlockSpec((rows, columns), lambda s, j, *_: (0, 0))
    steps = steps_of(xs)
    return pl.pallas_call(
        functools.partial(base_kernel, [x.shape[0] for x in xs], bool(held)),
        out_shape=jax.ShapeDtypeStruct((rows, columns), F32),
        grid_spec=pltpu.PrefetchScalarGridSpec(
            num_scalar_prefetch=2,
            grid=(steps, features // UNIT),
            in_specs=x_specs(xs) + [
                pl.BlockSpec((1, UNIT, columns), lambda s, j, source, valid: (source[s], offset // UNIT + j, 0))
            ] + [whole] * len(held),
            out_specs=whole,
        ),
        compiler_params=PARAMS,
        cost_estimate=pl.CostEstimate(
            flops=2 * steps * rows * features * columns,
            bytes_accessed=2 * steps * features * (rows + columns) + 8 * rows * columns,
            transcendentals=0,
        ),
    )(source, valid, *xs, weight, *held)


def low_kernel(counts, parts, has_total, last, rank_part, source, valid, *refs):
    refs = list(refs)
    xs = [refs.pop(0) for _ in counts]
    downs = [refs.pop(0) for _ in range(parts)]
    total = refs.pop(0) if has_total else None
    acc = refs.pop()
    start_total(acc, total)

    def body(x):
        down = jnp.concatenate([d[...] for d in downs], axis=0)
        acc[...] += lax.dot_general(x, down, (((1,), (1,)), ((), ())), preferred_element_type=F32)

    for_block(xs, counts, valid, body)
    if last:
        slot, live, out = refs

        @pl.when((pl.program_id(0) == pl.num_programs(0) - 1) & (pl.program_id(1) == pl.num_programs(1) - 1))
        def _():
            mine = jnp.zeros((acc.shape[0], rank_part), F32)
            for e in range(acc.shape[1] // rank_part):
                mine += jnp.where(slot[...] == e, acc[:, e * rank_part:(e + 1) * rank_part], 0.0)
            k = lax.broadcasted_iota(jnp.int32, mine.shape, 1)
            out[...] = jnp.where(k < live[...], mine, 0.0).astype(BF16)


def add_low(total, xs, source, valid, offset, downs, rank_part, ends=()):
    rows, features = xs[0].shape[1:]
    shard_units = downs[0].shape[1] // lax.axis_size("tensor") // UNIT
    depth = downs[0].shape[0]
    ranks = depth * len(downs)
    held = [] if total is None else [total]
    whole = pl.BlockSpec((rows, ranks), lambda s, j, *_: (0, 0))
    column = pl.BlockSpec((rows, 1), lambda s, j, *_: (0, 0))
    steps = steps_of(xs)
    down_spec = pl.BlockSpec(
        (depth, UNIT), lambda s, j, source, valid: (0, source[s] * shard_units + offset // UNIT + j)
    )
    return pl.pallas_call(
        functools.partial(low_kernel, [x.shape[0] for x in xs], len(downs), bool(held), bool(ends), rank_part),
        out_shape=jax.ShapeDtypeStruct((rows, rank_part), BF16) if ends else jax.ShapeDtypeStruct((rows, ranks), F32),
        grid_spec=pltpu.PrefetchScalarGridSpec(
            num_scalar_prefetch=2,
            grid=(steps, features // UNIT),
            in_specs=x_specs(xs) + [down_spec] * len(downs) + [whole] * len(held) + [column] * len(ends),
            out_specs=pl.BlockSpec((rows, rank_part), lambda s, j, *_: (0, 0)) if ends else whole,
            scratch_shapes=[pltpu.VMEM((rows, ranks), F32)] if ends else [],
        ),
        compiler_params=PARAMS,
        cost_estimate=pl.CostEstimate(
            flops=2 * steps * rows * features * ranks,
            bytes_accessed=2 * steps * features * (rows + ranks) + 8 * rows * ranks,
            transcendentals=0,
        ),
    )(source, valid, *xs, *downs, *held, *ends)


def finish_kernel(parts, holders, me, slot, total, *refs):
    lows, ups, (out, spread) = refs[:parts], refs[parts:parts + holders], refs[parts + holders:]
    rank_part = lows[0].shape[1]
    rank = parts * rank_part
    depth = ups[0].shape[0]

    @pl.when(pl.program_id(0) == 0)
    def _():
        low = jnp.concatenate([part[...].astype(F32) for part in lows], axis=1)
        low = pltpu.roll(low, me[0] * rank_part, 1)
        for e in range(spread.shape[1] // rank):
            spread[:, e * rank:(e + 1) * rank] = jnp.where(slot[...] == e, low, 0.0).astype(BF16)

    term = total[...]
    for j, up in enumerate(ups):
        term += jnp.dot(spread[:, j * depth:(j + 1) * depth], up[...], preferred_element_type=F32)
    out[...] = term.astype(BF16)


def finish(me, slot, total, ups, lows):
    rows, columns = total.shape
    depth = ups[0].shape[0]
    rank_part = lows[0].shape[1]
    part = min(columns, 512)
    return pl.pallas_call(
        functools.partial(finish_kernel, len(lows), len(ups)),
        grid=(columns // part,),
        out_shape=jax.ShapeDtypeStruct((rows, columns), BF16),
        in_specs=[
            pl.BlockSpec(memory_space=pltpu.SMEM),
            pl.BlockSpec((rows, 1), lambda n: (0, 0)),
            pl.BlockSpec((rows, part), lambda n: (0, n)),
        ] + [pl.BlockSpec((rows, rank_part), lambda n: (0, 0))] * len(lows)
        + [pl.BlockSpec((depth, part), lambda n: (0, n))] * len(ups),
        out_specs=pl.BlockSpec((rows, part), lambda n: (0, n)),
        scratch_shapes=[pltpu.VMEM((rows, depth * len(ups)), BF16)],
        compiler_params=PARAMS,
        cost_estimate=pl.CostEstimate(
            flops=2 * rows * depth * len(ups) * columns,
            bytes_accessed=6 * rows * columns + 2 * depth * len(ups) * columns,
            transcendentals=0,
        ),
    )(me, slot, total, *lows, *ups)


def after(value, *earlier):
    return lax.optimization_barrier((value,) + earlier)[0]


def asked_pages(requests, adapter_page_row, holder_length):
    n_dp = lax.axis_size("dp")
    dp = lax.axis_index("dp")
    count = adapter_page_row.shape[0]

    def pages_of(wanted):
        hit = wanted[:, None] == jnp.arange(count)[None, :]
        return jnp.sum(jnp.where(hit, adapter_page_row[None, :], 0), axis=1)

    def order_in(holders):
        same = holders[:, None] == holders[None, :]
        n = holders.shape[0]
        earlier = jnp.arange(n)[:, None] > jnp.arange(n)[None, :]
        return jnp.sum((same & earlier).astype(jnp.int32), axis=1)

    own = pages_of(requests[0])
    holders = own // holder_length
    slots = (holders ^ dp) * CAP + order_in(holders)
    places = []
    for j in range(n_dp):
        wanted = requests if j == 0 else lax.ppermute(requests, "dp", [(i, i ^ j) for i in range(n_dp)])
        pages = pages_of(wanted[0])
        holder = pages // holder_length
        order = jnp.where(holder == dp, order_in(holder), -1)
        hit = order[None, :] == jnp.arange(CAP)[:, None]
        places.append(jnp.sum(jnp.where(hit, (pages % holder_length)[None, :], 0), axis=1))
    return slots, places


def local(
    attention_result,
    output_weight,
    adapter_down_weight,
    adapter_up_weight,
    adapter_page_row,
    requests,
    row_request_entry,
    ranks,
):
    n_dp = lax.axis_size("dp")
    n_tensor = lax.axis_size("tensor")
    me = lax.axis_index("tensor")
    rows, width = attention_result.shape
    holder_length, rank_part, _ = adapter_down_weight.shape
    rank, columns = adapter_up_weight.shape[1:]
    own_list = requests[0]
    entries = own_list.shape[0]
    one_hot = row_request_entry[:, None] == jnp.arange(entries)[None, :]
    row_rank = jnp.sum(jnp.where(one_hot, ranks[own_list][None, :], 0), axis=1)
    if n_tensor != 4 or width != LINE + sum(GATHERED) or rank_part % 16:
        return plain(
            attention_result, output_weight, adapter_down_weight, adapter_up_weight, adapter_page_row,
            own_list, one_hot, row_rank,
        )

    weight = output_weight.reshape(n_tensor, width, columns)
    every = jnp.arange(n_tensor, dtype=jnp.int32)
    ones = jnp.ones((n_tensor,), jnp.int32)

    gathered, offsets, offset = [], [], LINE
    for features in GATHERED:
        gathered.append(lax.all_gather(attention_result[:, offset:offset + features], "tensor", axis=0))
        offsets.append(offset)
        offset += features

    line = attention_result[None, :, :LINE]
    right = [(i, i + 1) for i in range(n_tensor - 1)]
    left = [(i + 1, i) for i in range(n_tensor - 1)]
    right_1 = lax.ppermute(line, "tensor", right)
    left_1 = lax.ppermute(line, "tensor", left)

    slots, places = asked_pages(requests, adapter_page_row, holder_length)
    downs, ups = [], []
    for j in range(n_dp):
        down, up = pick_pages(places[j], adapter_down_weight, adapter_up_weight)
        if j:
            pairs = [(i, i ^ j) for i in range(n_dp)]
            down, up = lax.ppermute(down, "dp", pairs), lax.ppermute(up, "dp", pairs)
        downs.append(down.reshape(CAP * rank_part, -1))
        ups.append(up.reshape(CAP * rank, columns))

    right_2 = lax.ppermute(right_1, "tensor", right[1:])
    left_2 = lax.ppermute(left_1, "tensor", left[:-1])
    upper = me >= n_tensor // 2
    second = jnp.where(upper, right_2, left_2)
    third = lax.ppermute(second, "tensor", right[-1:] + left[:1])

    near = jnp.stack([me, me - 1, me + 1])
    far = jnp.where(upper, jnp.stack([me - 2, me - 3]), jnp.stack([me + 2, me + 3]))
    xs = [
        ([line, right_1, left_1], near, 0),
        ([second, third], far, 0),
        ([gathered[0]], every, offsets[0]),
        ([gathered[1]], every, offsets[1]),
    ]
    base = low = None
    slot = jnp.sum(jnp.where(one_hot, slots[None, :], 0), axis=1)[:, None]
    live = row_rank[:, None] - me * rank_part
    for i, (blocks, source, start) in enumerate(xs):
        valid = ((source >= 0) & (source < n_tensor)).astype(jnp.int32)
        source = jnp.clip(source, 0, n_tensor - 1).astype(jnp.int32)
        ends = (slot, live) if i == len(xs) - 1 else ()
        if ends:
            blocks = [after(blocks[0], base, low)]
        low = add_low(low, blocks, source, valid, start, downs, rank_part, ends)
        base = add_base(base, blocks, source, valid, start, weight)
    lows = [low] + [
        lax.ppermute(low, "tensor", [(i, (i - j) % n_tensor) for i in range(n_tensor)])
        for j in range(1, n_tensor)
    ]
    return finish(me[None], slot, base, ups, lows)


def gather_pages(block, n_dp):
    return [block] + [
        lax.ppermute(block, "dp", [(i, i ^ j) for i in range(n_dp)]) for j in range(1, n_dp)
    ]


def plain(x, output_weight, down_weight, up_weight, adapter_page_row, own_list, one_hot, row_rank):
    n_dp = lax.axis_size("dp")
    dp = lax.axis_index("dp")
    rows = x.shape[0]
    holder_length = down_weight.shape[0]
    rank, columns = up_weight.shape[1:]
    entries = one_hot.shape[1]
    pages = adapter_page_row[own_list]
    places = ((pages // holder_length) ^ dp) * holder_length + pages % holder_length

    def requested(block):
        blocks = jnp.concatenate(gather_pages(block, n_dp), axis=0)
        return jnp.concatenate(
            [lax.dynamic_slice_in_dim(blocks, places[e], 1, 0) for e in range(entries)], axis=0
        )

    down, up = requested(down_weight), requested(up_weight)
    x = lax.all_gather(x, "tensor", axis=1, tiled=True)
    base = jnp.dot(x, output_weight, preferred_element_type=F32)
    low = jnp.einsum("rd,ekd->rek", x, down, preferred_element_type=F32)
    low = jnp.sum(jnp.where(one_hot[:, :, None], low, 0.0), axis=1).astype(BF16)
    low = lax.all_gather(low, "tensor", axis=1, tiled=True)
    low = jnp.where(jnp.arange(rank)[None, :] < row_rank[:, None], low, jnp.zeros_like(low))
    spread = jnp.where(one_hot[:, :, None], low[:, None, :], jnp.zeros((), BF16))
    term = jnp.dot(
        spread.reshape(rows, entries * rank), up.reshape(entries * rank, columns), preferred_element_type=F32
    )
    return (base + term).astype(BF16)


def solution(mesh):
    in_specs = (
        P(("groups", "dp"), "tensor"),
        P(None, "tensor"),
        P("dp", "tensor", None),
        P("dp", None, "tensor"),
        P("groups"),
        P(("groups", "dp"), None),
        P(("groups", "dp")),
        P(),
    )
    out_specs = P(("groups", "dp"), "tensor")
    return jax.shard_map(local, mesh=mesh, in_specs=in_specs, out_specs=out_specs, check_vma=False)
```

```python
import functools

import jax
import jax.numpy as jnp
from jax import lax
from jax.experimental import pallas as pl
from jax.experimental.pallas import tpu as pltpu
from jax.sharding import PartitionSpec as P

CAP = 2
LINE = 768
GATHERED = (768, 512)
PARAMS = pltpu.CompilerParams(vmem_limit_bytes=60 * 2**20)
F32 = jnp.float32
BF16 = jnp.bfloat16


def pick_kernel(places, down, up, down_out, up_out):
    shards, _, width = down_out.shape[1:]
    for t in range(shards):
        down_out[0, t] = down[0, :, t * width:(t + 1) * width]
    up_out[...] = up[...]


def pick_pages(places, down, up, shards):
    count = places.shape[0]
    _, rank_part, features = down.shape
    shapes = [(shards, rank_part, features // shards), up.shape[1:]]
    return pl.pallas_call(
        pick_kernel,
        out_shape=[jax.ShapeDtypeStruct((count,) + shape, BF16) for shape in shapes],
        grid_spec=pltpu.PrefetchScalarGridSpec(
            num_scalar_prefetch=1,
            grid=(count,),
            in_specs=[pl.BlockSpec((1,) + a.shape[1:], lambda i, places: (places[i], 0, 0)) for a in (down, up)],
            out_specs=[
                pl.BlockSpec((1,) + shapes[0], lambda i, places: (i, 0, 0, 0)),
                pl.BlockSpec((1,) + shapes[1], lambda i, places: (i, 0, 0)),
            ],
        ),
        compiler_params=PARAMS,
    )(places, down, up)


def base_kernel(count, has_total, source, valid, *refs):
    xs, weights, out = refs[:count], refs[count:2 * count], refs[-1]
    shards = xs[0].shape[0]

    def product(x, weight):
        return sum(jnp.dot(x[t], weight[t], preferred_element_type=F32) for t in range(shards))

    first = product(xs[0], weights[0])
    out[...] = refs[-2][...] + first if has_total else first
    for i in range(1, count):

        @pl.when(valid[i] != 0)
        def _():
            out[...] += product(xs[i], weights[i])


def add_base(total, xs, source, valid, offset, weight):
    shards, rows, features = xs[0].shape
    columns = weight.shape[-1]
    part = min(columns, 512)
    held = [] if total is None else [total]
    tile = pl.BlockSpec((rows, part), lambda n, *_: (0, n))
    depth = len(xs) * shards * features

    def weight_spec(i):
        def index(n, source, valid):
            return 0 if shards > 1 else source[i], offset // features, n

        return pl.BlockSpec((shards, features, part), index)

    return pl.pallas_call(
        functools.partial(base_kernel, len(xs), bool(held)),
        out_shape=jax.ShapeDtypeStruct((rows, columns), F32),
        grid_spec=pltpu.PrefetchScalarGridSpec(
            num_scalar_prefetch=2,
            grid=(columns // part,),
            in_specs=[pl.BlockSpec(x.shape, lambda n, *_: (0, 0, 0)) for x in xs]
            + [weight_spec(i) for i in range(len(xs))] + [tile] * len(held),
            out_specs=tile,
        ),
        compiler_params=PARAMS,
        cost_estimate=pl.CostEstimate(
            flops=2 * depth * rows * columns,
            bytes_accessed=2 * depth * (rows + columns) + 8 * rows * columns,
            transcendentals=0,
        ),
    )(source, valid, *xs, *[weight] * len(xs), *held)


def low_kernel(count, shards, parts, has_total, last, rank_part, source, valid, *refs):
    refs = list(refs)
    xs = [refs.pop(0) for _ in range(count)]
    downs = [refs.pop(0) for _ in range(parts)]
    total = refs.pop(0) if has_total else None
    acc = refs.pop()
    step = pl.program_id(0)

    @pl.when(step == 0)
    def _():
        acc[...] = total[...] if has_total else jnp.zeros_like(acc)

    for i, x in enumerate(xs):

        @pl.when((step >= i * shards) & (step < (i + 1) * shards) & (valid[step] != 0))
        def _():
            down = jnp.concatenate([d[c, 0] for d in downs for c in range(CAP)], axis=0)
            acc[...] += lax.dot_general(x[0], down, (((1,), (1,)), ((), ())), preferred_element_type=F32)

    if last:
        slot, live, out = refs

        @pl.when(step == pl.num_programs(0) - 1)
        def _():
            mine = jnp.zeros((acc.shape[0], rank_part), F32)
            for e in range(acc.shape[1] // rank_part):
                mine += jnp.where(slot[...] == e, acc[:, e * rank_part:(e + 1) * rank_part], 0.0)
            k = lax.broadcasted_iota(jnp.int32, mine.shape, 1)
            out[...] = jnp.where(k < live[...], mine, 0.0).astype(BF16)


def add_low(total, xs, source, valid, offset, downs, ends=()):
    shards, rows, features = xs[0].shape
    rank_part = downs[0].shape[2]
    ranks = CAP * rank_part * len(downs)
    held = [] if total is None else [total]
    steps = len(xs) * shards
    whole = pl.BlockSpec((rows, ranks), lambda s, *_: (0, 0))
    column = pl.BlockSpec((rows, 1), lambda s, *_: (0, 0))
    x_specs = [
        pl.BlockSpec((1, rows, features), lambda s, *_, i=i: (jnp.clip(s - i * shards, 0, shards - 1), 0, 0))
        for i in range(len(xs))
    ]
    down_spec = pl.BlockSpec(
        (CAP, 1, rank_part, features), lambda s, source, valid: (0, source[s], 0, offset // features)
    )
    return pl.pallas_call(
        functools.partial(low_kernel, len(xs), shards, len(downs), bool(held), bool(ends), rank_part),
        out_shape=jax.ShapeDtypeStruct((rows, rank_part), BF16) if ends else jax.ShapeDtypeStruct((rows, ranks), F32),
        grid_spec=pltpu.PrefetchScalarGridSpec(
            num_scalar_prefetch=2,
            grid=(steps,),
            in_specs=x_specs + [down_spec] * len(downs) + [whole] * len(held) + [column] * len(ends),
            out_specs=pl.BlockSpec((rows, rank_part), lambda s, *_: (0, 0)) if ends else whole,
            scratch_shapes=[pltpu.VMEM((rows, ranks), F32)] if ends else [],
        ),
        compiler_params=PARAMS,
        cost_estimate=pl.CostEstimate(
            flops=2 * steps * rows * features * ranks,
            bytes_accessed=2 * steps * features * (rows + ranks) + 8 * rows * ranks,
            transcendentals=0,
        ),
    )(source, valid, *xs, *downs, *held, *ends)


def finish_kernel(parts, holders, me, slot, total, *refs):
    lows, ups, (out, spread) = refs[:parts], refs[parts:parts + holders], refs[parts + holders:]
    rank_part = lows[0].shape[1]
    rank = parts * rank_part
    depth = ups[0].shape[0]

    @pl.when(pl.program_id(0) == 0)
    def _():
        low = jnp.concatenate([part[...].astype(F32) for part in lows], axis=1)
        low = pltpu.roll(low, me[0] * rank_part, 1)
        for e in range(spread.shape[1] // rank):
            spread[:, e * rank:(e + 1) * rank] = jnp.where(slot[...] == e, low, 0.0).astype(BF16)

    term = total[...]
    for j, up in enumerate(ups):
        term += jnp.dot(spread[:, j * depth:(j + 1) * depth], up[...], preferred_element_type=F32)
    out[...] = term.astype(BF16)


def finish(me, slot, total, ups, lows):
    rows, columns = total.shape
    depth = ups[0].shape[0]
    rank_part = lows[0].shape[1]
    part = min(columns, 512)
    return pl.pallas_call(
        functools.partial(finish_kernel, len(lows), len(ups)),
        grid=(columns // part,),
        out_shape=jax.ShapeDtypeStruct((rows, columns), BF16),
        in_specs=[
            pl.BlockSpec(memory_space=pltpu.SMEM),
            pl.BlockSpec((rows, 1), lambda n: (0, 0)),
            pl.BlockSpec((rows, part), lambda n: (0, n)),
        ] + [pl.BlockSpec((rows, rank_part), lambda n: (0, 0))] * len(lows)
        + [pl.BlockSpec((depth, part), lambda n: (0, n))] * len(ups),
        out_specs=pl.BlockSpec((rows, part), lambda n: (0, n)),
        scratch_shapes=[pltpu.VMEM((rows, depth * len(ups)), BF16)],
        compiler_params=PARAMS,
        cost_estimate=pl.CostEstimate(
            flops=2 * rows * depth * len(ups) * columns,
            bytes_accessed=6 * rows * columns + 2 * depth * len(ups) * columns,
            transcendentals=0,
        ),
    )(me, slot, total, *lows, *ups)


def after(value, *earlier):
    return lax.optimization_barrier((value,) + earlier)[0]


def asked_pages(requests, adapter_page_row, holder_length):
    n_dp = lax.axis_size("dp")
    dp = lax.axis_index("dp")
    count = adapter_page_row.shape[0]

    def pages_of(wanted):
        hit = wanted[:, None] == jnp.arange(count)[None, :]
        return jnp.sum(jnp.where(hit, adapter_page_row[None, :], 0), axis=1)

    def order_in(holders):
        same = holders[:, None] == holders[None, :]
        n = holders.shape[0]
        earlier = jnp.arange(n)[:, None] > jnp.arange(n)[None, :]
        return jnp.sum((same & earlier).astype(jnp.int32), axis=1)

    own = pages_of(requests[0])
    holders = own // holder_length
    slots = (holders ^ dp) * CAP + order_in(holders)
    places = []
    for j in range(n_dp):
        wanted = requests if j == 0 else lax.ppermute(requests, "dp", [(i, i ^ j) for i in range(n_dp)])
        pages = pages_of(wanted[0])
        holder = pages // holder_length
        order = jnp.where(holder == dp, order_in(holder), -1)
        hit = order[None, :] == jnp.arange(CAP)[:, None]
        places.append(jnp.sum(jnp.where(hit, (pages % holder_length)[None, :], 0), axis=1))
    return slots, places


def local(
    attention_result,
    output_weight,
    adapter_down_weight,
    adapter_up_weight,
    adapter_page_row,
    requests,
    row_request_entry,
    ranks,
):
    n_dp = lax.axis_size("dp")
    n_tensor = lax.axis_size("tensor")
    me = lax.axis_index("tensor")
    rows, width = attention_result.shape
    holder_length, rank_part, _ = adapter_down_weight.shape
    rank, columns = adapter_up_weight.shape[1:]
    own_list = requests[0]
    entries = own_list.shape[0]
    one_hot = row_request_entry[:, None] == jnp.arange(entries)[None, :]
    row_rank = jnp.sum(jnp.where(one_hot, ranks[own_list][None, :], 0), axis=1)
    if n_tensor != 4 or width != LINE + sum(GATHERED) or rank_part % 16:
        return plain(
            attention_result, output_weight, adapter_down_weight, adapter_up_weight, adapter_page_row,
            own_list, one_hot, row_rank,
        )

    weight = output_weight.reshape(n_tensor, width, columns)
    every = jnp.arange(n_tensor, dtype=jnp.int32)
    ones = jnp.ones((n_tensor,), jnp.int32)

    gathered, offsets, offset = [], [], LINE
    x = attention_result
    for features in GATHERED:
        piece = x[:, offset:offset + features]
        gathered.append(lax.all_gather(piece, "tensor", axis=0))
        x = after(x, piece)
        offsets.append(offset)
        offset += features

    line = x[None, :, :LINE]
    right = [(i, i + 1) for i in range(n_tensor - 1)]
    left = [(i + 1, i) for i in range(n_tensor - 1)]
    right_1 = lax.ppermute(line, "tensor", right)
    left_1 = lax.ppermute(line, "tensor", left)

    slots, places = asked_pages(requests, adapter_page_row, holder_length)
    downs, ups = [], []
    for j in range(n_dp):
        down, up = pick_pages(places[j], adapter_down_weight, adapter_up_weight, n_tensor)
        if j:
            pairs = [(i, i ^ j) for i in range(n_dp)]
            down, up = lax.ppermute(down, "dp", pairs), lax.ppermute(up, "dp", pairs)
        downs.append(down)
        ups.append(up.reshape(CAP * rank, columns))

    right_2 = lax.ppermute(right_1, "tensor", right[1:])
    left_2 = lax.ppermute(left_1, "tensor", left[:-1])
    upper = me >= n_tensor // 2
    second = jnp.where(upper, right_2, left_2)
    third = lax.ppermute(second, "tensor", right[-1:] + left[:1])

    near = jnp.stack([me, me - 1, me + 1])
    far = jnp.where(upper, jnp.stack([me - 2, me - 3]), jnp.stack([me + 2, me + 3]))
    xs = [
        ([line, right_1, left_1], near, 0),
        ([second, third], far, 0),
        ([gathered[0]], every, offsets[0]),
        ([gathered[1]], every, offsets[1]),
    ]
    base = low = None
    slot = jnp.sum(jnp.where(one_hot, slots[None, :], 0), axis=1)[:, None]
    live = row_rank[:, None] - me * rank_part
    for i, (blocks, source, start) in enumerate(xs):
        valid = ((source >= 0) & (source < n_tensor)).astype(jnp.int32)
        source = jnp.clip(source, 0, n_tensor - 1).astype(jnp.int32)
        ends = (slot, live) if i == len(xs) - 1 else ()
        if ends:
            blocks = [after(blocks[0], base, low)]
        low = add_low(low, blocks, source, valid, start, downs, ends)
        base = add_base(base, blocks, source, valid, start, weight)
    lows = [low] + [
        lax.ppermute(low, "tensor", [(i, (i - j) % n_tensor) for i in range(n_tensor)])
        for j in range(1, n_tensor)
    ]
    return finish(me[None], slot, base, ups, lows)


def gather_pages(block, n_dp):
    return [block] + [
        lax.ppermute(block, "dp", [(i, i ^ j) for i in range(n_dp)]) for j in range(1, n_dp)
    ]


def plain(x, output_weight, down_weight, up_weight, adapter_page_row, own_list, one_hot, row_rank):
    n_dp = lax.axis_size("dp")
    dp = lax.axis_index("dp")
    rows = x.shape[0]
    holder_length = down_weight.shape[0]
    rank, columns = up_weight.shape[1:]
    entries = one_hot.shape[1]
    pages = adapter_page_row[own_list]
    places = ((pages // holder_length) ^ dp) * holder_length + pages % holder_length

    def requested(block):
        blocks = jnp.concatenate(gather_pages(block, n_dp), axis=0)
        return jnp.concatenate(
            [lax.dynamic_slice_in_dim(blocks, places[e], 1, 0) for e in range(entries)], axis=0
        )

    down, up = requested(down_weight), requested(up_weight)
    x = lax.all_gather(x, "tensor", axis=1, tiled=True)
    base = jnp.dot(x, output_weight, preferred_element_type=F32)
    low = jnp.einsum("rd,ekd->rek", x, down, preferred_element_type=F32)
    low = jnp.sum(jnp.where(one_hot[:, :, None], low, 0.0), axis=1).astype(BF16)
    low = lax.all_gather(low, "tensor", axis=1, tiled=True)
    low = jnp.where(jnp.arange(rank)[None, :] < row_rank[:, None], low, jnp.zeros_like(low))
    spread = jnp.where(one_hot[:, :, None], low[:, None, :], jnp.zeros((), BF16))
    term = jnp.dot(
        spread.reshape(rows, entries * rank), up.reshape(entries * rank, columns), preferred_element_type=F32
    )
    return (base + term).astype(BF16)


def solution(mesh):
    in_specs = (
        P(("groups", "dp"), "tensor"),
        P(None, "tensor"),
        P("dp", "tensor", None),
        P("dp", None, "tensor"),
        P("groups"),
        P(("groups", "dp"), None),
        P(("groups", "dp")),
        P(),
    )
    out_specs = P(("groups", "dp"), "tensor")
    return jax.shard_map(local, mesh=mesh, in_specs=in_specs, out_specs=out_specs, check_vma=False)
```

```python
import functools

import jax
import jax.numpy as jnp
from jax import lax
from jax.experimental import pallas as pl
from jax.experimental.pallas import tpu as pltpu
from jax.sharding import PartitionSpec as P

CAP = 2
LINE = 512
GATHERED = (1024, 512)
PARAMS = pltpu.CompilerParams(vmem_limit_bytes=60 * 2**20)
F32 = jnp.float32
BF16 = jnp.bfloat16


def pick_kernel(places, down, up, down_out, up_out):
    shards, _, width = down_out.shape[1:]
    for t in range(shards):
        down_out[0, t] = down[0, :, t * width:(t + 1) * width]
    up_out[...] = up[...]


def pick_pages(places, down, up, shards):
    count = places.shape[0]
    _, rank_part, features = down.shape
    shapes = [(shards, rank_part, features // shards), up.shape[1:]]
    return pl.pallas_call(
        pick_kernel,
        out_shape=[jax.ShapeDtypeStruct((count,) + shape, BF16) for shape in shapes],
        grid_spec=pltpu.PrefetchScalarGridSpec(
            num_scalar_prefetch=1,
            grid=(count,),
            in_specs=[pl.BlockSpec((1,) + a.shape[1:], lambda i, places: (places[i], 0, 0)) for a in (down, up)],
            out_specs=[
                pl.BlockSpec((1,) + shapes[0], lambda i, places: (i, 0, 0, 0)),
                pl.BlockSpec((1,) + shapes[1], lambda i, places: (i, 0, 0)),
            ],
        ),
        compiler_params=PARAMS,
    )(places, down, up)


def join_kernel(by_shard, *refs):
    *pages, out = refs
    if by_shard:
        out[0] = jnp.concatenate([p[c, 0] for p in pages for c in range(CAP)], axis=0)
        return
    for j, p in enumerate(pages):

        @pl.when(pl.program_id(0) == j)
        def _():
            out[...] = p[...]


def join_downs(downs):
    _, shards, rank_part, features = downs[0].shape
    slots = CAP * rank_part * len(downs)
    return pl.pallas_call(
        functools.partial(join_kernel, True),
        out_shape=jax.ShapeDtypeStruct((shards, slots, features), BF16),
        grid=(shards,),
        in_specs=[pl.BlockSpec((CAP, 1, rank_part, features), lambda t: (0, t, 0, 0))] * len(downs),
        out_specs=pl.BlockSpec((1, slots, features), lambda t: (t, 0, 0)),
        compiler_params=PARAMS,
    )(*downs)


def join_ups(ups):
    count, rank, columns = ups[0].shape
    return pl.pallas_call(
        functools.partial(join_kernel, False),
        out_shape=jax.ShapeDtypeStruct((count * len(ups), rank, columns), BF16),
        grid=(len(ups),),
        in_specs=[pl.BlockSpec(up.shape, lambda j: (0, 0, 0)) for up in ups],
        out_specs=pl.BlockSpec(ups[0].shape, lambda j: (j, 0, 0)),
        compiler_params=PARAMS,
    )(*ups).reshape(-1, columns)


def depth_of(weight):
    return weight[...].reshape(-1, weight.shape[-1])


def chunk_kernel(spans, has_total, source, valid, *refs):
    refs = list(refs)
    count = len(spans)
    xs, weights, downs = (refs[i * count:(i + 1) * count] for i in range(3))
    totals, (base, low) = refs[3 * count:-2], refs[-2:]

    def base_of(i):
        return jnp.dot(xs[i][...], depth_of(weights[i]), preferred_element_type=F32)

    def low_of(i):
        f = downs[i].shape[-1]
        return sum(
            lax.dot_general(
                xs[i][:, t * f:(t + 1) * f], downs[i][t], (((1,), (1,)), ((), ())), preferred_element_type=F32
            )
            for t in range(spans[i])
        )

    start = pl.program_id(0) == 0
    base[...] = totals[0][...] + base_of(0) if has_total else base_of(0)

    @pl.when(start)
    def _():
        low[...] = totals[1][...] + low_of(0) if has_total else low_of(0)

    for i in range(1, count):

        @pl.when(valid[i] != 0)
        def _():
            base[...] += base_of(i)

        @pl.when((valid[i] != 0) & start)
        def _():
            low[...] += low_of(i)


def add_chunk(totals, blocks, source, weight, down):
    n_tensor, _, columns = weight.shape
    slots = down.shape[1]
    rows = blocks[0][0].shape[0]
    part = min(columns, 512)
    valid = ((source >= 0) & (source < n_tensor)).astype(jnp.int32)
    source = jnp.clip(source, 0, n_tensor - 1).astype(jnp.int32)
    x_specs, weight_specs, down_specs, depth = [], [], [], 0
    for i, (x, span, first) in enumerate(blocks):
        f = x.shape[1] // span

        def place(source, i=i, span=span, at=first // f):
            return (0 if span > 1 else source[i]), at

        x_specs.append(pl.BlockSpec(x.shape, lambda n, *_: (0, 0)))
        weight_specs.append(
            pl.BlockSpec((span, f, part), lambda n, source, valid, place=place: place(source) + (n,))
        )
        down_specs.append(
            pl.BlockSpec(
                (span, slots, f),
                lambda n, source, valid, place=place: (place(source)[0], 0, place(source)[1]),
            )
        )
        depth += x.shape[1]
    tile = pl.BlockSpec((rows, part), lambda n, *_: (0, n))
    whole = pl.BlockSpec((rows, slots), lambda n, *_: (0, 0))
    return pl.pallas_call(
        functools.partial(chunk_kernel, [span for _, span, _ in blocks], bool(totals)),
        out_shape=[jax.ShapeDtypeStruct((rows, columns), F32), jax.ShapeDtypeStruct((rows, slots), F32)],
        grid_spec=pltpu.PrefetchScalarGridSpec(
            num_scalar_prefetch=2,
            grid=(columns // part,),
            in_specs=x_specs + weight_specs + down_specs + ([tile, whole] if totals else []),
            out_specs=[tile, whole],
        ),
        compiler_params=PARAMS,
        cost_estimate=pl.CostEstimate(
            flops=2 * depth * rows * (columns + slots),
            bytes_accessed=2 * depth * (rows + columns + slots) + 8 * rows * (columns + slots),
            transcendentals=0,
        ),
    )(source, valid, *[x for x, _, _ in blocks], *[weight] * len(blocks), *[down] * len(blocks), *totals)


def base_kernel(x, weight, total, out):
    out[...] = total[...] + jnp.dot(x[...], depth_of(weight), preferred_element_type=F32)


def add_base(total, x, first, weight):
    shards, _, columns = weight.shape
    rows, depth = x.shape
    features = depth // shards
    part = min(columns, 512)
    tile = pl.BlockSpec((rows, part), lambda n: (0, n))
    return pl.pallas_call(
        base_kernel,
        out_shape=jax.ShapeDtypeStruct((rows, columns), F32),
        grid=(columns // part,),
        in_specs=[
            pl.BlockSpec((rows, depth), lambda n: (0, 0)),
            pl.BlockSpec((shards, features, part), lambda n: (0, first // features, n)),
            tile,
        ],
        out_specs=tile,
        compiler_params=PARAMS,
        cost_estimate=pl.CostEstimate(
            flops=2 * depth * rows * columns,
            bytes_accessed=2 * depth * (rows + columns) + 8 * rows * columns,
            transcendentals=0,
        ),
    )(x, weight, total)


def low_kernel(x, down, total, slot, live, out, acc):
    step = pl.program_id(0)
    rank_part = out.shape[1]

    @pl.when(step == 0)
    def _():
        acc[...] = total[...]

    acc[...] += lax.dot_general(x[...], down[0], (((1,), (1,)), ((), ())), preferred_element_type=F32)

    @pl.when(step == pl.num_programs(0) - 1)
    def _():
        mine = jnp.zeros(out.shape, F32)
        for e in range(acc.shape[1] // rank_part):
            mine += jnp.where(slot[...] == e, acc[:, e * rank_part:(e + 1) * rank_part], 0.0)
        k = lax.broadcasted_iota(jnp.int32, mine.shape, 1)
        out[...] = jnp.where(k < live[...], mine, 0.0).astype(BF16)


def finish_low(total, x, first, down, slot, live, rank_part):
    shards, slots, _ = down.shape
    rows, depth = x.shape
    features = depth // shards
    column = pl.BlockSpec((rows, 1), lambda t: (0, 0))
    return pl.pallas_call(
        low_kernel,
        out_shape=jax.ShapeDtypeStruct((rows, rank_part), BF16),
        grid=(shards,),
        in_specs=[
            pl.BlockSpec((rows, features), lambda t: (0, t)),
            pl.BlockSpec((1, slots, features), lambda t: (t, 0, first // features)),
            pl.BlockSpec((rows, slots), lambda t: (0, 0)),
            column,
            column,
        ],
        out_specs=pl.BlockSpec((rows, rank_part), lambda t: (0, 0)),
        scratch_shapes=[pltpu.VMEM((rows, slots), F32)],
        compiler_params=PARAMS,
        cost_estimate=pl.CostEstimate(
            flops=2 * depth * rows * slots,
            bytes_accessed=2 * depth * (rows + slots) + 4 * rows * slots,
            transcendentals=0,
        ),
    )(x, down, total, slot, live)


def finish_kernel(parts, me, slot, total, up, *refs):
    lows, (out, spread) = refs[:parts], refs[parts:]
    rank_part = lows[0].shape[1]
    rank = parts * rank_part

    @pl.when(pl.program_id(0) == 0)
    def _():
        low = jnp.concatenate([part[...].astype(F32) for part in lows], axis=1)
        low = pltpu.roll(low, me[0] * rank_part, 1)
        for e in range(spread.shape[1] // rank):
            spread[:, e * rank:(e + 1) * rank] = jnp.where(slot[...] == e, low, 0.0).astype(BF16)

    out[...] = (total[...] + jnp.dot(spread[...], up[...], preferred_element_type=F32)).astype(BF16)


def finish(me, slot, total, up, lows):
    rows, columns = total.shape
    depth = up.shape[0]
    rank_part = lows[0].shape[1]
    part = min(columns, 512)
    return pl.pallas_call(
        functools.partial(finish_kernel, len(lows)),
        grid=(columns // part,),
        out_shape=jax.ShapeDtypeStruct((rows, columns), BF16),
        in_specs=[
            pl.BlockSpec(memory_space=pltpu.SMEM),
            pl.BlockSpec((rows, 1), lambda n: (0, 0)),
            pl.BlockSpec((rows, part), lambda n: (0, n)),
            pl.BlockSpec((depth, part), lambda n: (0, n)),
        ] + [pl.BlockSpec((rows, rank_part), lambda n: (0, 0))] * len(lows),
        out_specs=pl.BlockSpec((rows, part), lambda n: (0, n)),
        scratch_shapes=[pltpu.VMEM((rows, depth), BF16)],
        compiler_params=PARAMS,
        cost_estimate=pl.CostEstimate(
            flops=2 * rows * depth * columns,
            bytes_accessed=6 * rows * columns + 2 * depth * columns,
            transcendentals=0,
        ),
    )(me, slot, total, up, *lows)


def after(value, *earlier):
    return lax.optimization_barrier((value,) + earlier)[0]


def asked_pages(requests, adapter_page_row, holder_length):
    n_dp = lax.axis_size("dp")
    dp = lax.axis_index("dp")
    count = adapter_page_row.shape[0]

    def pages_of(wanted):
        hit = wanted[:, None] == jnp.arange(count)[None, :]
        return jnp.sum(jnp.where(hit, adapter_page_row[None, :], 0), axis=1)

    def order_in(holders):
        same = holders[:, None] == holders[None, :]
        n = holders.shape[0]
        earlier = jnp.arange(n)[:, None] > jnp.arange(n)[None, :]
        return jnp.sum((same & earlier).astype(jnp.int32), axis=1)

    own = pages_of(requests[0])
    holders = own // holder_length
    slots = (holders ^ dp) * CAP + order_in(holders)
    places = []
    for j in range(n_dp):
        wanted = requests if j == 0 else lax.ppermute(requests, "dp", [(i, i ^ j) for i in range(n_dp)])
        pages = pages_of(wanted[0])
        holder = pages // holder_length
        order = jnp.where(holder == dp, order_in(holder), -1)
        hit = order[None, :] == jnp.arange(CAP)[:, None]
        places.append(jnp.sum(jnp.where(hit, (pages % holder_length)[None, :], 0), axis=1))
    return slots, places


def local(
    attention_result,
    output_weight,
    adapter_down_weight,
    adapter_up_weight,
    adapter_page_row,
    requests,
    row_request_entry,
    ranks,
):
    n_dp = lax.axis_size("dp")
    n_tensor = lax.axis_size("tensor")
    me = lax.axis_index("tensor")
    rows, width = attention_result.shape
    holder_length, rank_part, _ = adapter_down_weight.shape
    rank, columns = adapter_up_weight.shape[1:]
    own_list = requests[0]
    entries = own_list.shape[0]
    one_hot = row_request_entry[:, None] == jnp.arange(entries)[None, :]
    row_rank = jnp.sum(jnp.where(one_hot, ranks[own_list][None, :], 0), axis=1)
    if n_tensor != 4 or width != LINE + sum(GATHERED) or rank_part % 16:
        return plain(
            attention_result, output_weight, adapter_down_weight, adapter_up_weight, adapter_page_row,
            own_list, one_hot, row_rank,
        )

    weight = output_weight.reshape(n_tensor, width, columns)
    gathered, x, first = [], attention_result, 0
    for features in GATHERED:
        piece = x[:, first:first + features]
        gathered.append(lax.all_gather(piece, "tensor", axis=1, tiled=True))
        x = after(x, piece)
        first += features + LINE

    middle = GATHERED[0]
    last = middle + LINE
    line = x[:, middle:last]
    right = [(i, i + 1) for i in range(n_tensor - 1)]
    left = [(i + 1, i) for i in range(n_tensor - 1)]
    right_1 = lax.ppermute(line, "tensor", right)
    left_1 = lax.ppermute(line, "tensor", left)

    slots, places = asked_pages(requests, adapter_page_row, holder_length)
    downs, ups = [], []
    for j in range(n_dp):
        down, up = pick_pages(places[j], adapter_down_weight, adapter_up_weight, n_tensor)
        if j:
            pairs = [(i, i ^ j) for i in range(n_dp)]
            down, up = lax.ppermute(down, "dp", pairs), lax.ppermute(up, "dp", pairs)
        downs.append(down)
        ups.append(up)

    right_2 = lax.ppermute(right_1, "tensor", right[1:])
    left_2 = lax.ppermute(left_1, "tensor", left[:-1])
    upper = me >= n_tensor // 2
    second = jnp.where(upper, right_2, left_2)
    third = lax.ppermute(second, "tensor", right[-1:] + left[:1])

    down = join_downs(after(tuple(downs), third))
    up = join_ups(ups)

    slot = jnp.sum(jnp.where(one_hot, slots[None, :], 0), axis=1)[:, None]
    live = row_rank[:, None] - me * rank_part
    near = jnp.stack([me, me - 1, me + 1])
    totals = add_chunk((), [(line, 1, middle), (right_1, 1, middle), (left_1, 1, middle)], near, weight, down)
    far = jnp.where(upper, jnp.stack([me - 2, me - 3, me]), jnp.stack([me + 2, me + 3, me]))
    totals = add_chunk(
        totals, [(second, 1, middle), (third, 1, middle), (gathered[0], n_tensor, 0)], far, weight, down
    )
    x = after(gathered[1], *totals, up)
    low = finish_low(totals[1], x, last, down, slot, live, rank_part)
    base = add_base(totals[0], x, last, weight)
    lows = [low] + [
        lax.ppermute(low, "tensor", [(i, (i - j) % n_tensor) for i in range(n_tensor)])
        for j in range(1, n_tensor)
    ]
    return finish(me[None], slot, base, up, lows)


def gather_pages(block, n_dp):
    return [block] + [
        lax.ppermute(block, "dp", [(i, i ^ j) for i in range(n_dp)]) for j in range(1, n_dp)
    ]


def plain(x, output_weight, down_weight, up_weight, adapter_page_row, own_list, one_hot, row_rank):
    n_dp = lax.axis_size("dp")
    dp = lax.axis_index("dp")
    rows = x.shape[0]
    holder_length = down_weight.shape[0]
    rank, columns = up_weight.shape[1:]
    entries = one_hot.shape[1]
    pages = adapter_page_row[own_list]
    places = ((pages // holder_length) ^ dp) * holder_length + pages % holder_length

    def requested(block):
        blocks = jnp.concatenate(gather_pages(block, n_dp), axis=0)
        return jnp.concatenate(
            [lax.dynamic_slice_in_dim(blocks, places[e], 1, 0) for e in range(entries)], axis=0
        )

    down, up = requested(down_weight), requested(up_weight)
    x = lax.all_gather(x, "tensor", axis=1, tiled=True)
    base = jnp.dot(x, output_weight, preferred_element_type=F32)
    low = jnp.einsum("rd,ekd->rek", x, down, preferred_element_type=F32)
    low = jnp.sum(jnp.where(one_hot[:, :, None], low, 0.0), axis=1).astype(BF16)
    low = lax.all_gather(low, "tensor", axis=1, tiled=True)
    low = jnp.where(jnp.arange(rank)[None, :] < row_rank[:, None], low, jnp.zeros_like(low))
    spread = jnp.where(one_hot[:, :, None], low[:, None, :], jnp.zeros((), BF16))
    term = jnp.dot(
        spread.reshape(rows, entries * rank), up.reshape(entries * rank, columns), preferred_element_type=F32
    )
    return (base + term).astype(BF16)


def solution(mesh):
    in_specs = (
        P(("groups", "dp"), "tensor"),
        P(None, "tensor"),
        P("dp", "tensor", None),
        P("dp", None, "tensor"),
        P("groups"),
        P(("groups", "dp"), None),
        P(("groups", "dp")),
        P(),
    )
    out_specs = P(("groups", "dp"), "tensor")
    return jax.shard_map(local, mesh=mesh, in_specs=in_specs, out_specs=out_specs, check_vma=False)
```

```python
import functools

import jax
import jax.numpy as jnp
from jax import lax
from jax.experimental import pallas as pl
from jax.experimental.pallas import tpu as pltpu
from jax.sharding import PartitionSpec as P

CAP = 2
UNIT = 512
LINE = 512
GATHERED = (1024, 512)
PARAMS = pltpu.CompilerParams(vmem_limit_bytes=48 * 2**20)
F32 = jnp.float32
BF16 = jnp.bfloat16


def pick_kernel(places, down, up, down_out, up_out):
    shards, _, width = down_out.shape[1:]
    for t in range(shards):
        down_out[0, t] = down[0, :, t * width:(t + 1) * width]
    up_out[...] = up[...]


def pick_pages(places, down, up, shards):
    count = places.shape[0]
    _, rank_part, features = down.shape
    shapes = [(shards, rank_part, features // shards), up.shape[1:]]
    return pl.pallas_call(
        pick_kernel,
        out_shape=[jax.ShapeDtypeStruct((count,) + shape, BF16) for shape in shapes],
        grid_spec=pltpu.PrefetchScalarGridSpec(
            num_scalar_prefetch=1,
            grid=(count,),
            in_specs=[pl.BlockSpec((1,) + a.shape[1:], lambda i, places: (places[i], 0, 0)) for a in (down, up)],
            out_specs=[
                pl.BlockSpec((1,) + shapes[0], lambda i, places: (i, 0, 0, 0)),
                pl.BlockSpec((1,) + shapes[1], lambda i, places: (i, 0, 0)),
            ],
        ),
        compiler_params=PARAMS,
    )(places, down, up)


def join_downs_kernel(*refs):
    *pages, out = refs
    units = out.shape[0]
    for u in range(units):
        out[u] = jnp.concatenate(
            [p[c, 0, :, u * UNIT:(u + 1) * UNIT] for p in pages for c in range(CAP)], axis=0
        )


def join_downs(downs):
    _, shards, rank_part, features = downs[0].shape
    slots = CAP * rank_part * len(downs)
    units = features // UNIT
    return pl.pallas_call(
        join_downs_kernel,
        out_shape=jax.ShapeDtypeStruct((shards * units, slots, UNIT), BF16),
        grid=(shards,),
        in_specs=[pl.BlockSpec((CAP, 1, rank_part, features), lambda t: (0, t, 0, 0))] * len(downs),
        out_specs=pl.BlockSpec((units, slots, UNIT), lambda t: (t, 0, 0)),
        compiler_params=PARAMS,
    )(*downs)


def join_ups_kernel(*refs):
    *pages, out = refs
    for j, p in enumerate(pages):

        @pl.when(pl.program_id(0) == j)
        def _():
            out[...] = p[...]


def join_ups(ups):
    count, rank, columns = ups[0].shape
    return pl.pallas_call(
        join_ups_kernel,
        out_shape=jax.ShapeDtypeStruct((count * len(ups), rank, columns), BF16),
        grid=(len(ups),),
        in_specs=[pl.BlockSpec(up.shape, lambda j: (0, 0, 0)) for up in ups],
        out_specs=pl.BlockSpec(ups[0].shape, lambda j: (j, 0, 0)),
        compiler_params=PARAMS,
    )(*ups).reshape(-1, columns)


RESIDENT = pl.BlockSpec(memory_space=pltpu.VMEM)


def unit_steps(x):
    return x.shape[0] * (x.shape[2] // UNIT)


def x_specs(xs):
    specs, first = [], 0
    for x in xs:
        units = x.shape[2] // UNIT

        def index(s, *_, first=first, units=units, last=x.shape[0] - 1):
            return jnp.clip((s - first) // units, 0, last), 0, 0

        specs.append(pl.BlockSpec((1,) + x.shape[1:], index))
        first += unit_steps(x)
    return specs


def for_unit(xs, counts, valid, body):
    s, first = pl.program_id(0), 0
    for x, count in zip(xs, counts):
        units = x.shape[2] // UNIT

        @pl.when((s >= first) & (s < first + count) & (valid[s] != 0))
        def _():
            if units == 1:
                body(x[0])
            else:
                at = pl.multiple_of(lax.rem(s - first, units) * UNIT, UNIT)
                body(x[0, :, pl.ds(at, UNIT)])

        first += count


def chunk_kernel(counts, held, with_base, with_low, rank_part, unit, valid, *refs):
    refs = list(refs)
    xs = [refs.pop(0) for _ in counts]
    weight = refs.pop(0) if with_base else None
    down = refs.pop(0) if with_low else None
    ends = [refs.pop(0) for _ in range(2)] if rank_part else None
    totals = [refs.pop(0) for _ in range(held)]
    base = refs.pop(0) if with_base else None
    low = refs.pop(0) if with_low and not rank_part else None
    if rank_part:
        out, low = refs

    @pl.when(pl.program_id(0) == 0)
    def _():
        if rank_part:
            low[...] = totals[0][...]
        elif not held:
            base[...] = jnp.zeros_like(base)
            low[...] = jnp.zeros_like(low)

    def body(x):
        if with_base:
            part = min(base.shape[1], 512)
            for n in range(0, base.shape[1], part):
                base[:, n:n + part] += jnp.dot(x, weight[0, :, n:n + part], preferred_element_type=F32)
        if with_low:
            low[...] += lax.dot_general(x, down[0], (((1,), (1,)), ((), ())), preferred_element_type=F32)

    for_unit(xs, counts, valid, body)
    if rank_part:
        slot, live = ends

        @pl.when(pl.program_id(0) == pl.num_programs(0) - 1)
        def _():
            mine = jnp.zeros(out.shape, F32)
            for e in range(low.shape[1] // rank_part):
                mine += jnp.where(slot[...] == e, low[:, e * rank_part:(e + 1) * rank_part], 0.0)
            k = lax.broadcasted_iota(jnp.int32, mine.shape, 1)
            out[...] = jnp.where(k < live[...], mine, 0.0).astype(BF16)


def add_chunk(totals, xs, unit, valid, weight=None, down=None, ends=(), rank_part=0):
    rows = xs[0].shape[1]
    columns = 0 if weight is None else weight.shape[-1]
    slots = 0 if down is None else down.shape[1]
    steps = sum(unit_steps(x) for x in xs)
    walked = [a for a in (weight, down) if a is not None]
    out_shape, aliases = [], {}
    if rank_part:
        out_shape = [jax.ShapeDtypeStruct((rows, rank_part), BF16)]
    else:
        out_shape = [pltpu.VMEM((rows, a), F32) for a in (columns, slots) if a]
        first = 2 + len(xs) + len(walked) + len(ends)
        aliases = {first + i: i for i in range(len(totals))}
    outs = pl.pallas_call(
        functools.partial(
            chunk_kernel, [unit_steps(x) for x in xs], len(totals), weight is not None, down is not None, rank_part
        ),
        out_shape=out_shape,
        grid_spec=pltpu.PrefetchScalarGridSpec(
            num_scalar_prefetch=2,
            grid=(steps,),
            in_specs=x_specs(xs)
            + [pl.BlockSpec((1,) + a.shape[1:], lambda s, unit, valid: (unit[s], 0, 0)) for a in walked]
            + [pl.BlockSpec((rows, 1), lambda s, *_: (0, 0))] * len(ends)
            + [RESIDENT] * len(totals),
            out_specs=[RESIDENT if not rank_part else pl.BlockSpec((rows, rank_part), lambda s, *_: (0, 0))]
            * len(out_shape),
            scratch_shapes=[pltpu.VMEM((rows, slots), F32)] if rank_part else [],
        ),
        input_output_aliases=aliases,
        compiler_params=PARAMS,
        cost_estimate=pl.CostEstimate(
            flops=2 * steps * UNIT * rows * (columns + slots),
            bytes_accessed=2 * steps * UNIT * (rows + columns + slots),
            transcendentals=0,
        ),
    )(unit, valid, *xs, *walked, *ends, *totals)
    return outs


def finish_kernel(parts, me, slot, total, up, *refs):
    lows, (out, acc, spread) = refs[:parts], refs[parts:]
    rank_part = lows[0].shape[1]
    rank = parts * rank_part
    step = pl.program_id(0)
    depth = up.shape[0]

    @pl.when(step == 0)
    def _():
        low = jnp.concatenate([part[...].astype(F32) for part in lows], axis=1)
        low = pltpu.roll(low, me[0] * rank_part, 1)
        for e in range(spread.shape[0] * depth // rank):
            own = jnp.where(slot[...] == e, low, 0.0).astype(BF16)
            spread[e * rank // depth, :, e * rank % depth:e * rank % depth + rank] = own

    last = pl.num_programs(0) - 1
    part = min(out.shape[1], 512)
    for n in range(0, out.shape[1], part):
        cut = slice(n, n + part)
        term = jnp.dot(spread[step], up[:, cut], preferred_element_type=F32)

        @pl.when(step == 0)
        def _():
            acc[:, cut] = total[:, cut] + term

        @pl.when((step > 0) & (step < last))
        def _():
            acc[:, cut] += term

        @pl.when(step == last)
        def _():
            out[:, cut] = (acc[:, cut] + term).astype(BF16)


def finish(me, slot, total, up, lows):
    rows, columns = total.shape
    rank_part = lows[0].shape[1]
    depth = 2 * len(lows) * rank_part
    steps = up.shape[0] // depth
    return pl.pallas_call(
        functools.partial(finish_kernel, len(lows)),
        grid=(steps,),
        out_shape=jax.ShapeDtypeStruct((rows, columns), BF16),
        in_specs=[
            pl.BlockSpec(memory_space=pltpu.SMEM),
            pl.BlockSpec((rows, 1), lambda s: (0, 0)),
            RESIDENT,
            pl.BlockSpec((depth, columns), lambda s: (s, 0)),
        ] + [pl.BlockSpec((rows, rank_part), lambda s: (0, 0))] * len(lows),
        out_specs=pl.BlockSpec((rows, columns), lambda s: (0, 0)),
        scratch_shapes=[pltpu.VMEM((rows, columns), F32), pltpu.VMEM((steps, rows, depth), BF16)],
        compiler_params=PARAMS,
        cost_estimate=pl.CostEstimate(
            flops=2 * rows * up.shape[0] * columns,
            bytes_accessed=2 * (rows + up.shape[0]) * columns,
            transcendentals=0,
        ),
    )(me, slot, total, up, *lows)


def after(value, *earlier):
    return lax.optimization_barrier((value,) + earlier)[0]


def asked_pages(requests, adapter_page_row, holder_length):
    n_dp = lax.axis_size("dp")
    dp = lax.axis_index("dp")
    count = adapter_page_row.shape[0]

    def pages_of(wanted):
        hit = wanted[:, None] == jnp.arange(count)[None, :]
        return jnp.sum(jnp.where(hit, adapter_page_row[None, :], 0), axis=1)

    def order_in(holders):
        same = holders[:, None] == holders[None, :]
        n = holders.shape[0]
        earlier = jnp.arange(n)[:, None] > jnp.arange(n)[None, :]
        return jnp.sum((same & earlier).astype(jnp.int32), axis=1)

    own = pages_of(requests[0])
    holders = own // holder_length
    slots = (holders ^ dp) * CAP + order_in(holders)
    places = []
    for j in range(n_dp):
        wanted = requests if j == 0 else lax.ppermute(requests, "dp", [(i, i ^ j) for i in range(n_dp)])
        pages = pages_of(wanted[0])
        holder = pages // holder_length
        order = jnp.where(holder == dp, order_in(holder), -1)
        hit = order[None, :] == jnp.arange(CAP)[:, None]
        places.append(jnp.sum(jnp.where(hit, (pages % holder_length)[None, :], 0), axis=1))
    return slots, places


def local(
    attention_result,
    output_weight,
    adapter_down_weight,
    adapter_up_weight,
    adapter_page_row,
    requests,
    row_request_entry,
    ranks,
):
    n_dp = lax.axis_size("dp")
    n_tensor = lax.axis_size("tensor")
    me = lax.axis_index("tensor")
    rows, width = attention_result.shape
    holder_length, rank_part, _ = adapter_down_weight.shape
    rank, columns = adapter_up_weight.shape[1:]
    own_list = requests[0]
    entries = own_list.shape[0]
    one_hot = row_request_entry[:, None] == jnp.arange(entries)[None, :]
    row_rank = jnp.sum(jnp.where(one_hot, ranks[own_list][None, :], 0), axis=1)
    if n_tensor != 4 or width != LINE + sum(GATHERED) or rank_part % 16:
        return plain(
            attention_result, output_weight, adapter_down_weight, adapter_up_weight, adapter_page_row,
            own_list, one_hot, row_rank,
        )

    units = width // UNIT
    weight = output_weight.reshape(n_tensor * units, UNIT, columns)
    gathered, x, first = [], attention_result, 0
    for features in GATHERED:
        piece = x[:, first:first + features]
        gathered.append(lax.all_gather(piece, "tensor", axis=0))
        x = after(x, piece)
        first += features + LINE

    middle = GATHERED[0]
    last = middle + LINE
    line = x[None, :, middle:last]
    right = [(i, i + 1) for i in range(n_tensor - 1)]
    left = [(i + 1, i) for i in range(n_tensor - 1)]
    right_1 = lax.ppermute(line, "tensor", right)
    left_1 = lax.ppermute(line, "tensor", left)

    slots, places = asked_pages(requests, adapter_page_row, holder_length)
    downs, ups = [], []
    for j in range(n_dp):
        down, up = pick_pages(places[j], adapter_down_weight, adapter_up_weight, n_tensor)
        if j:
            pairs = [(i, i ^ j) for i in range(n_dp)]
            down, up = lax.ppermute(down, "dp", pairs), lax.ppermute(up, "dp", pairs)
        downs.append(down)
        ups.append(up)

    right_2 = lax.ppermute(right_1, "tensor", right[1:])
    left_2 = lax.ppermute(left_1, "tensor", left[:-1])
    upper = me >= n_tensor // 2
    second = jnp.where(upper, right_2, left_2)
    third = lax.ppermute(second, "tensor", right[-1:] + left[:1])
    down = join_downs(after(tuple(downs), third))
    up = join_ups(ups)

    slot = jnp.sum(jnp.where(one_hot, slots[None, :], 0), axis=1)[:, None]
    live = row_rank[:, None] - me * rank_part
    every = jnp.arange(n_tensor)

    def places_of(*spans):
        unit, valid = [], []
        for source, first, length in spans:
            source = jnp.atleast_1d(source)
            there = (source >= 0) & (source < n_tensor)
            source = jnp.clip(source, 0, n_tensor - 1)
            ids = source[:, None] * units + first // UNIT + jnp.arange(length // UNIT)[None, :]
            unit.append(ids.reshape(-1))
            valid.append(jnp.broadcast_to(there[:, None], ids.shape).reshape(-1))
        return jnp.concatenate(unit).astype(jnp.int32), jnp.concatenate(valid).astype(jnp.int32)

    near = places_of(*[(me + o, middle, LINE) for o in (0, -1, 1)])
    totals = add_chunk((), [line, right_1, left_1], *near, weight, down)
    toward = jnp.where(upper, -1, 1)
    far = places_of((me + 2 * toward, middle, LINE), (me + 3 * toward, middle, LINE), (every, 0, GATHERED[0]))
    totals = add_chunk(totals, [second, third, gathered[0]], *far, weight, down)
    x = pltpu.with_memory_space_constraint(after(gathered[1], *totals, up), pltpu.HBM)
    at = places_of((every, last, GATHERED[1]))
    low, = add_chunk(totals[1:], [x], *at, None, down, (slot, live), rank_part)
    base, = add_chunk(totals[:1], [x], *at, weight)
    lows = [low] + [
        lax.ppermute(low, "tensor", [(i, (i - j) % n_tensor) for i in range(n_tensor)])
        for j in range(1, n_tensor)
    ]
    return finish(me[None], slot, base, up, lows)


def gather_pages(block, n_dp):
    return [block] + [
        lax.ppermute(block, "dp", [(i, i ^ j) for i in range(n_dp)]) for j in range(1, n_dp)
    ]


def plain(x, output_weight, down_weight, up_weight, adapter_page_row, own_list, one_hot, row_rank):
    n_dp = lax.axis_size("dp")
    dp = lax.axis_index("dp")
    rows = x.shape[0]
    holder_length = down_weight.shape[0]
    rank, columns = up_weight.shape[1:]
    entries = one_hot.shape[1]
    pages = adapter_page_row[own_list]
    places = ((pages // holder_length) ^ dp) * holder_length + pages % holder_length

    def requested(block):
        blocks = jnp.concatenate(gather_pages(block, n_dp), axis=0)
        return jnp.concatenate(
            [lax.dynamic_slice_in_dim(blocks, places[e], 1, 0) for e in range(entries)], axis=0
        )

    down, up = requested(down_weight), requested(up_weight)
    x = lax.all_gather(x, "tensor", axis=1, tiled=True)
    base = jnp.dot(x, output_weight, preferred_element_type=F32)
    low = jnp.einsum("rd,ekd->rek", x, down, preferred_element_type=F32)
    low = jnp.sum(jnp.where(one_hot[:, :, None], low, 0.0), axis=1).astype(BF16)
    low = lax.all_gather(low, "tensor", axis=1, tiled=True)
    low = jnp.where(jnp.arange(rank)[None, :] < row_rank[:, None], low, jnp.zeros_like(low))
    spread = jnp.where(one_hot[:, :, None], low[:, None, :], jnp.zeros((), BF16))
    term = jnp.dot(
        spread.reshape(rows, entries * rank), up.reshape(entries * rank, columns), preferred_element_type=F32
    )
    return (base + term).astype(BF16)


def solution(mesh):
    in_specs = (
        P(("groups", "dp"), "tensor"),
        P(None, "tensor"),
        P("dp", "tensor", None),
        P("dp", None, "tensor"),
        P("groups"),
        P(("groups", "dp"), None),
        P(("groups", "dp")),
        P(),
    )
    out_specs = P(("groups", "dp"), "tensor")
    return jax.shard_map(local, mesh=mesh, in_specs=in_specs, out_specs=out_specs, check_vma=False)
```

```python
import functools

import jax
import jax.numpy as jnp
from jax import lax
from jax.experimental import pallas as pl
from jax.experimental.pallas import tpu as pltpu
from jax.sharding import PartitionSpec as P

CAP = 2
ALIGN = 256
LINE = 512
GATHERED = (1280, 256)
PARAMS = pltpu.CompilerParams(vmem_limit_bytes=48 * 2**20)
TAIL_PARAMS = pltpu.CompilerParams(vmem_limit_bytes=24 * 2**20)
F32 = jnp.float32
BF16 = jnp.bfloat16


def pick_kernel(places, down, up, down_out, up_out):
    shards, _, width = down_out.shape[1:]
    for t in range(shards):
        down_out[0, t] = down[0, :, t * width:(t + 1) * width]
    up_out[...] = up[...]


def pick_pages(places, down, up, shards):
    count = places.shape[0]
    _, rank_part, features = down.shape
    shapes = [(shards, rank_part, features // shards), up.shape[1:]]
    return pl.pallas_call(
        pick_kernel,
        out_shape=[jax.ShapeDtypeStruct((count,) + shape, BF16) for shape in shapes],
        grid_spec=pltpu.PrefetchScalarGridSpec(
            num_scalar_prefetch=1,
            grid=(count,),
            in_specs=[pl.BlockSpec((1,) + a.shape[1:], lambda i, places: (places[i], 0, 0)) for a in (down, up)],
            out_specs=[
                pl.BlockSpec((1,) + shapes[0], lambda i, places: (i, 0, 0, 0)),
                pl.BlockSpec((1,) + shapes[1], lambda i, places: (i, 0, 0)),
            ],
        ),
        compiler_params=PARAMS,
    )(places, down, up)


def join_downs_kernel(*refs):
    *pages, out = refs
    joined = jnp.concatenate([p[c, 0] for p in pages for c in range(CAP)], axis=0)
    out[...] = joined.T


def join_downs(downs):
    _, shards, rank_part, features = downs[0].shape
    slots = CAP * rank_part * len(downs)
    return pl.pallas_call(
        join_downs_kernel,
        out_shape=jax.ShapeDtypeStruct((shards * features, slots), BF16),
        grid=(shards,),
        in_specs=[pl.BlockSpec((CAP, 1, rank_part, features), lambda t: (0, t, 0, 0))] * len(downs),
        out_specs=pl.BlockSpec((features, slots), lambda t: (t, 0)),
        compiler_params=PARAMS,
    )(*downs)


def join_ups_kernel(*refs):
    *pages, out = refs
    for j, p in enumerate(pages):

        @pl.when(pl.program_id(0) == j)
        def _():
            out[...] = p[...]


def join_ups(ups):
    count, rank, columns = ups[0].shape
    return pl.pallas_call(
        join_ups_kernel,
        out_shape=jax.ShapeDtypeStruct((count * len(ups), rank, columns), BF16),
        grid=(len(ups),),
        in_specs=[pl.BlockSpec(up.shape, lambda j: (0, 0, 0)) for up in ups],
        out_specs=pl.BlockSpec(ups[0].shape, lambda j: (j, 0, 0)),
        compiler_params=PARAMS,
    )(*ups).reshape(-1, columns)


RESIDENT = pl.BlockSpec(memory_space=pltpu.VMEM)
IN_HBM = pl.BlockSpec(memory_space=pltpu.HBM)


def chunk_kernel(counts, held, start, valid, *refs):
    refs = list(refs)
    xs = [refs.pop(0) for _ in counts]
    weight, down = refs.pop(0), refs.pop(0)
    totals, (base, low) = refs[:-2], refs[-2:]
    step = pl.program_id(0)

    @pl.when(step == 0)
    def _():
        base[...] = totals[0][...] if held else jnp.zeros_like(base)
        low[...] = totals[1][...] if held else jnp.zeros_like(low)

    first = 0
    for x, count in zip(xs, counts):

        @pl.when((step >= first) & (step < first + count) & (valid[step] != 0))
        def _():
            part = min(base.shape[1], 512)
            for n in range(0, base.shape[1], part):
                base[:, n:n + part] += jnp.dot(x[0], weight[:, n:n + part], preferred_element_type=F32)
            low[...] += jnp.dot(x[0], down[...], preferred_element_type=F32)

        first += count


def add_chunk(totals, xs, source, first, weight, down):
    rows, features = xs[0].shape[1:]
    columns, slots = weight.shape[1], down.shape[1]
    counts = [x.shape[0] for x in xs]
    steps = sum(counts)
    n_tensor = lax.axis_size("tensor")
    valid = ((source >= 0) & (source < n_tensor)).astype(jnp.int32)
    start = (jnp.clip(source, 0, n_tensor - 1) * (weight.shape[0] // n_tensor) + first) // ALIGN
    start = start.astype(jnp.int32)
    x_specs, begin = [], 0
    for count in counts:
        x_specs.append(
            pl.BlockSpec(
                (1, rows, features),
                lambda s, *_, begin=begin, count=count: (jnp.clip(s - begin, 0, count - 1), 0, 0),
            )
        )
        begin += count
    walked = [
        pl.BlockSpec((pl.Element(features), pl.Element(a)), lambda s, start, valid: (start[s] * ALIGN, 0))
        for a in (columns, slots)
    ]
    whole = [pl.BlockSpec((rows, a), lambda s, *_: (0, 0)) for a in (columns, slots)]
    return pl.pallas_call(
        functools.partial(chunk_kernel, counts, bool(totals)),
        out_shape=[jax.ShapeDtypeStruct((rows, a), F32) for a in (columns, slots)],
        grid_spec=pltpu.PrefetchScalarGridSpec(
            num_scalar_prefetch=2,
            grid=(steps,),
            in_specs=x_specs + walked + (whole if totals else []),
            out_specs=whole,
        ),
        compiler_params=PARAMS,
        cost_estimate=pl.CostEstimate(
            flops=2 * steps * features * rows * (columns + slots),
            bytes_accessed=2 * steps * features * (rows + columns + slots) + 8 * rows * (columns + slots),
            transcendentals=0,
        ),
    )(start, valid, *xs, weight, down, *totals)


def low_kernel(first, x_hbm, down, total, slot, live, out, x, rows_of, sems):
    shards, _, features = x.shape
    width = down.shape[0] // shards
    rank_part = out.shape[1]
    copies = [
        pltpu.make_async_copy(down.at[pl.ds(t * width + first, features)], rows_of.at[t], sems.at[t])
        for t in range(shards)
    ]
    copies += [pltpu.make_async_copy(x_hbm.at[t], x.at[t], sems.at[shards + t]) for t in range(shards)]
    for copy in copies:
        copy.start()
    low = total[...]
    for t in range(shards):
        copies[t].wait()
        copies[shards + t].wait()
        low += jnp.dot(x[t], rows_of[t], preferred_element_type=F32)
    lane = lax.broadcasted_iota(jnp.int32, low.shape, 1)
    own = jnp.where(lane // rank_part == slot[...], low, 0.0).astype(BF16)
    fold = (
        lax.rem(lax.broadcasted_iota(jnp.int32, (low.shape[1], rank_part), 0), rank_part)
        == lax.broadcasted_iota(jnp.int32, (low.shape[1], rank_part), 1)
    ).astype(BF16)
    mine = jnp.dot(own, fold, preferred_element_type=F32)
    k = lax.broadcasted_iota(jnp.int32, mine.shape, 1)
    out[...] = jnp.where(k < live[...], mine, 0.0).astype(BF16)


def finish_low(total, x, first, down, slot, live, rank_part):
    shards, rows, features = x.shape
    slots = down.shape[1]
    return pl.pallas_call(
        functools.partial(low_kernel, first),
        out_shape=jax.ShapeDtypeStruct((rows, rank_part), BF16),
        in_specs=[IN_HBM, IN_HBM, RESIDENT, RESIDENT, RESIDENT],
        out_specs=RESIDENT,
        scratch_shapes=[
            pltpu.VMEM(x.shape, BF16),
            pltpu.VMEM((shards, features, slots), BF16),
            pltpu.SemaphoreType.DMA((2 * shards,)),
        ],
        compiler_params=TAIL_PARAMS,
        cost_estimate=pl.CostEstimate(
            flops=2 * shards * features * rows * slots,
            bytes_accessed=2 * shards * features * (rows + slots) + 4 * rows * slots,
            transcendentals=0,
        ),
    )(x, down, total, slot, live)


def base_kernel(first, x, weight, total, up, out, up_out, xs, ws, ts, sems, up_sem):
    shards, rows, features = x.shape
    columns = out.shape[1]
    parts, _, _, part = ws.shape
    width = weight.shape[0] // shards
    for t in range(shards):
        pltpu.make_async_copy(x.at[t], xs.at[t], sems.at[parts, t]).start()

    def copies(n):
        cut = pl.ds(n * part, part)
        return [
            pltpu.make_async_copy(
                weight.at[pl.ds(t * width + first, features), cut], ws.at[n, t], sems.at[n, t]
            )
            for t in range(shards)
        ] + [pltpu.make_async_copy(total.at[:, cut], ts.at[n], sems.at[n, shards])]

    for n in range(parts):
        for copy in copies(n):
            copy.start()
    pltpu.make_async_copy(up, up_out, up_sem).start()
    for t in range(shards):
        pltpu.make_async_copy(x.at[t], xs.at[t], sems.at[parts, t]).wait()
    joined = jnp.concatenate([xs[t] for t in range(shards)], axis=1)
    for n in range(parts):
        for copy in copies(n):
            copy.wait()
        w = ws[n].reshape(shards * features, part)
        out[:, n * part:(n + 1) * part] = ts[n] + jnp.dot(joined, w, preferred_element_type=F32)
    pltpu.make_async_copy(up, up_out, up_sem).wait()


def add_last(total, x, first, weight, up):
    shards, rows, features = x.shape
    columns = weight.shape[1]
    part = min(columns, 512)
    parts = columns // part
    return pl.pallas_call(
        functools.partial(base_kernel, first),
        out_shape=[pltpu.VMEM((rows, columns), F32), pltpu.VMEM(up.shape, BF16)],
        in_specs=[IN_HBM] * 4,
        out_specs=[RESIDENT] * 2,
        scratch_shapes=[
            pltpu.VMEM((shards, rows, features), BF16),
            pltpu.VMEM((parts, shards, features, part), BF16),
            pltpu.VMEM((parts, rows, part), F32),
            pltpu.SemaphoreType.DMA((parts + 1, shards + 1)),
            pltpu.SemaphoreType.DMA,
        ],
        compiler_params=TAIL_PARAMS,
        cost_estimate=pl.CostEstimate(
            flops=2 * shards * features * rows * columns,
            bytes_accessed=2 * shards * features * (rows + columns) + 4 * rows * columns,
            transcendentals=0,
        ),
    )(x, weight, total, up)


def finish_kernel(parts, me, slot, total, up, *refs):
    lows, (out, spread) = refs[:parts], refs[parts:]
    rank_part = lows[0].shape[1]
    rank = parts * rank_part
    part = out.shape[1]

    @pl.when(pl.program_id(0) == 0)
    def _():
        low = jnp.concatenate([part[...].astype(F32) for part in lows], axis=1)
        low = pltpu.roll(low, me[0] * rank_part, 1)
        for e in range(spread.shape[1] // rank):
            spread[:, e * rank:(e + 1) * rank] = jnp.where(slot[...] == e, low, 0.0).astype(BF16)

    cut = pl.ds(pl.multiple_of(pl.program_id(0) * part, part), part)
    out[...] = (total[:, cut] + jnp.dot(spread[...], up[:, cut], preferred_element_type=F32)).astype(BF16)


def finish(me, slot, total, up, lows):
    rows, columns = total.shape
    depth = up.shape[0]
    part = min(columns, 512)
    return pl.pallas_call(
        functools.partial(finish_kernel, len(lows)),
        grid=(columns // part,),
        out_shape=jax.ShapeDtypeStruct((rows, columns), BF16),
        in_specs=[pl.BlockSpec(memory_space=pltpu.SMEM)] + [RESIDENT] * (3 + len(lows)),
        out_specs=pl.BlockSpec((rows, part), lambda n: (0, n)),
        scratch_shapes=[pltpu.VMEM((rows, depth), BF16)],
        compiler_params=TAIL_PARAMS,
        cost_estimate=pl.CostEstimate(
            flops=2 * rows * depth * columns,
            bytes_accessed=2 * rows * columns,
            transcendentals=0,
        ),
    )(me, slot, total, up, *lows)


def after(value, *earlier):
    return lax.optimization_barrier((value,) + earlier)[0]


def asked_pages(requests, adapter_page_row, holder_length):
    n_dp = lax.axis_size("dp")
    dp = lax.axis_index("dp")
    count = adapter_page_row.shape[0]

    def pages_of(wanted):
        hit = wanted[:, None] == jnp.arange(count)[None, :]
        return jnp.sum(jnp.where(hit, adapter_page_row[None, :], 0), axis=1)

    def order_in(holders):
        same = holders[:, None] == holders[None, :]
        n = holders.shape[0]
        earlier = jnp.arange(n)[:, None] > jnp.arange(n)[None, :]
        return jnp.sum((same & earlier).astype(jnp.int32), axis=1)

    own = pages_of(requests[0])
    holders = own // holder_length
    slots = (holders ^ dp) * CAP + order_in(holders)
    places = []
    for j in range(n_dp):
        wanted = requests if j == 0 else lax.ppermute(requests, "dp", [(i, i ^ j) for i in range(n_dp)])
        pages = pages_of(wanted[0])
        holder = pages // holder_length
        order = jnp.where(holder == dp, order_in(holder), -1)
        hit = order[None, :] == jnp.arange(CAP)[:, None]
        places.append(jnp.sum(jnp.where(hit, (pages % holder_length)[None, :], 0), axis=1))
    return slots, places


def local(
    attention_result,
    output_weight,
    adapter_down_weight,
    adapter_up_weight,
    adapter_page_row,
    requests,
    row_request_entry,
    ranks,
):
    n_dp = lax.axis_size("dp")
    n_tensor = lax.axis_size("tensor")
    me = lax.axis_index("tensor")
    rows, width = attention_result.shape
    holder_length, rank_part, _ = adapter_down_weight.shape
    rank, columns = adapter_up_weight.shape[1:]
    own_list = requests[0]
    entries = own_list.shape[0]
    one_hot = row_request_entry[:, None] == jnp.arange(entries)[None, :]
    row_rank = jnp.sum(jnp.where(one_hot, ranks[own_list][None, :], 0), axis=1)
    if n_tensor != 4 or width != LINE + sum(GATHERED) or rank_part % 16:
        return plain(
            attention_result, output_weight, adapter_down_weight, adapter_up_weight, adapter_page_row,
            own_list, one_hot, row_rank,
        )

    gathered, x, first = [], attention_result, 0
    for features in GATHERED:
        piece = x[:, first:first + features]
        gathered.append(lax.all_gather(piece, "tensor", axis=0))
        x = after(x, piece)
        first += features + LINE

    middle = GATHERED[0]
    last = middle + LINE
    line = x[None, :, middle:last]
    right = [(i, i + 1) for i in range(n_tensor - 1)]
    left = [(i + 1, i) for i in range(n_tensor - 1)]
    right_1 = lax.ppermute(line, "tensor", right)
    left_1 = lax.ppermute(line, "tensor", left)

    slots, places = asked_pages(requests, adapter_page_row, holder_length)
    downs, ups = [], []
    for j in range(n_dp):
        down, up = pick_pages(places[j], adapter_down_weight, adapter_up_weight, n_tensor)
        if j:
            pairs = [(i, i ^ j) for i in range(n_dp)]
            down, up = lax.ppermute(down, "dp", pairs), lax.ppermute(up, "dp", pairs)
        downs.append(down)
        ups.append(up)

    right_2 = lax.ppermute(right_1, "tensor", right[1:])
    left_2 = lax.ppermute(left_1, "tensor", left[:-1])
    upper = me >= n_tensor // 2
    second = jnp.where(upper, right_2, left_2)
    third = lax.ppermute(second, "tensor", right[-1:] + left[:1])
    down = join_downs(after(tuple(downs), third))
    up = join_ups(ups)

    slot = jnp.sum(jnp.where(one_hot, slots[None, :], 0), axis=1)[:, None]
    live = row_rank[:, None] - me * rank_part
    toward = jnp.where(upper, -1, 1)
    source = me + jnp.stack([jnp.zeros_like(me), -jnp.ones_like(me), jnp.ones_like(me), 2 * toward, 3 * toward])
    blocks = [line, right_1, left_1, second, third]
    totals = add_chunk((), blocks, source, middle, output_weight, down)
    totals = add_chunk(totals, gathered[:1], jnp.arange(n_tensor), 0, output_weight, down)
    x = pltpu.with_memory_space_constraint(after(gathered[1], *totals, up), pltpu.HBM)
    low = finish_low(totals[1], x, last, down, slot, live, rank_part)
    base, up = add_last(totals[0], x, last, output_weight, up)
    lows = [low] + [
        lax.ppermute(low, "tensor", [(i, (i - j) % n_tensor) for i in range(n_tensor)])
        for j in range(1, n_tensor)
    ]
    return finish(me[None], slot, base, up, lows)


def gather_pages(block, n_dp):
    return [block] + [
        lax.ppermute(block, "dp", [(i, i ^ j) for i in range(n_dp)]) for j in range(1, n_dp)
    ]


def plain(x, output_weight, down_weight, up_weight, adapter_page_row, own_list, one_hot, row_rank):
    n_dp = lax.axis_size("dp")
    dp = lax.axis_index("dp")
    rows = x.shape[0]
    holder_length = down_weight.shape[0]
    rank, columns = up_weight.shape[1:]
    entries = one_hot.shape[1]
    pages = adapter_page_row[own_list]
    places = ((pages // holder_length) ^ dp) * holder_length + pages % holder_length

    def requested(block):
        blocks = jnp.concatenate(gather_pages(block, n_dp), axis=0)
        return jnp.concatenate(
            [lax.dynamic_slice_in_dim(blocks, places[e], 1, 0) for e in range(entries)], axis=0
        )

    down, up = requested(down_weight), requested(up_weight)
    x = lax.all_gather(x, "tensor", axis=1, tiled=True)
    base = jnp.dot(x, output_weight, preferred_element_type=F32)
    low = jnp.einsum("rd,ekd->rek", x, down, preferred_element_type=F32)
    low = jnp.sum(jnp.where(one_hot[:, :, None], low, 0.0), axis=1).astype(BF16)
    low = lax.all_gather(low, "tensor", axis=1, tiled=True)
    low = jnp.where(jnp.arange(rank)[None, :] < row_rank[:, None], low, jnp.zeros_like(low))
    spread = jnp.where(one_hot[:, :, None], low[:, None, :], jnp.zeros((), BF16))
    term = jnp.dot(
        spread.reshape(rows, entries * rank), up.reshape(entries * rank, columns), preferred_element_type=F32
    )
    return (base + term).astype(BF16)


def solution(mesh):
    in_specs = (
        P(("groups", "dp"), "tensor"),
        P(None, "tensor"),
        P("dp", "tensor", None),
        P("dp", None, "tensor"),
        P("groups"),
        P(("groups", "dp"), None),
        P(("groups", "dp")),
        P(),
    )
    out_specs = P(("groups", "dp"), "tensor")
    return jax.shard_map(local, mesh=mesh, in_specs=in_specs, out_specs=out_specs, check_vma=False)
```

```python
import functools

import jax
import jax.numpy as jnp
from jax import lax
from jax.experimental import pallas as pl
from jax.experimental.pallas import tpu as pltpu
from jax.sharding import PartitionSpec as P

CAP = 2
HALF = 1024
PARAMS = pltpu.CompilerParams(vmem_limit_bytes=48 * 2**20)
TAIL_PARAMS = pltpu.CompilerParams(vmem_limit_bytes=24 * 2**20)
F32 = jnp.float32
BF16 = jnp.bfloat16


def pick_kernel(places, down, up, down_out, up_out):
    shards, _, width = down_out.shape[1:]
    for t in range(shards):
        down_out[0, t] = down[0, :, t * width:(t + 1) * width]
    up_out[...] = up[...]


def pick_pages(places, down, up, shards):
    count = places.shape[0]
    _, rank_part, features = down.shape
    shapes = [(shards, rank_part, features // shards), up.shape[1:]]
    return pl.pallas_call(
        pick_kernel,
        out_shape=[jax.ShapeDtypeStruct((count,) + shape, BF16) for shape in shapes],
        grid_spec=pltpu.PrefetchScalarGridSpec(
            num_scalar_prefetch=1,
            grid=(count,),
            in_specs=[pl.BlockSpec((1,) + a.shape[1:], lambda i, places: (places[i], 0, 0)) for a in (down, up)],
            out_specs=[
                pl.BlockSpec((1,) + shapes[0], lambda i, places: (i, 0, 0, 0)),
                pl.BlockSpec((1,) + shapes[1], lambda i, places: (i, 0, 0)),
            ],
        ),
        compiler_params=PARAMS,
    )(places, down, up)


def join_downs_kernel(*refs):
    *pages, out = refs
    joined = jnp.concatenate([p[c, 0] for p in pages for c in range(CAP)], axis=0)
    out[...] = joined.T


def join_downs(downs):
    _, shards, rank_part, features = downs[0].shape
    slots = CAP * rank_part * len(downs)
    return pl.pallas_call(
        join_downs_kernel,
        out_shape=jax.ShapeDtypeStruct((shards * features, slots), BF16),
        grid=(shards,),
        in_specs=[pl.BlockSpec((CAP, 1, rank_part, features), lambda t: (0, t, 0, 0))] * len(downs),
        out_specs=pl.BlockSpec((features, slots), lambda t: (t, 0)),
        compiler_params=PARAMS,
    )(*downs)


def join_ups_kernel(*refs):
    *pages, out = refs
    for j, p in enumerate(pages):

        @pl.when(pl.program_id(0) == j)
        def _():
            out[...] = p[...]


def join_ups(ups):
    count, rank, columns = ups[0].shape
    return pl.pallas_call(
        join_ups_kernel,
        out_shape=jax.ShapeDtypeStruct((count * len(ups), rank, columns), BF16),
        grid=(len(ups),),
        in_specs=[pl.BlockSpec(up.shape, lambda j: (0, 0, 0)) for up in ups],
        out_specs=pl.BlockSpec(ups[0].shape, lambda j: (j, 0, 0)),
        compiler_params=PARAMS,
    )(*ups).reshape(-1, columns)


RESIDENT = pl.BlockSpec(memory_space=pltpu.VMEM)
IN_HBM = pl.BlockSpec(memory_space=pltpu.HBM)


def chunk_kernel(count, halves, held, with_base, with_low, start, valid, *refs):
    refs = list(refs)
    xs = [refs.pop(0) for _ in range(count)]
    weight = refs.pop(0) if with_base else None
    down = refs.pop(0) if with_low else None
    outs = [refs.pop() for _ in range(with_base + with_low)][::-1]
    step = pl.program_id(0)

    @pl.when(step == 0)
    def _():
        for i, out in enumerate(outs):
            out[...] = refs[i][...] if held else jnp.zeros_like(out)

    for i, x in enumerate(xs):

        @pl.when((step >= i * halves) & (step < (i + 1) * halves) & (valid[step] != 0))
        def _():
            if with_base:
                base = outs[0]
                part = min(base.shape[1], 512)
                for n in range(0, base.shape[1], part):
                    base[:, n:n + part] += jnp.dot(x[...], weight[:, n:n + part], preferred_element_type=F32)
            if with_low:
                outs[-1][...] += jnp.dot(x[...], down[...], preferred_element_type=F32)


def add_chunk(totals, xs, source, weight, down):
    rows, width = xs[0].shape
    walked = [a for a in (weight, down) if a is not None]
    n_tensor = walked[0].shape[0] // width
    halves = width // HALF
    steps = len(xs) * halves
    valid = jnp.repeat(((source >= 0) & (source < n_tensor)).astype(jnp.int32), halves)
    start = jnp.clip(source, 0, n_tensor - 1)[:, None] * halves + jnp.arange(halves)[None, :]
    start = start.reshape(-1).astype(jnp.int32)
    whole = [pl.BlockSpec((rows, a.shape[1]), lambda s, *_: (0, 0)) for a in walked]
    columns = sum(a.shape[1] for a in walked)
    return pl.pallas_call(
        functools.partial(chunk_kernel, len(xs), halves, bool(totals), weight is not None, down is not None),
        out_shape=[jax.ShapeDtypeStruct((rows, a.shape[1]), F32) for a in walked],
        grid_spec=pltpu.PrefetchScalarGridSpec(
            num_scalar_prefetch=2,
            grid=(steps,),
            in_specs=[
                pl.BlockSpec((rows, HALF), lambda s, *_, i=i: (0, jnp.clip(s - i * halves, 0, halves - 1)))
                for i in range(len(xs))
            ]
            + [pl.BlockSpec((HALF, a.shape[1]), lambda s, start, valid: (start[s], 0)) for a in walked]
            + (whole if totals else []),
            out_specs=whole,
        ),
        compiler_params=PARAMS,
        cost_estimate=pl.CostEstimate(
            flops=2 * len(xs) * width * rows * columns,
            bytes_accessed=2 * len(xs) * width * (rows + columns) + 8 * rows * columns,
            transcendentals=0,
        ),
    )(start, valid, *xs, *walked, *totals)


def pin_kernel(source, weight, down, base, low, up, weight_out, down_out, base_out, low_out, up_out, sems):
    width = weight_out.shape[0]
    rows = pl.ds(pl.multiple_of(source[0] * width, width), width)
    pairs = [
        (weight.at[rows], weight_out), (down.at[rows], down_out), (base, base_out), (low, low_out), (up, up_out)
    ]
    copies = [pltpu.make_async_copy(a, b, sems.at[i]) for i, (a, b) in enumerate(pairs)]
    for copy in copies:
        copy.start()
    for copy in copies:
        copy.wait()


def pin(source, width, weight, down, base, low, up):
    shapes = [((width,) + a.shape[1:], a.dtype) for a in (weight, down)]
    shapes += [(a.shape, a.dtype) for a in (base, low, up)]
    return pl.pallas_call(
        pin_kernel,
        out_shape=[pltpu.VMEM(*a) for a in shapes],
        in_specs=[pl.BlockSpec(memory_space=pltpu.SMEM)] + [IN_HBM] * 5,
        out_specs=[RESIDENT] * 5,
        scratch_shapes=[pltpu.SemaphoreType.DMA((5,))],
        compiler_params=TAIL_PARAMS,
        cost_estimate=pl.CostEstimate(
            flops=0, bytes_accessed=sum(a[0] * a[1] for a, _ in shapes) * 3, transcendentals=0
        ),
    )(source, weight, down, base, low, up)


def low_kernel(rank_part, which, from_left, from_right, down, total, slot, live, out, x, sem):
    @pl.when(which[0] > 0)
    def _():
        pltpu.make_async_copy(from_left, x, sem).start()

    @pl.when(which[0] < 0)
    def _():
        pltpu.make_async_copy(from_right, x, sem).start()

    @pl.when(which[0] != 0)
    def _():
        pltpu.make_async_copy(from_left, x, sem).wait()

    @pl.when(which[0] == 0)
    def _():
        x[...] = jnp.zeros_like(x)

    low = total[...] + jnp.dot(x[...], down[...], preferred_element_type=F32)
    lane = lax.broadcasted_iota(jnp.int32, low.shape, 1)
    own = jnp.where(lane // rank_part == slot[...], low, 0.0).astype(BF16)
    fold = (
        lax.rem(lax.broadcasted_iota(jnp.int32, (low.shape[1], rank_part), 0), rank_part)
        == lax.broadcasted_iota(jnp.int32, (low.shape[1], rank_part), 1)
    ).astype(BF16)
    mine = jnp.dot(own, fold, preferred_element_type=F32)
    k = lax.broadcasted_iota(jnp.int32, mine.shape, 1)
    out[...] = jnp.where(k < live[...], mine, 0.0).astype(BF16)


def finish_low(which, from_left, from_right, down, total, slot, live, rank_part):
    rows, width = from_left.shape
    slots = down.shape[1]
    return pl.pallas_call(
        functools.partial(low_kernel, rank_part),
        out_shape=[pltpu.VMEM((rows, rank_part), BF16), pltpu.VMEM((rows, width), BF16)],
        in_specs=[pl.BlockSpec(memory_space=pltpu.SMEM), IN_HBM, IN_HBM] + [RESIDENT] * 4,
        out_specs=[RESIDENT] * 2,
        scratch_shapes=[pltpu.SemaphoreType.DMA],
        compiler_params=TAIL_PARAMS,
        cost_estimate=pl.CostEstimate(
            flops=2 * width * rows * slots, bytes_accessed=2 * width * rows, transcendentals=0
        ),
    )(which, from_left, from_right, down, total, slot, live)


def base_kernel(which, x, weight, total, out):
    @pl.when(which[0] != 0)
    def _():
        part = min(out.shape[1], 512)
        for n in range(0, out.shape[1], part):
            out[:, n:n + part] = total[:, n:n + part] + jnp.dot(
                x[...], weight[:, n:n + part], preferred_element_type=F32
            )


def add_last(which, x, weight, total):
    rows, width = x.shape
    columns = weight.shape[1]
    return pl.pallas_call(
        base_kernel,
        out_shape=pltpu.VMEM((rows, columns), F32),
        in_specs=[pl.BlockSpec(memory_space=pltpu.SMEM)] + [RESIDENT] * 3,
        out_specs=RESIDENT,
        input_output_aliases={3: 0},
        compiler_params=TAIL_PARAMS,
        cost_estimate=pl.CostEstimate(flops=2 * width * rows * columns, bytes_accessed=0, transcendentals=0),
    )(which, x, weight, total)


def finish_kernel(parts, me, slot, total, up, *refs):
    lows, (out, spread) = refs[:parts], refs[parts:]
    rank_part = lows[0].shape[1]
    rank = parts * rank_part
    part = out.shape[1]

    @pl.when(pl.program_id(0) == 0)
    def _():
        low = jnp.concatenate([part[...].astype(F32) for part in lows], axis=1)
        low = pltpu.roll(low, me[0] * rank_part, 1)
        for e in range(spread.shape[1] // rank):
            spread[:, e * rank:(e + 1) * rank] = jnp.where(slot[...] == e, low, 0.0).astype(BF16)

    cut = pl.ds(pl.multiple_of(pl.program_id(0) * part, part), part)
    out[...] = (total[:, cut] + jnp.dot(spread[...], up[:, cut], preferred_element_type=F32)).astype(BF16)


def finish(me, slot, total, up, lows):
    rows, columns = total.shape
    depth = up.shape[0]
    part = min(columns, 512)
    return pl.pallas_call(
        functools.partial(finish_kernel, len(lows)),
        grid=(columns // part,),
        out_shape=jax.ShapeDtypeStruct((rows, columns), BF16),
        in_specs=[pl.BlockSpec(memory_space=pltpu.SMEM)] + [RESIDENT] * (3 + len(lows)),
        out_specs=pl.BlockSpec((rows, part), lambda n: (0, n)),
        scratch_shapes=[pltpu.VMEM((rows, depth), BF16)],
        compiler_params=TAIL_PARAMS,
        cost_estimate=pl.CostEstimate(
            flops=2 * rows * depth * columns,
            bytes_accessed=2 * rows * columns,
            transcendentals=0,
        ),
    )(me, slot, total, up, *lows)


def after(value, *earlier):
    return lax.optimization_barrier((value,) + earlier)[0]


def asked_pages(requests, adapter_page_row, holder_length):
    n_dp = lax.axis_size("dp")
    dp = lax.axis_index("dp")
    count = adapter_page_row.shape[0]

    def pages_of(wanted):
        hit = wanted[:, None] == jnp.arange(count)[None, :]
        return jnp.sum(jnp.where(hit, adapter_page_row[None, :], 0), axis=1)

    def order_in(holders):
        same = holders[:, None] == holders[None, :]
        n = holders.shape[0]
        earlier = jnp.arange(n)[:, None] > jnp.arange(n)[None, :]
        return jnp.sum((same & earlier).astype(jnp.int32), axis=1)

    own = pages_of(requests[0])
    holders = own // holder_length
    slots = (holders ^ dp) * CAP + order_in(holders)
    places = []
    for j in range(n_dp):
        wanted = requests if j == 0 else lax.ppermute(requests, "dp", [(i, i ^ j) for i in range(n_dp)])
        pages = pages_of(wanted[0])
        holder = pages // holder_length
        order = jnp.where(holder == dp, order_in(holder), -1)
        hit = order[None, :] == jnp.arange(CAP)[:, None]
        places.append(jnp.sum(jnp.where(hit, (pages % holder_length)[None, :], 0), axis=1))
    return slots, places


def local(
    attention_result,
    output_weight,
    adapter_down_weight,
    adapter_up_weight,
    adapter_page_row,
    requests,
    row_request_entry,
    ranks,
):
    n_dp = lax.axis_size("dp")
    n_tensor = lax.axis_size("tensor")
    me = lax.axis_index("tensor")
    rows, width = attention_result.shape
    holder_length, rank_part, _ = adapter_down_weight.shape
    rank, columns = adapter_up_weight.shape[1:]
    own_list = requests[0]
    entries = own_list.shape[0]
    one_hot = row_request_entry[:, None] == jnp.arange(entries)[None, :]
    row_rank = jnp.sum(jnp.where(one_hot, ranks[own_list][None, :], 0), axis=1)
    if n_tensor != 4 or width % HALF or rank_part % 16:
        return plain(
            attention_result, output_weight, adapter_down_weight, adapter_up_weight, adapter_page_row,
            own_list, one_hot, row_rank,
        )

    right = [(i, i + 1) for i in range(n_tensor - 1)]
    left = [(i + 1, i) for i in range(n_tensor - 1)]
    own = attention_result
    right_1 = lax.ppermute(own, "tensor", right)
    left_1 = lax.ppermute(own, "tensor", left)

    slots, places = asked_pages(requests, adapter_page_row, holder_length)
    downs, ups = [], []
    for j in range(n_dp):
        down, up = pick_pages(places[j], adapter_down_weight, adapter_up_weight, n_tensor)
        if j:
            pairs = [(i, i ^ j) for i in range(n_dp)]
            down = lax.ppermute(down, "dp", pairs)
            up = lax.ppermute(after(up, right_1, left_1), "dp", pairs)
        downs.append(down)
        ups.append(up)

    right_2 = lax.ppermute(right_1, "tensor", right[1:])
    left_2 = lax.ppermute(left_1, "tensor", left[:-1])
    near = me + jnp.array([0, -1, 1], jnp.int32)
    base, = add_chunk((), [own, right_1, left_1], near, output_weight, None)
    base, right_2, left_2 = lax.optimization_barrier((base, right_2, left_2))
    right_3 = lax.ppermute(right_2, "tensor", right[2:])
    left_3 = lax.ppermute(left_2, "tensor", left[:-2])

    down = join_downs(after(tuple(downs), base))
    low, = add_chunk((), [own, right_1, left_1], near, None, down)
    far = me + jnp.array([-2, 2], jnp.int32)
    base, low = add_chunk((base, low), [right_2, left_2], far, output_weight, down)
    up = join_ups(after(tuple(ups), base))
    which = jnp.where(me == n_tensor - 1, 1, jnp.where(me == 0, -1, 0)).astype(jnp.int32)
    source = jnp.where(me == 0, n_tensor - 1, 0).astype(jnp.int32)
    slot = jnp.sum(jnp.where(one_hot, slots[None, :], 0), axis=1)[:, None]
    live = row_rank[:, None] - me * rank_part
    rest = (which[None], slot, live)
    pinned = pin(after(source[None], rest), width, output_weight, down, base, low, up)
    weight, down, base, low, up, right_3, left_3 = lax.optimization_barrier((*pinned, right_3, left_3))
    which, slot, live = rest
    low, x = finish_low(which, right_3, left_3, down, low, slot, live, rank_part)
    base = add_last(which, x, weight, base)
    lows = [low] + [
        lax.ppermute(low, "tensor", [(i, (i - j) % n_tensor) for i in range(n_tensor)])
        for j in range(1, n_tensor)
    ]
    return finish(me[None], slot, base, up, lows)


def gather_pages(block, n_dp):
    return [block] + [
        lax.ppermute(block, "dp", [(i, i ^ j) for i in range(n_dp)]) for j in range(1, n_dp)
    ]


def plain(x, output_weight, down_weight, up_weight, adapter_page_row, own_list, one_hot, row_rank):
    n_dp = lax.axis_size("dp")
    dp = lax.axis_index("dp")
    rows = x.shape[0]
    holder_length = down_weight.shape[0]
    rank, columns = up_weight.shape[1:]
    entries = one_hot.shape[1]
    pages = adapter_page_row[own_list]
    places = ((pages // holder_length) ^ dp) * holder_length + pages % holder_length

    def requested(block):
        blocks = jnp.concatenate(gather_pages(block, n_dp), axis=0)
        return jnp.concatenate(
            [lax.dynamic_slice_in_dim(blocks, places[e], 1, 0) for e in range(entries)], axis=0
        )

    down, up = requested(down_weight), requested(up_weight)
    x = lax.all_gather(x, "tensor", axis=1, tiled=True)
    base = jnp.dot(x, output_weight, preferred_element_type=F32)
    low = jnp.einsum("rd,ekd->rek", x, down, preferred_element_type=F32)
    low = jnp.sum(jnp.where(one_hot[:, :, None], low, 0.0), axis=1).astype(BF16)
    low = lax.all_gather(low, "tensor", axis=1, tiled=True)
    low = jnp.where(jnp.arange(rank)[None, :] < row_rank[:, None], low, jnp.zeros_like(low))
    spread = jnp.where(one_hot[:, :, None], low[:, None, :], jnp.zeros((), BF16))
    term = jnp.dot(
        spread.reshape(rows, entries * rank), up.reshape(entries * rank, columns), preferred_element_type=F32
    )
    return (base + term).astype(BF16)


def solution(mesh):
    in_specs = (
        P(("groups", "dp"), "tensor"),
        P(None, "tensor"),
        P("dp", "tensor", None),
        P("dp", None, "tensor"),
        P("groups"),
        P(("groups", "dp"), None),
        P(("groups", "dp")),
        P(),
    )
    out_specs = P(("groups", "dp"), "tensor")
    return jax.shard_map(local, mesh=mesh, in_specs=in_specs, out_specs=out_specs, check_vma=False)
```

```python
import functools

import jax
import jax.numpy as jnp
from jax import lax
from jax.experimental import pallas as pl
from jax.experimental.pallas import tpu as pltpu
from jax.sharding import PartitionSpec as P

CAP = 2
HALF = 1024
PARAMS = pltpu.CompilerParams(vmem_limit_bytes=48 * 2**20)
TAIL_PARAMS = pltpu.CompilerParams(vmem_limit_bytes=24 * 2**20)
F32 = jnp.float32
BF16 = jnp.bfloat16


def pick_kernel(places, down, up, first, rest):
    rank_part, width = down.shape[1], first.shape[2]
    step = pl.program_id(0)
    for c, out in enumerate((first, rest)):

        @pl.when(step == c)
        def _():
            for t in range(down.shape[2] // width):
                out[0, t * rank_part:(t + 1) * rank_part] = down[0, :, t * width:(t + 1) * width]
            rest[1 + c] = up[0]


def pick_pages(places, down, up):
    block = up.shape[1:]
    return pl.pallas_call(
        pick_kernel,
        out_shape=[jax.ShapeDtypeStruct((count,) + block, BF16) for count in (1, 3)],
        grid_spec=pltpu.PrefetchScalarGridSpec(
            num_scalar_prefetch=1,
            grid=(CAP,),
            in_specs=[pl.BlockSpec((1,) + a.shape[1:], lambda i, places: (places[i], 0, 0)) for a in (down, up)],
            out_specs=[pl.BlockSpec((count,) + block, lambda i, places: (0, 0, 0)) for count in (1, 3)],
        ),
        compiler_params=TAIL_PARAMS,
    )(places, down, up)


def join_downs_kernel(*refs):
    *pages, out = refs
    out[...] = jnp.concatenate([p[0] for p in pages], axis=0).T


def join_downs(pages, shards):
    _, rank, columns = pages[0].shape
    rank_part = rank // shards
    slots = rank_part * len(pages)
    return pl.pallas_call(
        join_downs_kernel,
        out_shape=jax.ShapeDtypeStruct((shards * columns, slots), BF16),
        grid=(shards,),
        in_specs=[pl.BlockSpec((1, rank_part, columns), lambda t: (0, t, 0))] * len(pages),
        out_specs=pl.BlockSpec((columns, slots), lambda t: (t, 0)),
        compiler_params=PARAMS,
    )(*pages)


def join_ups_kernel(*refs):
    *pages, out = refs
    for j, p in enumerate(pages):

        @pl.when(pl.program_id(0) == j)
        def _():
            out[...] = p[1:]


def join_ups(pages):
    _, rank, columns = pages[0].shape
    return pl.pallas_call(
        join_ups_kernel,
        out_shape=jax.ShapeDtypeStruct((CAP * len(pages), rank, columns), BF16),
        grid=(len(pages),),
        in_specs=[pl.BlockSpec(p.shape, lambda j: (0, 0, 0)) for p in pages],
        out_specs=pl.BlockSpec((CAP, rank, columns), lambda j: (j, 0, 0)),
        compiler_params=PARAMS,
    )(*pages).reshape(-1, columns)


RESIDENT = pl.BlockSpec(memory_space=pltpu.VMEM)
IN_HBM = pl.BlockSpec(memory_space=pltpu.HBM)


def chunk_kernel(count, halves, held, with_base, with_low, start, valid, *refs):
    refs = list(refs)
    xs = [refs.pop(0) for _ in range(count)]
    weight = refs.pop(0) if with_base else None
    down = refs.pop(0) if with_low else None
    outs = [refs.pop() for _ in range(with_base + with_low)][::-1]
    step = pl.program_id(0)

    @pl.when(step == 0)
    def _():
        for i, out in enumerate(outs):
            out[...] = refs[i][...] if held else jnp.zeros_like(out)

    for i, x in enumerate(xs):

        @pl.when((step >= i * halves) & (step < (i + 1) * halves) & (valid[step] != 0))
        def _():
            if with_base:
                base = outs[0]
                part = min(base.shape[1], 512)
                for n in range(0, base.shape[1], part):
                    base[:, n:n + part] += jnp.dot(x[...], weight[:, n:n + part], preferred_element_type=F32)
            if with_low:
                outs[-1][...] += jnp.dot(x[...], down[...], preferred_element_type=F32)


def add_chunk(totals, xs, source, weight, down):
    rows, width = xs[0].shape
    walked = [a for a in (weight, down) if a is not None]
    n_tensor = walked[0].shape[0] // width
    halves = width // HALF
    steps = len(xs) * halves
    valid = jnp.repeat(((source >= 0) & (source < n_tensor)).astype(jnp.int32), halves)
    start = jnp.clip(source, 0, n_tensor - 1)[:, None] * halves + jnp.arange(halves)[None, :]
    if len(xs) > 1:
        idle = jnp.concatenate([start[1:2, :1], start[:-1, -1:]], axis=0)
        start = jnp.where(((source >= 0) & (source < n_tensor))[:, None], start, idle)
    start = start.reshape(-1).astype(jnp.int32)
    whole = [pl.BlockSpec((rows, a.shape[1]), lambda s, *_: (0, 0)) for a in walked]
    columns = sum(a.shape[1] for a in walked)
    return pl.pallas_call(
        functools.partial(chunk_kernel, len(xs), halves, bool(totals), weight is not None, down is not None),
        out_shape=[jax.ShapeDtypeStruct((rows, a.shape[1]), F32) for a in walked],
        grid_spec=pltpu.PrefetchScalarGridSpec(
            num_scalar_prefetch=2,
            grid=(steps,),
            in_specs=[
                pl.BlockSpec((rows, HALF), lambda s, *_, i=i: (0, jnp.clip(s - i * halves, 0, halves - 1)))
                for i in range(len(xs))
            ]
            + [pl.BlockSpec((HALF, a.shape[1]), lambda s, start, valid: (start[s], 0)) for a in walked]
            + (whole if totals else []),
            out_specs=whole,
        ),
        compiler_params=PARAMS,
        cost_estimate=pl.CostEstimate(
            flops=2 * len(xs) * width * rows * columns,
            bytes_accessed=2 * len(xs) * width * (rows + columns) + 8 * rows * columns,
            transcendentals=0,
        ),
    )(start, valid, *xs, *walked, *totals)


def pin_kernel(source, weight, down, base, low, up, weight_out, down_out, base_out, low_out, up_out, sems):
    width, columns = weight_out.shape
    rows = pl.ds(pl.multiple_of(source[0] * width, width), width)
    pairs = [
        (weight.at[rows, pl.ds(0, columns)], weight_out),
        (down.at[rows], down_out),
        (base, base_out),
        (low, low_out),
        (up, up_out),
    ]
    copies = [pltpu.make_async_copy(a, b, sems.at[i]) for i, (a, b) in enumerate(pairs)]
    for copy in copies:
        copy.start()
    for copy in copies:
        copy.wait()


def pin(source, width, weight, down, base, low, up):
    shapes = [((width, weight.shape[1] // 2), BF16), ((width, down.shape[1]), BF16)]
    shapes += [(a.shape, a.dtype) for a in (base, low, up)]
    return pl.pallas_call(
        pin_kernel,
        out_shape=[pltpu.VMEM(*a) for a in shapes],
        in_specs=[pl.BlockSpec(memory_space=pltpu.SMEM)] + [IN_HBM] * 5,
        out_specs=[RESIDENT] * 5,
        scratch_shapes=[pltpu.SemaphoreType.DMA((5,))],
        compiler_params=TAIL_PARAMS,
        cost_estimate=pl.CostEstimate(
            flops=0, bytes_accessed=sum(a[0] * a[1] for a, _ in shapes) * 3, transcendentals=0
        ),
    )(source, weight, down, base, low, up)


def low_kernel(rank_part, which, from_left, from_right, down, total, slot, live, out, x, sem):
    @pl.when(which[0] > 0)
    def _():
        pltpu.make_async_copy(from_left, x, sem).start()

    @pl.when(which[0] < 0)
    def _():
        pltpu.make_async_copy(from_right, x, sem).start()

    @pl.when(which[0] != 0)
    def _():
        pltpu.make_async_copy(from_left, x, sem).wait()

    @pl.when(which[0] == 0)
    def _():
        x[...] = jnp.zeros_like(x)

    low = total[...] + jnp.dot(x[...], down[...], preferred_element_type=F32)
    lane = lax.broadcasted_iota(jnp.int32, low.shape, 1)
    own = jnp.where(lane // rank_part == slot[...], low, 0.0).astype(BF16)
    fold = (
        lax.rem(lax.broadcasted_iota(jnp.int32, (low.shape[1], rank_part), 0), rank_part)
        == lax.broadcasted_iota(jnp.int32, (low.shape[1], rank_part), 1)
    ).astype(BF16)
    mine = jnp.dot(own, fold, preferred_element_type=F32)
    k = lax.broadcasted_iota(jnp.int32, mine.shape, 1)
    out[...] = jnp.where(k < live[...], mine, 0.0).astype(BF16)


def finish_low(which, from_left, from_right, down, total, slot, live, rank_part):
    rows, width = from_left.shape
    slots = down.shape[1]
    return pl.pallas_call(
        functools.partial(low_kernel, rank_part),
        out_shape=[pltpu.VMEM((rows, rank_part), BF16), pltpu.VMEM((rows, width), BF16)],
        in_specs=[pl.BlockSpec(memory_space=pltpu.SMEM), IN_HBM, IN_HBM] + [RESIDENT] * 4,
        out_specs=[RESIDENT] * 2,
        scratch_shapes=[pltpu.SemaphoreType.DMA],
        compiler_params=TAIL_PARAMS,
        cost_estimate=pl.CostEstimate(
            flops=2 * width * rows * slots, bytes_accessed=2 * width * rows, transcendentals=0
        ),
    )(which, from_left, from_right, down, total, slot, live)


def base_kernel(which, source, x, near, weight, total, out, rest, sems):
    width, columns = near.shape
    parts, _, part = rest.shape
    rows = pl.ds(pl.multiple_of(source[0] * width, width), width)

    @pl.when(which[0] != 0)
    def _():
        copies = [
            pltpu.make_async_copy(weight.at[rows, pl.ds(columns + n * part, part)], rest.at[n], sems.at[n])
            for n in range(parts)
        ]
        for copy in copies:
            copy.start()
        for n in range(2 * parts):
            cut = slice(n * part, (n + 1) * part)
            if n < parts:
                rows_of = near[:, cut]
            else:
                copies[n - parts].wait()
                rows_of = rest[n - parts]
            out[:, cut] = total[:, cut] + jnp.dot(x[...], rows_of, preferred_element_type=F32)


def add_last(which, source, x, near, weight, total):
    rows, width = x.shape
    columns = weight.shape[1]
    part = columns // 4
    return pl.pallas_call(
        base_kernel,
        out_shape=pltpu.VMEM((rows, columns), F32),
        in_specs=[pl.BlockSpec(memory_space=pltpu.SMEM)] * 2 + [RESIDENT, RESIDENT, IN_HBM, RESIDENT],
        out_specs=RESIDENT,
        scratch_shapes=[pltpu.VMEM((2, width, part), BF16), pltpu.SemaphoreType.DMA((2,))],
        input_output_aliases={5: 0},
        compiler_params=TAIL_PARAMS,
        cost_estimate=pl.CostEstimate(
            flops=2 * width * rows * columns, bytes_accessed=width * columns, transcendentals=0
        ),
    )(which, source, x, near, weight, total)


def finish_kernel(parts, me, slot, total, up, *refs):
    lows, (out, spread) = refs[:parts], refs[parts:]
    rank_part = lows[0].shape[1]
    rank = parts * rank_part
    part = out.shape[1]

    @pl.when(pl.program_id(0) == 0)
    def _():
        low = jnp.concatenate([part[...].astype(F32) for part in lows], axis=1)
        low = pltpu.roll(low, me[0] * rank_part, 1)
        for e in range(spread.shape[1] // rank):
            spread[:, e * rank:(e + 1) * rank] = jnp.where(slot[...] == e, low, 0.0).astype(BF16)

    cut = pl.ds(pl.multiple_of(pl.program_id(0) * part, part), part)
    out[...] = (total[:, cut] + jnp.dot(spread[...], up[:, cut], preferred_element_type=F32)).astype(BF16)


def finish(me, slot, total, up, lows):
    rows, columns = total.shape
    depth = up.shape[0]
    part = min(columns, 512)
    return pl.pallas_call(
        functools.partial(finish_kernel, len(lows)),
        grid=(columns // part,),
        out_shape=jax.ShapeDtypeStruct((rows, columns), BF16),
        in_specs=[pl.BlockSpec(memory_space=pltpu.SMEM)] + [RESIDENT] * (3 + len(lows)),
        out_specs=pl.BlockSpec((rows, part), lambda n: (0, n)),
        scratch_shapes=[pltpu.VMEM((rows, depth), BF16)],
        compiler_params=TAIL_PARAMS,
        cost_estimate=pl.CostEstimate(
            flops=2 * rows * depth * columns,
            bytes_accessed=2 * rows * columns,
            transcendentals=0,
        ),
    )(me, slot, total, up, *lows)


def after(value, *earlier):
    return lax.optimization_barrier((value,) + earlier)[0]


def asked_pages(requests, adapter_page_row, holder_length):
    n_dp = lax.axis_size("dp")
    dp = lax.axis_index("dp")
    count = adapter_page_row.shape[0]

    def pages_of(wanted):
        hit = wanted[:, None] == jnp.arange(count)[None, :]
        return jnp.sum(jnp.where(hit, adapter_page_row[None, :], 0), axis=1)

    def order_in(holders):
        same = holders[:, None] == holders[None, :]
        n = holders.shape[0]
        earlier = jnp.arange(n)[:, None] > jnp.arange(n)[None, :]
        return jnp.sum((same & earlier).astype(jnp.int32), axis=1)

    own = pages_of(requests[0])
    holders = own // holder_length
    slots = (holders ^ dp) * CAP + order_in(holders)
    places = []
    for j in range(n_dp):
        wanted = requests if j == 0 else lax.ppermute(requests, "dp", [(i, i ^ j) for i in range(n_dp)])
        pages = pages_of(wanted[0])
        holder = pages // holder_length
        order = jnp.where(holder == dp, order_in(holder), -1)
        hit = order[None, :] == jnp.arange(CAP)[:, None]
        places.append(jnp.sum(jnp.where(hit, (pages % holder_length)[None, :], 0), axis=1))
    return slots, places


def local(
    attention_result,
    output_weight,
    adapter_down_weight,
    adapter_up_weight,
    adapter_page_row,
    requests,
    row_request_entry,
    ranks,
):
    n_dp = lax.axis_size("dp")
    n_tensor = lax.axis_size("tensor")
    me = lax.axis_index("tensor")
    rows, width = attention_result.shape
    holder_length, rank_part, _ = adapter_down_weight.shape
    rank, columns = adapter_up_weight.shape[1:]
    own_list = requests[0]
    entries = own_list.shape[0]
    one_hot = row_request_entry[:, None] == jnp.arange(entries)[None, :]
    row_rank = jnp.sum(jnp.where(one_hot, ranks[own_list][None, :], 0), axis=1)
    if n_tensor != 4 or width % HALF or rank_part % 16 or width != columns:
        return plain(
            attention_result, output_weight, adapter_down_weight, adapter_up_weight, adapter_page_row,
            own_list, one_hot, row_rank,
        )

    right = [(i, i + 1) for i in range(n_tensor - 1)]
    left = [(i + 1, i) for i in range(n_tensor - 1)]
    own = attention_result
    right_1 = lax.ppermute(own, "tensor", right)
    left_1 = lax.ppermute(own, "tensor", left)

    slots, places = asked_pages(requests, adapter_page_row, holder_length)
    firsts, rests = zip(*[pick_pages(places[j], adapter_down_weight, adapter_up_weight) for j in range(n_dp)])

    def send(pages):
        return (pages[0],) + tuple(
            lax.ppermute(pages[j], "dp", [(i, i ^ j) for i in range(n_dp)]) for j in range(1, n_dp)
        )

    firsts = send(firsts)
    right_1, left_1 = lax.optimization_barrier((right_1, left_1, *firsts))[:2]
    rests = send(rests)
    right_2 = lax.ppermute(right_1, "tensor", right[1:])
    left_2 = lax.ppermute(left_1, "tensor", left[:-1])
    near = me + jnp.array([0, -1, 1], jnp.int32)
    far = me + jnp.array([-2, 2], jnp.int32)
    base, = add_chunk((), [own, right_1, left_1], near, output_weight, None)
    base, right_2, left_2 = lax.optimization_barrier((base, right_2, left_2))
    right_3 = lax.ppermute(right_2, "tensor", right[2:])
    left_3 = lax.ppermute(left_2, "tensor", left[:-2])

    base, = add_chunk((base,), [right_2, left_2], far, output_weight, None)
    rests = after(rests, base)
    down = join_downs([p for pair in zip(firsts, rests) for p in pair], n_tensor)
    up = join_ups(rests)
    blocks = [own, right_1, left_1, right_2, left_2]
    low, = add_chunk((), blocks, jnp.concatenate([near, far]), None, down)

    which = jnp.where(me == n_tensor - 1, 1, jnp.where(me == 0, -1, 0)).astype(jnp.int32)
    source = jnp.where(me == 0, n_tensor - 1, 0).astype(jnp.int32)
    slot = jnp.sum(jnp.where(one_hot, slots[None, :], 0), axis=1)[:, None]
    live = row_rank[:, None] - me * rank_part
    source, which, slot, live = lax.optimization_barrier((source[None], which[None], slot, live, low))[:4]
    pinned = pin(source, width, output_weight, down, base, low, up)
    part, down, base, low, up, right_3, left_3 = lax.optimization_barrier((*pinned, right_3, left_3))
    low, x = finish_low(which, right_3, left_3, down, low, slot, live, rank_part)
    base = add_last(which, source, x, part, output_weight, base)
    lows = [low] + [
        lax.ppermute(low, "tensor", [(i, (i - j) % n_tensor) for i in range(n_tensor)])
        for j in range(1, n_tensor)
    ]
    return finish(me[None], slot, base, up, lows)


def gather_pages(block, n_dp):
    return [block] + [
        lax.ppermute(block, "dp", [(i, i ^ j) for i in range(n_dp)]) for j in range(1, n_dp)
    ]


def plain(x, output_weight, down_weight, up_weight, adapter_page_row, own_list, one_hot, row_rank):
    n_dp = lax.axis_size("dp")
    dp = lax.axis_index("dp")
    rows = x.shape[0]
    holder_length = down_weight.shape[0]
    rank, columns = up_weight.shape[1:]
    entries = one_hot.shape[1]
    pages = adapter_page_row[own_list]
    places = ((pages // holder_length) ^ dp) * holder_length + pages % holder_length

    def requested(block):
        blocks = jnp.concatenate(gather_pages(block, n_dp), axis=0)
        return jnp.concatenate(
            [lax.dynamic_slice_in_dim(blocks, places[e], 1, 0) for e in range(entries)], axis=0
        )

    down, up = requested(down_weight), requested(up_weight)
    x = lax.all_gather(x, "tensor", axis=1, tiled=True)
    base = jnp.dot(x, output_weight, preferred_element_type=F32)
    low = jnp.einsum("rd,ekd->rek", x, down, preferred_element_type=F32)
    low = jnp.sum(jnp.where(one_hot[:, :, None], low, 0.0), axis=1).astype(BF16)
    low = lax.all_gather(low, "tensor", axis=1, tiled=True)
    low = jnp.where(jnp.arange(rank)[None, :] < row_rank[:, None], low, jnp.zeros_like(low))
    spread = jnp.where(one_hot[:, :, None], low[:, None, :], jnp.zeros((), BF16))
    term = jnp.dot(
        spread.reshape(rows, entries * rank), up.reshape(entries * rank, columns), preferred_element_type=F32
    )
    return (base + term).astype(BF16)


def solution(mesh):
    in_specs = (
        P(("groups", "dp"), "tensor"),
        P(None, "tensor"),
        P("dp", "tensor", None),
        P("dp", None, "tensor"),
        P("groups"),
        P(("groups", "dp"), None),
        P(("groups", "dp")),
        P(),
    )
    out_specs = P(("groups", "dp"), "tensor")
    return jax.shard_map(local, mesh=mesh, in_specs=in_specs, out_specs=out_specs, check_vma=False)
```

```python
import functools

import jax
import jax.numpy as jnp
from jax import lax
from jax.experimental import pallas as pl
from jax.experimental.pallas import tpu as pltpu
from jax.sharding import PartitionSpec as P

PARAMS = pltpu.CompilerParams(vmem_limit_bytes=48 * 2**20)
TAIL_PARAMS = pltpu.CompilerParams(vmem_limit_bytes=24 * 2**20)
F32 = jnp.float32
BF16 = jnp.bfloat16


def start_pages(places, blocks, length, targets, sems, rows_of):
    for e, target in enumerate(targets):
        for j, block in enumerate(blocks):

            @pl.when(places[e] // length == j)
            def _():
                pltpu.make_async_copy(rows_of(block.at[lax.rem(places[e], length)]), target, sems[e]).start()


def join_downs_kernel(places, *refs):
    *blocks, out, held, sems = refs
    length, rank_part, _ = blocks[0].shape
    shards, slots, width = held.shape
    step = pl.program_id(0)

    def targets(t):
        return [held.at[t, pl.ds(e * rank_part, rank_part)] for e in range(slots // rank_part)]

    @pl.when(step == 0)
    def _():
        for t in range(shards):
            semaphores = [sems.at[t, e] for e in range(slots // rank_part)]
            start_pages(
                places, blocks, length, targets(t), semaphores, lambda page: page.at[:, pl.ds(t * width, width)]
            )

    for t in range(shards):

        @pl.when(step == t)
        def _():
            for e, target in enumerate(targets(t)):
                source = blocks[0].at[0, :, pl.ds(t * width, width)]
                pltpu.make_async_copy(source, target, sems.at[t, e]).wait()
            out[...] = held[t].T


def join_downs(places, blocks, shards):
    entries = places.shape[0]
    _, rank_part, features = blocks[0].shape
    width, slots = features // shards, entries * rank_part
    return pl.pallas_call(
        join_downs_kernel,
        out_shape=jax.ShapeDtypeStruct((features, slots), BF16),
        grid=(shards,),
        in_specs=[pl.BlockSpec(memory_space=pltpu.SMEM)] + [pl.BlockSpec(memory_space=pltpu.HBM)] * len(blocks),
        out_specs=pl.BlockSpec((width, slots), lambda t: (t, 0)),
        scratch_shapes=[pltpu.VMEM((shards, slots, width), BF16), pltpu.SemaphoreType.DMA((shards, entries))],
        compiler_params=TAIL_PARAMS,
        cost_estimate=pl.CostEstimate(flops=0, bytes_accessed=4 * features * slots, transcendentals=0),
    )(places, *blocks)


RESIDENT = pl.BlockSpec(memory_space=pltpu.VMEM)
IN_HBM = pl.BlockSpec(memory_space=pltpu.HBM)


def chunk_kernel(held, with_base, with_low, start, valid, *refs):
    refs = list(refs)
    xs = [refs.pop(0) for _ in range(valid.shape[0])]
    weight = refs.pop(0) if with_base else None
    down = refs.pop(0) if with_low else None
    outs = [refs.pop() for _ in range(with_base + with_low)][::-1]
    step = pl.program_id(0)

    @pl.when(step == 0)
    def _():
        for i, out in enumerate(outs):
            out[...] = refs[i][...] if held else jnp.zeros_like(out)

    for i, x in enumerate(xs):

        @pl.when((step == i) & (valid[step] != 0))
        def _():
            if with_base:
                base = outs[0]
                part = min(base.shape[1], 512)
                for n in range(0, base.shape[1], part):
                    base[:, n:n + part] += jnp.dot(x[...], weight[:, n:n + part], preferred_element_type=F32)
            if with_low:
                outs[-1][...] += jnp.dot(x[...], down[...], preferred_element_type=F32)


def add_chunk(totals, xs, source, half, weight, down):
    rows, width = xs[0].shape
    walked = [a for a in (weight, down) if a is not None]
    n_tensor = walked[0].shape[0] // (2 * width)
    steps = len(xs)
    there = (source >= 0) & (source < n_tensor)
    start = 2 * jnp.clip(source, 0, n_tensor - 1) + jnp.array(half, jnp.int32)
    start = jnp.where(there, start, jnp.concatenate([start[1:2], start[:-1]])).astype(jnp.int32)
    valid = there.astype(jnp.int32)
    whole = [pl.BlockSpec((rows, a.shape[1]), lambda s, *_: (0, 0)) for a in walked]
    columns = sum(a.shape[1] for a in walked)
    return pl.pallas_call(
        functools.partial(chunk_kernel, bool(totals), weight is not None, down is not None),
        out_shape=[jax.ShapeDtypeStruct((rows, a.shape[1]), F32) for a in walked],
        grid_spec=pltpu.PrefetchScalarGridSpec(
            num_scalar_prefetch=2,
            grid=(steps,),
            in_specs=[pl.BlockSpec((rows, width), lambda s, *_: (0, 0))] * steps
            + [pl.BlockSpec((width, a.shape[1]), lambda s, start, valid: (start[s], 0)) for a in walked]
            + (whole if totals else []),
            out_specs=whole,
        ),
        compiler_params=PARAMS,
        cost_estimate=pl.CostEstimate(
            flops=2 * steps * width * rows * columns,
            bytes_accessed=2 * steps * width * (rows + columns) + 8 * rows * columns,
            transcendentals=0,
        ),
    )(start, valid, *xs, *walked, *totals)


def pin_kernel(start, places, weight, down, base, low, *refs):
    *blocks, weight_out, down_out, base_out, low_out, up_out, sems = refs
    width = weight_out.shape[0]
    length, rank, _ = blocks[0].shape
    rows = pl.ds(pl.multiple_of(start[0] * width, width), width)
    pairs = [(weight.at[rows], weight_out), (down.at[rows], down_out), (base, base_out), (low, low_out)]
    copies = [pltpu.make_async_copy(a, b, sems.at[i]) for i, (a, b) in enumerate(pairs)]
    pages = [up_out.at[pl.ds(e * rank, rank)] for e in range(up_out.shape[0] // rank)]
    for copy in copies:
        copy.start()
    page_sems = [sems.at[len(copies) + e] for e in range(len(pages))]
    start_pages(places, blocks, length, pages, page_sems, lambda page: page)
    for copy in copies:
        copy.wait()
    for page, sem in zip(pages, page_sems):
        pltpu.make_async_copy(blocks[0].at[0], page, sem).wait()


def pin(start, places, width, weight, down, base, low, blocks):
    entries = places.shape[0]
    rank, columns = blocks[0].shape[1:]
    shapes = [((width, a.shape[1]), BF16) for a in (weight, down)] + [(a.shape, a.dtype) for a in (base, low)]
    shapes += [((entries * rank, columns), BF16)]
    return pl.pallas_call(
        pin_kernel,
        out_shape=[pltpu.VMEM(*a) for a in shapes],
        in_specs=[pl.BlockSpec(memory_space=pltpu.SMEM)] * 2 + [IN_HBM] * (4 + len(blocks)),
        out_specs=[RESIDENT] * 5,
        scratch_shapes=[pltpu.SemaphoreType.DMA((4 + entries,))],
        compiler_params=TAIL_PARAMS,
        cost_estimate=pl.CostEstimate(
            flops=0, bytes_accessed=sum(a[0] * a[1] for a, _ in shapes) * 3, transcendentals=0
        ),
    )(start, places, weight, down, base, low, *blocks)


def low_kernel(rank_part, which, from_left, from_right, down, total, slot, live, out, x, sem):
    @pl.when(which[0] > 0)
    def _():
        pltpu.make_async_copy(from_left, x, sem).start()

    @pl.when(which[0] < 0)
    def _():
        pltpu.make_async_copy(from_right, x, sem).start()

    @pl.when(which[0] != 0)
    def _():
        pltpu.make_async_copy(from_left, x, sem).wait()

    @pl.when(which[0] == 0)
    def _():
        x[...] = jnp.zeros_like(x)

    low = total[...] + jnp.dot(x[...], down[...], preferred_element_type=F32)
    lane = lax.broadcasted_iota(jnp.int32, low.shape, 1)
    own = jnp.where(lane // rank_part == slot[...], low, 0.0).astype(BF16)
    fold = (
        lax.rem(lax.broadcasted_iota(jnp.int32, (low.shape[1], rank_part), 0), rank_part)
        == lax.broadcasted_iota(jnp.int32, (low.shape[1], rank_part), 1)
    ).astype(BF16)
    mine = jnp.dot(own, fold, preferred_element_type=F32)
    k = lax.broadcasted_iota(jnp.int32, mine.shape, 1)
    out[...] = jnp.where(k < live[...], mine, 0.0).astype(BF16)


def finish_low(which, from_left, from_right, down, total, slot, live, rank_part):
    rows, width = from_left.shape
    slots = down.shape[1]
    return pl.pallas_call(
        functools.partial(low_kernel, rank_part),
        out_shape=[pltpu.VMEM((rows, rank_part), BF16), pltpu.VMEM((rows, width), BF16)],
        in_specs=[pl.BlockSpec(memory_space=pltpu.SMEM), IN_HBM, IN_HBM] + [RESIDENT] * 4,
        out_specs=[RESIDENT] * 2,
        scratch_shapes=[pltpu.SemaphoreType.DMA],
        compiler_params=TAIL_PARAMS,
        cost_estimate=pl.CostEstimate(
            flops=2 * width * rows * slots, bytes_accessed=2 * width * rows, transcendentals=0
        ),
    )(which, from_left, from_right, down, total, slot, live)


def base_kernel(which, x, weight, total, out):
    @pl.when(which[0] != 0)
    def _():
        part = min(out.shape[1], 512)
        for n in range(0, out.shape[1], part):
            cut = slice(n, n + part)
            out[:, cut] = total[:, cut] + jnp.dot(x[...], weight[:, cut], preferred_element_type=F32)


def add_last(which, x, weight, total):
    rows, width = x.shape
    columns = weight.shape[1]
    return pl.pallas_call(
        base_kernel,
        out_shape=pltpu.VMEM((rows, columns), F32),
        in_specs=[pl.BlockSpec(memory_space=pltpu.SMEM)] + [RESIDENT] * 3,
        out_specs=RESIDENT,
        input_output_aliases={3: 0},
        compiler_params=TAIL_PARAMS,
        cost_estimate=pl.CostEstimate(flops=2 * width * rows * columns, bytes_accessed=0, transcendentals=0),
    )(which, x, weight, total)


def finish_kernel(parts, me, slot, total, up, *refs):
    lows, (out, spread) = refs[:parts], refs[parts:]
    rank_part = lows[0].shape[1]
    rank = parts * rank_part
    part = out.shape[1]

    @pl.when(pl.program_id(0) == 0)
    def _():
        low = jnp.concatenate([part[...].astype(F32) for part in lows], axis=1)
        low = pltpu.roll(low, me[0] * rank_part, 1)
        for e in range(spread.shape[1] // rank):
            spread[:, e * rank:(e + 1) * rank] = jnp.where(slot[...] == e, low, 0.0).astype(BF16)

    cut = pl.ds(pl.multiple_of(pl.program_id(0) * part, part), part)
    out[...] = (total[:, cut] + jnp.dot(spread[...], up[:, cut], preferred_element_type=F32)).astype(BF16)


def finish(me, slot, total, up, lows):
    rows, columns = total.shape
    depth = up.shape[0]
    part = min(columns, 512)
    return pl.pallas_call(
        functools.partial(finish_kernel, len(lows)),
        grid=(columns // part,),
        out_shape=jax.ShapeDtypeStruct((rows, columns), BF16),
        in_specs=[pl.BlockSpec(memory_space=pltpu.SMEM)] + [RESIDENT] * (3 + len(lows)),
        out_specs=pl.BlockSpec((rows, part), lambda n: (0, n)),
        scratch_shapes=[pltpu.VMEM((rows, depth), BF16)],
        compiler_params=TAIL_PARAMS,
        cost_estimate=pl.CostEstimate(
            flops=2 * rows * depth * columns,
            bytes_accessed=2 * rows * columns,
            transcendentals=0,
        ),
    )(me, slot, total, up, *lows)


def after(value, *earlier):
    return lax.optimization_barrier((value,) + earlier)[0]


def looked_up(table, ids):
    hit = ids[:, None] == jnp.arange(table.shape[0])[None, :]
    return jnp.sum(jnp.where(hit, table[None, :], 0), axis=1)


def local(
    attention_result,
    output_weight,
    adapter_down_weight,
    adapter_up_weight,
    adapter_page_row,
    requests,
    row_request_entry,
    ranks,
):
    n_dp = lax.axis_size("dp")
    n_tensor = lax.axis_size("tensor")
    me = lax.axis_index("tensor")
    rows, width = attention_result.shape
    holder_length, rank_part, _ = adapter_down_weight.shape
    rank, columns = adapter_up_weight.shape[1:]
    own_list = requests[0]
    entries = own_list.shape[0]
    one_hot = row_request_entry[:, None] == jnp.arange(entries)[None, :]
    row_rank = jnp.sum(jnp.where(one_hot, looked_up(ranks, own_list)[None, :], 0), axis=1)
    pages = looked_up(adapter_page_row, own_list)
    apart = (pages // holder_length) ^ lax.axis_index("dp")
    places = apart * holder_length + pages % holder_length
    if n_tensor != 4 or n_dp != 4 or width % 256 or rank_part % 16 or entries * rank_part > 256:
        return plain(
            attention_result, output_weight, adapter_down_weight, adapter_up_weight, places, one_hot, row_rank
        )

    places = (apart % 2 * 2 + apart // 2) * holder_length + pages % holder_length

    def across(x, distance):
        return lax.ppermute(x, "dp", [(i, i ^ distance) for i in range(n_dp)])

    right = [(i, i + 1) for i in range(n_tensor - 1)]
    left = [(i + 1, i) for i in range(n_tensor - 1)]

    def onward(from_left, from_right, step):
        return (
            lax.ppermute(from_left, "tensor", right[step:]),
            lax.ppermute(from_right, "tensor", left[:len(left) - step]),
        )

    first = attention_result[:, :width // 2]
    second = after(attention_result, first)[:, width // 2:]
    first_1 = onward(first, first, 0)
    second_1 = onward(second, second, 0)
    far_down = across(adapter_down_weight, 2)
    far_up = across(after(adapter_up_weight, far_down), 2)

    first_2 = onward(*first_1, 1)
    second_1 = lax.optimization_barrier((*first_1, *second_1))[2:]
    second_2 = onward(*second_1, 1)
    downs = jnp.concatenate([adapter_down_weight, after(far_down, *second_1)], axis=0)
    downs = (downs, across(downs, 1))
    near = me + jnp.array([0, 0, -1, 1, -1, 1], jnp.int32)
    far = me + jnp.array([-2, 2, -2, 2], jnp.int32)
    last = me + jnp.array([-3, 3], jnp.int32)
    near_xs = [first, second, *first_1, *second_1]
    far_xs = [*first_2, *second_2]
    near_half, far_half = (0, 1, 0, 0, 1, 1), (0, 0, 1, 1)
    base, = add_chunk((), near_xs, near, near_half, output_weight, None)
    first_2 = lax.optimization_barrier((base, *first_2))[1:]
    first_3 = onward(*first_2, 2)
    second_2 = lax.optimization_barrier((*first_2, *second_2))[2:]
    second_3 = onward(*second_2, 2)
    ups = jnp.concatenate([adapter_up_weight, after(far_up, *second_2)], axis=0)
    ups = (ups, across(ups, 1))

    base, = add_chunk((base,), far_xs, far, far_half, output_weight, None)
    down = join_downs(places, after(downs, base), n_tensor)
    low, = add_chunk((), near_xs + far_xs, jnp.concatenate([near, far]), near_half + far_half, None, down)
    base, low = add_chunk((base, low), list(first_3), last, (0, 0), output_weight, down)

    which = jnp.where(me == n_tensor - 1, 1, jnp.where(me == 0, -1, 0)).astype(jnp.int32)[None]
    start = jnp.where(me == 0, 2 * n_tensor - 1, 1).astype(jnp.int32)[None]
    slot = row_request_entry[:, None]
    live = row_rank[:, None] - me * rank_part
    start, which, slot, live = lax.optimization_barrier((start, which, slot, live, low))[:4]
    pinned = pin(start, places, width // 2, output_weight, down, base, low, ups)
    weight, down, base, low, up, *second_3 = lax.optimization_barrier((*pinned, *second_3))
    low, x = finish_low(which, *second_3, down, low, slot, live, rank_part)
    base = add_last(which, x, weight, base)
    lows = [low] + [
        lax.ppermute(low, "tensor", [(i, (i - j) % n_tensor) for i in range(n_tensor)])
        for j in range(1, n_tensor)
    ]
    return finish(me[None], slot, base, up, lows)


def gather_pages(block, n_dp):
    return [block] + [
        lax.ppermute(block, "dp", [(i, i ^ j) for i in range(n_dp)]) for j in range(1, n_dp)
    ]


def plain(x, output_weight, down_weight, up_weight, places, one_hot, row_rank):
    n_dp = lax.axis_size("dp")
    rows = x.shape[0]
    rank, columns = up_weight.shape[1:]
    entries = one_hot.shape[1]

    def requested(block):
        blocks = jnp.concatenate(gather_pages(block, n_dp), axis=0)
        return jnp.concatenate(
            [lax.dynamic_slice_in_dim(blocks, places[e], 1, 0) for e in range(entries)], axis=0
        )

    down, up = requested(down_weight), requested(up_weight)
    x = lax.all_gather(x, "tensor", axis=1, tiled=True)
    base = jnp.dot(x, output_weight, preferred_element_type=F32)
    low = jnp.einsum("rd,ekd->rek", x, down, preferred_element_type=F32)
    low = jnp.sum(jnp.where(one_hot[:, :, None], low, 0.0), axis=1).astype(BF16)
    low = lax.all_gather(low, "tensor", axis=1, tiled=True)
    low = jnp.where(jnp.arange(rank)[None, :] < row_rank[:, None], low, jnp.zeros_like(low))
    spread = jnp.where(one_hot[:, :, None], low[:, None, :], jnp.zeros((), BF16))
    term = jnp.dot(
        spread.reshape(rows, entries * rank), up.reshape(entries * rank, columns), preferred_element_type=F32
    )
    return (base + term).astype(BF16)


def solution(mesh):
    in_specs = (
        P(("groups", "dp"), "tensor"),
        P(None, "tensor"),
        P("dp", "tensor", None),
        P("dp", None, "tensor"),
        P("groups"),
        P(("groups", "dp"), None),
        P(("groups", "dp")),
        P(),
    )
    out_specs = P(("groups", "dp"), "tensor")
    return jax.shard_map(local, mesh=mesh, in_specs=in_specs, out_specs=out_specs, check_vma=False)
```

```python
import functools

import jax
import jax.numpy as jnp
from jax import lax
from jax.experimental import pallas as pl
from jax.experimental.pallas import tpu as pltpu
from jax.sharding import PartitionSpec as P

PARAMS = pltpu.CompilerParams(vmem_limit_bytes=48 * 2**20)
TAIL_PARAMS = pltpu.CompilerParams(vmem_limit_bytes=24 * 2**20)
F32 = jnp.float32
BF16 = jnp.bfloat16


def start_pages(places, blocks, length, targets, sems, rows_of):
    for e, target in enumerate(targets):
        for j, block in enumerate(blocks):

            @pl.when(places[e] // length == j)
            def _():
                pltpu.make_async_copy(rows_of(block.at[lax.rem(places[e], length)]), target, sems[e]).start()


def join_downs_kernel(places, *refs):
    *blocks, out, held, sems = refs
    length, rank_part, _ = blocks[0].shape
    shards, slots, width = held.shape
    step = pl.program_id(0)

    def targets(t):
        return [held.at[t, pl.ds(e * rank_part, rank_part)] for e in range(slots // rank_part)]

    @pl.when(step == 0)
    def _():
        for t in range(shards):
            semaphores = [sems.at[t, e] for e in range(slots // rank_part)]
            start_pages(
                places, blocks, length, targets(t), semaphores, lambda page: page.at[:, pl.ds(t * width, width)]
            )

    for t in range(shards):

        @pl.when(step == t)
        def _():
            for e, target in enumerate(targets(t)):
                source = blocks[0].at[0, :, pl.ds(t * width, width)]
                pltpu.make_async_copy(source, target, sems.at[t, e]).wait()
            out[...] = held[t].T


def join_downs(places, blocks, shards):
    entries = places.shape[0]
    _, rank_part, features = blocks[0].shape
    width, slots = features // shards, entries * rank_part
    return pl.pallas_call(
        join_downs_kernel,
        out_shape=jax.ShapeDtypeStruct((features, slots), BF16),
        grid=(shards,),
        in_specs=[pl.BlockSpec(memory_space=pltpu.SMEM)] + [pl.BlockSpec(memory_space=pltpu.HBM)] * len(blocks),
        out_specs=pl.BlockSpec((width, slots), lambda t: (t, 0)),
        scratch_shapes=[pltpu.VMEM((shards, slots, width), BF16), pltpu.SemaphoreType.DMA((shards, entries))],
        compiler_params=TAIL_PARAMS,
        cost_estimate=pl.CostEstimate(flops=0, bytes_accessed=4 * features * slots, transcendentals=0),
    )(places, *blocks)


RESIDENT = pl.BlockSpec(memory_space=pltpu.VMEM)
IN_HBM = pl.BlockSpec(memory_space=pltpu.HBM)


def near_kernel(start, valid, *refs):
    *xs, weight, down, base, low = refs
    step = pl.program_id(0)

    @pl.when(step == 0)
    def _():
        base[...] = jnp.zeros_like(base)
        low[...] = jnp.zeros_like(low)

    for i, x in enumerate(xs):

        @pl.when((step // 2 == i) & (valid[i] != 0))
        def _():
            part = min(base.shape[1], 512)
            for n in range(0, base.shape[1], part):
                base[:, n:n + part] += jnp.dot(x[...], weight[:, n:n + part], preferred_element_type=F32)
            low[...] += jnp.dot(x[...], down[...], preferred_element_type=F32)


def near_products(xs, source, weight, down):
    rows, width = xs[0].shape
    half = width // 2
    n_tensor = weight.shape[0] // width
    there = (source >= 0) & (source < n_tensor)
    start = 2 * jnp.clip(source, 0, n_tensor - 1)[:, None] + jnp.arange(2)[None, :]
    before = jnp.broadcast_to(jnp.roll(start[:, 1:], 1, axis=0), start.shape)
    start = jnp.where(there[:, None], start, before).reshape(-1).astype(jnp.int32)
    columns, slots = weight.shape[1], down.shape[1]
    whole = [pl.BlockSpec((rows, a), lambda s, *_: (0, 0)) for a in (columns, slots)]
    steps = 2 * len(xs)
    return pl.pallas_call(
        near_kernel,
        out_shape=[jax.ShapeDtypeStruct((rows, a), F32) for a in (columns, slots)],
        grid_spec=pltpu.PrefetchScalarGridSpec(
            num_scalar_prefetch=2,
            grid=(steps,),
            in_specs=[
                pl.BlockSpec((rows, half), lambda s, *_, i=i: (0, jnp.clip(s - 2 * i, 0, 1)))
                for i in range(len(xs))
            ]
            + [pl.BlockSpec((half, a), lambda s, start, valid: (start[s], 0)) for a in (columns, slots)],
            out_specs=whole,
        ),
        compiler_params=PARAMS,
        cost_estimate=pl.CostEstimate(
            flops=2 * steps * half * rows * (columns + slots),
            bytes_accessed=2 * steps * half * (rows + columns + slots) + 4 * rows * (columns + slots),
            transcendentals=0,
        ),
    )(start, there.astype(jnp.int32), *xs, weight, down)


def fold_entry(low, slot, rank_part):
    lane = lax.broadcasted_iota(jnp.int32, low.shape, 1)
    own = jnp.where(lane // rank_part == slot, low, 0.0)
    shape = (low.shape[1], rank_part)
    fold = lax.rem(lax.broadcasted_iota(jnp.int32, shape, 0), rank_part) == lax.broadcasted_iota(jnp.int32, shape, 1)
    return jnp.dot(own, fold.astype(F32), precision=lax.Precision.HIGHEST, preferred_element_type=F32)


def far_kernel(start, first, second, weight, down, other_down, slot, base_in, low_in, base, low, other, acc, other_acc):
    step = pl.program_id(0)
    rank_part = low.shape[1]

    @pl.when(step == 0)
    def _():
        base[...] = base_in[...]
        acc[...] = low_in[...]
        other_acc[...] = jnp.zeros_like(other_acc)

    for i, x in enumerate((first, second)):

        @pl.when(step == i)
        def _():
            part = min(base.shape[1], 512)
            for n in range(0, base.shape[1], part):
                base[:, n:n + part] += jnp.dot(x[...], weight[:, n:n + part], preferred_element_type=F32)
            acc[...] += jnp.dot(x[...], down[...], preferred_element_type=F32)
            other_acc[...] += jnp.dot(x[...], other_down[...], preferred_element_type=F32)

    @pl.when(step == 1)
    def _():
        low[...] = fold_entry(acc[...], slot[...], rank_part)
        other[...] = fold_entry(other_acc[...], slot[...], rank_part)


def add_far(base, low, first, second, source, weight, down, other_down, slot, rank_part):
    rows, width = first.shape
    columns, slots = weight.shape[1], down.shape[1]
    start = (2 * source + jnp.arange(2)).astype(jnp.int32)

    def whole(a):
        return pl.BlockSpec((rows, a), lambda s, start: (0, 0))

    return pl.pallas_call(
        far_kernel,
        out_shape=[jax.ShapeDtypeStruct((rows, a), F32) for a in (columns, rank_part, rank_part)],
        grid_spec=pltpu.PrefetchScalarGridSpec(
            num_scalar_prefetch=1,
            grid=(2,),
            in_specs=[
                whole(width),
                whole(width),
                pl.BlockSpec((width, columns), lambda s, start: (start[s], 0)),
                pl.BlockSpec((width, slots), lambda s, start: (start[s], 0)),
                pl.BlockSpec((width, slots), lambda s, start: (s, 0)),
                whole(1),
                whole(columns),
                whole(slots),
            ],
            out_specs=[whole(columns), whole(rank_part), whole(rank_part)],
            scratch_shapes=[pltpu.VMEM((rows, slots), F32)] * 2,
        ),
        compiler_params=PARAMS,
        cost_estimate=pl.CostEstimate(
            flops=4 * width * rows * (columns + 2 * slots),
            bytes_accessed=4 * width * (rows + columns + 2 * slots) + 8 * rows * columns,
            transcendentals=0,
        ),
    )(start, first, second, weight, down, other_down, slot, base, low)


def prepare_kernel(facts, places, base, third, weight, *refs):
    *refs, total, last_rows, x, rows_of, up, spread, sems = refs
    *lows, slot = refs[2:]
    blocks = refs[:2]
    width = x.shape[1]
    length, rank, _ = blocks[0].shape
    rank_part = lows[0].shape[1]
    count = up.shape[0] // rank
    me, which, start = facts[0], facts[1], facts[2]
    part = min(total.shape[1], 512)

    def rows_at(half):
        return weight.at[pl.ds(pl.multiple_of((start + half) * width, width), width)]

    to_total = pltpu.make_async_copy(base, total, sems.at[0])
    to_x = pltpu.make_async_copy(third, x, sems.at[1])
    to_rows = pltpu.make_async_copy(rows_at(0), rows_of, sems.at[2])
    to_last = pltpu.make_async_copy(rows_at(1), last_rows, sems.at[3])
    pages = [up.at[pl.ds(e * rank, rank)] for e in range(count)]
    page_sems = [sems.at[4 + e] for e in range(count)]
    start_pages(places, blocks, length, pages, page_sems, lambda page: page)
    to_total.start()

    @pl.when(which != 0)
    def _():
        to_x.start()
        to_rows.start()
        to_last.start()

    low = jnp.concatenate([part_of[...].astype(F32) for part_of in lows], axis=1)
    low = pltpu.roll(low, me * rank_part, 1)
    for e in range(count):
        spread[:, e * rank:(e + 1) * rank] = jnp.where(slot[...] == e, low, 0.0).astype(BF16)
    for page, sem in zip(pages, page_sems):
        pltpu.make_async_copy(blocks[0].at[0], page, sem).wait()
    to_total.wait()
    for n in range(0, total.shape[1], part):
        cut = slice(n, n + part)
        total[:, cut] += jnp.dot(spread[...], up[:, cut], preferred_element_type=F32)

    @pl.when(which != 0)
    def _():
        to_x.wait()
        to_rows.wait()
        for n in range(0, total.shape[1], part):
            cut = slice(n, n + part)
            total[:, cut] += jnp.dot(x[...], rows_of[:, cut], preferred_element_type=F32)
        to_last.wait()


def prepare(facts, places, base, third, weight, blocks, lows, slot):
    rows, columns = base.shape
    width = third.shape[1]
    rank = blocks[0].shape[1]
    entries = places.shape[0]
    return pl.pallas_call(
        prepare_kernel,
        out_shape=[pltpu.VMEM((rows, columns), F32), pltpu.VMEM((width, columns), BF16)],
        in_specs=[pl.BlockSpec(memory_space=pltpu.SMEM)] * 2 + [IN_HBM] * 5 + [RESIDENT] * (len(lows) + 1),
        out_specs=[RESIDENT] * 2,
        scratch_shapes=[
            pltpu.VMEM((rows, width), BF16),
            pltpu.VMEM((width, columns), BF16),
            pltpu.VMEM((entries * rank, columns), BF16),
            pltpu.VMEM((rows, entries * rank), BF16),
            pltpu.SemaphoreType.DMA((4 + entries,)),
        ],
        compiler_params=TAIL_PARAMS,
        cost_estimate=pl.CostEstimate(
            flops=2 * (width + entries * rank) * rows * columns,
            bytes_accessed=2 * (2 * width + entries * rank + 2 * rows) * columns,
            transcendentals=0,
        ),
    )(facts, places, base, third, weight, *blocks, *lows, slot)


def last_kernel(facts, total, weight, x, out):
    part = out.shape[1]
    cut = pl.ds(pl.multiple_of(pl.program_id(0) * part, part), part)

    @pl.when(facts[1] != 0)
    def _():
        out[...] = (total[:, cut] + jnp.dot(x[...], weight[:, cut], preferred_element_type=F32)).astype(BF16)

    @pl.when(facts[1] == 0)
    def _():
        out[...] = total[:, cut].astype(BF16)


def add_last(facts, total, weight, x):
    rows, columns = total.shape
    part = min(columns, 512)
    return pl.pallas_call(
        last_kernel,
        out_shape=jax.ShapeDtypeStruct((rows, columns), BF16),
        grid=(columns // part,),
        in_specs=[pl.BlockSpec(memory_space=pltpu.SMEM), RESIDENT, RESIDENT, pl.BlockSpec(x.shape, lambda n: (0, 0))],
        out_specs=pl.BlockSpec((rows, part), lambda n: (0, n)),
        compiler_params=TAIL_PARAMS,
        cost_estimate=pl.CostEstimate(
            flops=2 * x.shape[1] * rows * columns, bytes_accessed=2 * rows * columns, transcendentals=0
        ),
    )(facts, total, weight, x)


def after(value, *earlier):
    return lax.optimization_barrier((value,) + earlier)[0]


def looked_up(table, ids):
    hit = ids[:, None] == jnp.arange(table.shape[0])[None, :]
    return jnp.sum(jnp.where(hit, table[None, :], 0), axis=1)


def local(
    attention_result,
    output_weight,
    adapter_down_weight,
    adapter_up_weight,
    adapter_page_row,
    requests,
    row_request_entry,
    ranks,
):
    n_dp = lax.axis_size("dp")
    n_tensor = lax.axis_size("tensor")
    me = lax.axis_index("tensor")
    rows, width = attention_result.shape
    holder_length, rank_part, _ = adapter_down_weight.shape
    rank, columns = adapter_up_weight.shape[1:]
    own_list = requests[0]
    entries = own_list.shape[0]
    one_hot = row_request_entry[:, None] == jnp.arange(entries)[None, :]
    row_rank = jnp.sum(jnp.where(one_hot, looked_up(ranks, own_list)[None, :], 0), axis=1)
    pages = looked_up(adapter_page_row, own_list)
    apart = (pages // holder_length) ^ lax.axis_index("dp")
    places = apart * holder_length + pages % holder_length
    if n_tensor != 4 or n_dp != 4 or width % 256 or rank_part % 16 or entries * rank_part > 256:
        return plain(
            attention_result, output_weight, adapter_down_weight, adapter_up_weight, places, one_hot, row_rank
        )

    places = (apart % 2 * 2 + apart // 2) * holder_length + pages % holder_length

    def across(x, distance):
        return lax.ppermute(x, "dp", [(i, i ^ distance) for i in range(n_dp)])

    right = [(i, i + 1) for i in range(n_tensor - 1)]
    left = [(i + 1, i) for i in range(n_tensor - 1)]
    upper = me >= n_tensor // 2
    ends = me * (n_tensor - 1 - me) == 0
    slot = row_request_entry[:, None]

    right_1 = lax.ppermute(attention_result, "tensor", right)
    left_1 = lax.ppermute(attention_result, "tensor", left)
    far_down = across(adapter_down_weight, 2)
    far_up = across(adapter_up_weight, 2)

    right_2 = lax.ppermute(right_1, "tensor", right[1:])
    left_2 = lax.ppermute(left_1, "tensor", left[:-1])
    downs = jnp.concatenate([adapter_down_weight, after(far_down, right_1, left_1)], axis=0)
    downs = (downs, across(downs, 1))
    down = join_downs(places, downs, n_tensor)
    farthest = jnp.where(upper, 0, n_tensor - 1)
    other_down = lax.dynamic_slice_in_dim(down, farthest * width, width, 0)
    other_down = lax.ppermute(other_down, "tensor", [(0, 1), (3, 2)])

    near = me + jnp.array([0, -1, 1], jnp.int32)
    base, low = near_products([attention_result, right_1, left_1], near, output_weight, down)

    right_2, left_2 = lax.optimization_barrier((base, right_2, left_2))[1:]
    half = width // 2
    first_2 = jnp.where(upper, right_2[:, :half], left_2[:, :half])
    first_3 = lax.ppermute(first_2, "tensor", right[-1:] + left[:1])
    second_2 = jnp.where(upper, right_2[:, half:], left_2[:, half:])
    second_3 = lax.ppermute(second_2, "tensor", right[-1:] + left[:1])

    ups = jnp.concatenate([adapter_up_weight, after(far_up, second_2)], axis=0)
    ups = (ups, across(ups, 1))
    source = jnp.where(upper, me - 2, me + 2)
    base, low, other = add_far(base, low, first_2, second_2, source, output_weight, down, other_down, slot, rank_part)
    low = low + lax.ppermute(other, "tensor", [(1, 0), (2, 3)])
    live = row_rank[:, None] - me * rank_part
    low = jnp.where(jnp.arange(rank_part)[None, :] < live, low, 0.0).astype(BF16)
    lows = [low] + [
        lax.ppermute(low, "tensor", [(i, (i - j) % n_tensor) for i in range(n_tensor)])
        for j in range(1, n_tensor)
    ]
    facts = jnp.stack([me, ends.astype(jnp.int32), 2 * farthest]).astype(jnp.int32)
    total, rows_of = prepare(facts, places, base, first_3, output_weight, ups, lows, slot)
    total, rows_of, second_3 = lax.optimization_barrier((total, rows_of, second_3))
    return add_last(facts, total, rows_of, second_3)


def gather_pages(block, n_dp):
    return [block] + [
        lax.ppermute(block, "dp", [(i, i ^ j) for i in range(n_dp)]) for j in range(1, n_dp)
    ]


def plain(x, output_weight, down_weight, up_weight, places, one_hot, row_rank):
    n_dp = lax.axis_size("dp")
    rows = x.shape[0]
    rank, columns = up_weight.shape[1:]
    entries = one_hot.shape[1]

    def requested(block):
        blocks = jnp.concatenate(gather_pages(block, n_dp), axis=0)
        return jnp.concatenate(
            [lax.dynamic_slice_in_dim(blocks, places[e], 1, 0) for e in range(entries)], axis=0
        )

    down, up = requested(down_weight), requested(up_weight)
    x = lax.all_gather(x, "tensor", axis=1, tiled=True)
    base = jnp.dot(x, output_weight, preferred_element_type=F32)
    low = jnp.einsum("rd,ekd->rek", x, down, preferred_element_type=F32)
    low = jnp.sum(jnp.where(one_hot[:, :, None], low, 0.0), axis=1).astype(BF16)
    low = lax.all_gather(low, "tensor", axis=1, tiled=True)
    low = jnp.where(jnp.arange(rank)[None, :] < row_rank[:, None], low, jnp.zeros_like(low))
    spread = jnp.where(one_hot[:, :, None], low[:, None, :], jnp.zeros((), BF16))
    term = jnp.dot(
        spread.reshape(rows, entries * rank), up.reshape(entries * rank, columns), preferred_element_type=F32
    )
    return (base + term).astype(BF16)


def solution(mesh):
    in_specs = (
        P(("groups", "dp"), "tensor"),
        P(None, "tensor"),
        P("dp", "tensor", None),
        P("dp", None, "tensor"),
        P("groups"),
        P(("groups", "dp"), None),
        P(("groups", "dp")),
        P(),
    )
    out_specs = P(("groups", "dp"), "tensor")
    return jax.shard_map(local, mesh=mesh, in_specs=in_specs, out_specs=out_specs, check_vma=False)
```

```python
import functools

import jax
import jax.numpy as jnp
from jax import lax
from jax.experimental import pallas as pl
from jax.experimental.pallas import tpu as pltpu
from jax.sharding import PartitionSpec as P

PARAMS = pltpu.CompilerParams(vmem_limit_bytes=48 * 2**20)
TAIL_PARAMS = pltpu.CompilerParams(vmem_limit_bytes=24 * 2**20)
F32 = jnp.float32
BF16 = jnp.bfloat16


def start_pages(places, blocks, length, targets, sems, rows_of):
    for e, target in enumerate(targets):
        for j, block in enumerate(blocks):

            @pl.when(places[e] // length == j)
            def _():
                pltpu.make_async_copy(rows_of(block.at[lax.rem(places[e], length)]), target, sems[e]).start()


def join_downs_kernel(places, *refs):
    *blocks, out, held, sems = refs
    length, rank_part, _ = blocks[0].shape
    shards, slots, width = held.shape
    step = pl.program_id(0)

    def targets(t):
        return [held.at[t, pl.ds(e * rank_part, rank_part)] for e in range(slots // rank_part)]

    @pl.when(step == 0)
    def _():
        for t in range(shards):
            semaphores = [sems.at[t, e] for e in range(slots // rank_part)]
            start_pages(
                places, blocks, length, targets(t), semaphores, lambda page: page.at[:, pl.ds(t * width, width)]
            )

    for t in range(shards):

        @pl.when(step == t)
        def _():
            for e, target in enumerate(targets(t)):
                source = blocks[0].at[0, :, pl.ds(t * width, width)]
                pltpu.make_async_copy(source, target, sems.at[t, e]).wait()
            out[...] = held[t].T


def join_downs(places, blocks, shards):
    entries = places.shape[0]
    _, rank_part, features = blocks[0].shape
    width, slots = features // shards, entries * rank_part
    return pl.pallas_call(
        join_downs_kernel,
        out_shape=jax.ShapeDtypeStruct((features, slots), BF16),
        grid=(shards,),
        in_specs=[pl.BlockSpec(memory_space=pltpu.SMEM)] + [pl.BlockSpec(memory_space=pltpu.HBM)] * len(blocks),
        out_specs=pl.BlockSpec((width, slots), lambda t: (t, 0)),
        scratch_shapes=[pltpu.VMEM((shards, slots, width), BF16), pltpu.SemaphoreType.DMA((shards, entries))],
        compiler_params=TAIL_PARAMS,
        cost_estimate=pl.CostEstimate(flops=0, bytes_accessed=4 * features * slots, transcendentals=0),
    )(places, *blocks)


RESIDENT = pl.BlockSpec(memory_space=pltpu.VMEM)
IN_HBM = pl.BlockSpec(memory_space=pltpu.HBM)


def fold_entry(low, slot, rank_part):
    lane = lax.broadcasted_iota(jnp.int32, low.shape, 1)
    own = jnp.where(lane // rank_part == slot, low, 0.0)
    shape = (low.shape[1], rank_part)
    fold = lax.rem(lax.broadcasted_iota(jnp.int32, shape, 0), rank_part) == lax.broadcasted_iota(jnp.int32, shape, 1)
    return jnp.dot(own, fold.astype(F32), precision=lax.Precision.HIGHEST, preferred_element_type=F32)


def shards_kernel(with_low, start, valid, *refs):
    refs = list(refs)
    xs = [refs.pop(0) for _ in range(valid.shape[0])]
    weight = refs.pop(0)
    if with_low:
        down, slot, base, low, acc = refs
    else:
        base_in, base = refs
    step = pl.program_id(0)

    @pl.when(step == 0)
    def _():
        base[...] = jnp.zeros_like(base) if with_low else base_in[...]
        if with_low:
            acc[...] = jnp.zeros_like(acc)

    for i, x in enumerate(xs):

        @pl.when((step // 2 == i) & (valid[i] != 0))
        def _():
            part = min(base.shape[1], 512)
            for n in range(0, base.shape[1], part):
                base[:, n:n + part] += jnp.dot(x[...], weight[:, n:n + part], preferred_element_type=F32)
            if with_low:
                acc[...] += jnp.dot(x[...], down[...], preferred_element_type=F32)

    if with_low:

        @pl.when(step == pl.num_programs(0) - 1)
        def _():
            low[...] = fold_entry(acc[...], slot[...], low.shape[1])


def add_shards(base, xs, source, weight, down=None, slot=None, rank_part=0):
    rows, width = xs[0].shape
    half = width // 2
    columns = weight.shape[1]
    n_tensor = weight.shape[0] // width
    there = (source >= 0) & (source < n_tensor)
    start = 2 * jnp.clip(source, 0, n_tensor - 1)[:, None] + jnp.arange(2)[None, :]
    idle = jnp.concatenate([start[1:2, :1], start[:-1, 1:]], axis=0)
    start = jnp.where(there[:, None], start, idle).reshape(-1).astype(jnp.int32)
    steps = 2 * len(xs)

    def whole(a):
        return pl.BlockSpec((rows, a), lambda s, *_: (0, 0))

    def walked(a):
        return pl.BlockSpec((half, a.shape[1]), lambda s, start, valid: (start[s], 0))

    in_specs = [
        pl.BlockSpec((rows, half), lambda s, *_, i=i: (0, jnp.clip(s - 2 * i, 0, 1))) for i in range(len(xs))
    ] + [walked(weight)]
    out_shape = [jax.ShapeDtypeStruct((rows, columns), F32)]
    scratch = []
    slots = 0
    if base is None:
        slots = down.shape[1]
        in_specs += [walked(down), whole(1)]
        out_shape += [jax.ShapeDtypeStruct((rows, rank_part), F32)]
        scratch = [pltpu.VMEM((rows, slots), F32)]
        rest = (down, slot)
    else:
        in_specs += [whole(columns)]
        rest = (base,)
    return pl.pallas_call(
        functools.partial(shards_kernel, base is None),
        out_shape=out_shape,
        grid_spec=pltpu.PrefetchScalarGridSpec(
            num_scalar_prefetch=2,
            grid=(steps,),
            in_specs=in_specs,
            out_specs=[whole(a.shape[1]) for a in out_shape],
            scratch_shapes=scratch,
        ),
        compiler_params=PARAMS,
        cost_estimate=pl.CostEstimate(
            flops=2 * steps * half * rows * (columns + slots),
            bytes_accessed=2 * steps * half * (rows + columns + slots) + 8 * rows * columns,
            transcendentals=0,
        ),
    )(start, there.astype(jnp.int32), *xs, weight, *rest)


def half_kernel(start, valid, x, weight, base_in, base):
    step = pl.program_id(0)

    @pl.when(step == 0)
    def _():
        base[...] = base_in[...]

    @pl.when(valid[0] != 0)
    def _():
        part = min(base.shape[1], 512)
        for n in range(0, base.shape[1], part):
            base[:, n:n + part] += jnp.dot(x[...], weight[:, n:n + part], preferred_element_type=F32)


def add_half(base, x, valid, source, weight):
    rows, half = x.shape
    columns = weight.shape[1]
    step = half // 2
    whole = pl.BlockSpec((rows, columns), lambda s, *_: (0, 0))
    return pl.pallas_call(
        half_kernel,
        out_shape=jax.ShapeDtypeStruct((rows, columns), F32),
        grid_spec=pltpu.PrefetchScalarGridSpec(
            num_scalar_prefetch=2,
            grid=(2,),
            in_specs=[
                pl.BlockSpec((rows, step), lambda s, *_: (0, s)),
                pl.BlockSpec((step, columns), lambda s, source, valid: (source[0] * 4 + s, 0)),
                whole,
            ],
            out_specs=whole,
        ),
        compiler_params=PARAMS,
        cost_estimate=pl.CostEstimate(
            flops=2 * half * rows * columns,
            bytes_accessed=2 * half * (rows + columns) + 8 * rows * columns,
            transcendentals=0,
        ),
    )(source[None], valid[None], x, weight, base)


def far_low_kernel(
    facts, left_1, left_2, right_1, right_2, down, other_down, slot, row_rank, low, other_low,
    out, near_x, far_x, rows_of, other_rows, sems
):
    me, end, source, upper = facts[0], facts[1], facts[2], facts[3]
    width = far_x.shape[1]
    rank_part = low.shape[1]
    start = pl.multiple_of(source * width, width)

    @pl.when(upper != 0)
    def _():
        pltpu.make_async_copy(left_2, far_x, sems.at[0]).start()
        pltpu.make_async_copy(left_1, near_x, sems.at[1]).start()

    @pl.when(upper == 0)
    def _():
        pltpu.make_async_copy(right_2, far_x, sems.at[0]).start()
        pltpu.make_async_copy(right_1, near_x, sems.at[1]).start()

    copies = [
        pltpu.make_async_copy(down.at[pl.ds(start, width)], rows_of, sems.at[2]),
        pltpu.make_async_copy(other_down, other_rows, sems.at[3]),
    ]
    for copy in copies:
        copy.start()
    pltpu.make_async_copy(left_2, far_x, sems.at[0]).wait()

    def finished(total, sums, place):
        sums = total[...] + fold_entry(sums, slot[...], rank_part)
        k = lax.broadcasted_iota(jnp.int32, sums.shape, 1) + place * rank_part
        return jnp.where(k < row_rank[...], sums, 0.0)

    copies[0].wait()
    own = finished(low, jnp.dot(far_x[...], rows_of[...], preferred_element_type=F32), me)
    pltpu.make_async_copy(left_1, near_x, sems.at[1]).wait()
    copies[1].wait()
    far_rows = other_rows[pl.ds(pl.multiple_of((1 - upper) * width, width), width)]
    near_rows = other_rows[pl.ds(pl.multiple_of(upper * width, width), width)]
    sums = jnp.dot(far_x[...], far_rows, preferred_element_type=F32)
    sums += jnp.dot(near_x[...], near_rows, preferred_element_type=F32)
    other = finished(other_low, sums, end)
    at_left = jnp.concatenate([other, own], axis=1)
    at_right = jnp.concatenate([own, other], axis=1)
    out[...] = jnp.where(upper != 0, at_right, at_left).astype(BF16)


def far_low(facts, left_1, left_2, right_1, right_2, down, other_down, slot, row_rank, low, other_low):
    rows, width = left_1.shape
    slots = down.shape[1]
    return pl.pallas_call(
        far_low_kernel,
        out_shape=jax.ShapeDtypeStruct((rows, 2 * low.shape[1]), BF16),
        in_specs=[pl.BlockSpec(memory_space=pltpu.SMEM)] + [IN_HBM] * 6 + [RESIDENT] * 4,
        out_specs=RESIDENT,
        scratch_shapes=[
            pltpu.VMEM((rows, width), BF16),
            pltpu.VMEM((rows, width), BF16),
            pltpu.VMEM((width, slots), BF16),
            pltpu.VMEM((2 * width, slots), BF16),
            pltpu.SemaphoreType.DMA((4,)),
        ],
        compiler_params=TAIL_PARAMS,
        cost_estimate=pl.CostEstimate(
            flops=6 * width * rows * slots, bytes_accessed=2 * width * (2 * rows + 3 * slots), transcendentals=0
        ),
    )(facts, left_1, left_2, right_1, right_2, down, other_down, slot, row_rank, low, other_low)


def prepare_kernel(facts, places, base, sent, received, weight, *refs):
    *blocks, slot, total, last_rows, mid, mid_rows, up, spread, sems = refs
    mid_width, last_width = mid_rows.shape[0], last_rows.shape[0]
    width = mid_width + last_width
    length, rank, _ = blocks[0].shape
    count = up.shape[0] // rank
    which, start = facts[0], facts[1] * 2 * width + width
    part = min(total.shape[1], 512)

    def rows_at(first, length):
        return weight.at[pl.ds(pl.multiple_of(start + first, length), length)]

    to_total = pltpu.make_async_copy(base, total, sems.at[0])
    to_mid_rows = pltpu.make_async_copy(rows_at(0, mid_width), mid_rows, sems.at[1])
    to_last = pltpu.make_async_copy(rows_at(mid_width, last_width), last_rows, sems.at[2])
    pages = [up.at[pl.ds(e * rank, rank)] for e in range(count)]
    page_sems = [sems.at[4 + e] for e in range(count)]

    @pl.when(which == 0)
    def _():
        pltpu.make_async_copy(sent, mid, sems.at[3]).start()

    @pl.when(which != 0)
    def _():
        pltpu.make_async_copy(received, mid, sems.at[3]).start()

    to_total.start()
    start_pages(places, blocks, length, pages, page_sems, lambda page: page)

    @pl.when(which != 0)
    def _():
        to_mid_rows.start()
        to_last.start()

    pltpu.make_async_copy(sent, mid, sems.at[3]).wait()
    for e in range(count):
        spread[:, e * rank:(e + 1) * rank] = jnp.where(
            slot[...] == e, mid[:, mid_width:].astype(F32), 0.0
        ).astype(BF16)
    for page, sem in zip(pages, page_sems):
        pltpu.make_async_copy(blocks[0].at[0], page, sem).wait()
    to_total.wait()
    for n in range(0, total.shape[1], part):
        cut = slice(n, n + part)
        total[:, cut] += jnp.dot(spread[...], up[:, cut], preferred_element_type=F32)

    @pl.when(which != 0)
    def _():
        to_mid_rows.wait()
        for n in range(0, total.shape[1], part):
            cut = slice(n, n + part)
            total[:, cut] += jnp.dot(mid[:, :mid_width], mid_rows[:, cut], preferred_element_type=F32)
        to_last.wait()


def prepare(facts, places, base, sent, received, weight, blocks, slot):
    rows, columns = base.shape
    rank = blocks[0].shape[1]
    entries = places.shape[0]
    mid_width = sent.shape[1] - rank
    last_width = mid_width
    return pl.pallas_call(
        prepare_kernel,
        out_shape=[pltpu.VMEM((rows, columns), F32), pltpu.VMEM((last_width, columns), BF16)],
        in_specs=[pl.BlockSpec(memory_space=pltpu.SMEM)] * 2 + [IN_HBM] * (4 + len(blocks)) + [RESIDENT],
        out_specs=[RESIDENT] * 2,
        scratch_shapes=[
            pltpu.VMEM(sent.shape, BF16),
            pltpu.VMEM((mid_width, columns), BF16),
            pltpu.VMEM((entries * rank, columns), BF16),
            pltpu.VMEM((rows, entries * rank), BF16),
            pltpu.SemaphoreType.DMA((4 + entries,)),
        ],
        compiler_params=TAIL_PARAMS,
        cost_estimate=pl.CostEstimate(
            flops=2 * (mid_width + entries * rank) * rows * columns,
            bytes_accessed=2 * (columns + entries * rank + 2 * rows) * columns,
            transcendentals=0,
        ),
    )(facts, places, base, sent, received, weight, *blocks, slot)


def last_kernel(facts, total, weight, x, out):
    part = out.shape[1]
    cut = pl.ds(pl.multiple_of(pl.program_id(0) * part, part), part)

    @pl.when(facts[0] != 0)
    def _():
        out[...] = (total[:, cut] + jnp.dot(x[...], weight[:, cut], preferred_element_type=F32)).astype(BF16)

    @pl.when(facts[0] == 0)
    def _():
        out[...] = total[:, cut].astype(BF16)


def add_last(facts, total, weight, x):
    rows, columns = total.shape
    part = min(columns, 512)
    return pl.pallas_call(
        last_kernel,
        out_shape=jax.ShapeDtypeStruct((rows, columns), BF16),
        grid=(columns // part,),
        in_specs=[pl.BlockSpec(memory_space=pltpu.SMEM), RESIDENT, RESIDENT, pl.BlockSpec(x.shape, lambda n: (0, 0))],
        out_specs=pl.BlockSpec((rows, part), lambda n: (0, n)),
        compiler_params=TAIL_PARAMS,
        cost_estimate=pl.CostEstimate(
            flops=2 * x.shape[1] * rows * columns, bytes_accessed=2 * rows * columns, transcendentals=0
        ),
    )(facts, total, weight, x)


def after(value, *earlier):
    return lax.optimization_barrier((value,) + earlier)[0]


def looked_up(table, ids):
    hit = ids[:, None] == jnp.arange(table.shape[0])[None, :]
    return jnp.sum(jnp.where(hit, table[None, :], 0), axis=1)


def local(
    attention_result,
    output_weight,
    adapter_down_weight,
    adapter_up_weight,
    adapter_page_row,
    requests,
    row_request_entry,
    ranks,
):
    n_dp = lax.axis_size("dp")
    n_tensor = lax.axis_size("tensor")
    me = lax.axis_index("tensor")
    rows, width = attention_result.shape
    holder_length, rank_part, _ = adapter_down_weight.shape
    rank, columns = adapter_up_weight.shape[1:]
    own_list = requests[0]
    entries = own_list.shape[0]
    one_hot = row_request_entry[:, None] == jnp.arange(entries)[None, :]
    row_rank = jnp.sum(jnp.where(one_hot, looked_up(ranks, own_list)[None, :], 0), axis=1)
    pages = looked_up(adapter_page_row, own_list)
    places = ((pages // holder_length) ^ lax.axis_index("dp")) * holder_length + pages % holder_length
    if n_tensor != 4 or n_dp != 4 or width % 512 or columns != width or rank_part % 16 or entries * rank_part > 256:
        return plain(
            attention_result, output_weight, adapter_down_weight, adapter_up_weight, places, one_hot, row_rank
        )


    def across(x, distance):
        return lax.ppermute(x, "dp", [(i, i ^ distance) for i in range(n_dp)])

    right = [(i, i + 1) for i in range(n_tensor - 1)]
    left = [(i + 1, i) for i in range(n_tensor - 1)]
    upper = me >= n_tensor // 2
    ends = me * (n_tensor - 1 - me) == 0
    slot = row_request_entry[:, None]

    right_1 = lax.ppermute(attention_result, "tensor", right)
    left_1 = lax.ppermute(attention_result, "tensor", left)
    far_down = across(adapter_down_weight, 2)
    far_up = across(adapter_up_weight, 2)
    near_down = across(adapter_down_weight, 1)

    right_2 = lax.ppermute(right_1, "tensor", right[1:])
    left_2 = lax.ppermute(left_1, "tensor", left[:-1])
    downs = (adapter_down_weight, near_down, far_down, across(after(far_down, right_1, left_1), 1))
    down = join_downs(places, downs, n_tensor)
    farthest = jnp.where(upper, 0, n_tensor - 1)
    other_down = lax.dynamic_slice_in_dim(down, jnp.where(upper, 0, 2 * width), 2 * width, 0)
    other_down = lax.ppermute(other_down, "tensor", [(0, 1), (3, 2)])

    near = me + jnp.array([0, -1, 1], jnp.int32)
    base, low = add_shards(
        None, [attention_result, right_1, left_1], near, output_weight, down, slot, rank_part
    )
    other_low = lax.ppermute(low, "tensor", [(0, 1), (3, 2)])

    right_2, left_2, other_down, other_low = lax.optimization_barrier((right_2, left_2, other_down, other_low))
    third = right[-1:] + left[:1]
    cuts = (0, width // 2, width // 4 * 3, width)

    def piece(i):
        cut = slice(cuts[i], cuts[i + 1])
        return jnp.where(upper, right_2[:, cut], left_2[:, cut])

    first_2 = piece(0)
    first_3 = lax.ppermute(first_2, "tensor", third)
    right_2, left_2 = lax.optimization_barrier((first_2, right_2, left_2))[1:]
    end = jnp.where(upper, n_tensor - 1, 0)
    source = jnp.where(upper, me - 2, me + 2)
    pair = far_low(
        jnp.stack([me, end, source, upper.astype(jnp.int32)]).astype(jnp.int32),
        right_1, right_2, left_1, left_2, down, other_down, slot, row_rank[:, None], low, other_low,
    )
    from_middle = lax.ppermute(pair, "tensor", [(1, 2), (2, 1)])
    far = me + jnp.array([-2, 2], jnp.int32)
    base, = add_shards(after(base, pair), [right_2, left_2], far, output_weight)
    low = jnp.where(upper, jnp.concatenate([from_middle, pair], axis=1), jnp.concatenate([pair, from_middle], axis=1))
    second_2 = jnp.concatenate([piece(1), low], axis=1)
    second_3 = lax.ppermute(second_2, "tensor", third)
    right_2, left_2 = lax.optimization_barrier((second_2, right_2, left_2))[1:]
    last_3 = lax.ppermute(piece(2), "tensor", third)
    ups = (adapter_up_weight, across(after(adapter_up_weight, far_down), 1), far_up, across(after(far_up, first_2), 1))
    facts = jnp.stack([ends.astype(jnp.int32), farthest]).astype(jnp.int32)
    base = add_half(base, first_3, facts[0], facts[1], output_weight)
    total, rows_of = prepare(facts, places, base, second_2, second_3, output_weight, ups, slot)
    total, rows_of, last_3 = lax.optimization_barrier((total, rows_of, last_3))
    return add_last(facts, total, rows_of, last_3)


def gather_pages(block, n_dp):
    return [block] + [
        lax.ppermute(block, "dp", [(i, i ^ j) for i in range(n_dp)]) for j in range(1, n_dp)
    ]


def plain(x, output_weight, down_weight, up_weight, places, one_hot, row_rank):
    n_dp = lax.axis_size("dp")
    rows = x.shape[0]
    rank, columns = up_weight.shape[1:]
    entries = one_hot.shape[1]

    def requested(block):
        blocks = jnp.concatenate(gather_pages(block, n_dp), axis=0)
        return jnp.concatenate(
            [lax.dynamic_slice_in_dim(blocks, places[e], 1, 0) for e in range(entries)], axis=0
        )

    down, up = requested(down_weight), requested(up_weight)
    x = lax.all_gather(x, "tensor", axis=1, tiled=True)
    base = jnp.dot(x, output_weight, preferred_element_type=F32)
    low = jnp.einsum("rd,ekd->rek", x, down, preferred_element_type=F32)
    low = jnp.sum(jnp.where(one_hot[:, :, None], low, 0.0), axis=1).astype(BF16)
    low = lax.all_gather(low, "tensor", axis=1, tiled=True)
    low = jnp.where(jnp.arange(rank)[None, :] < row_rank[:, None], low, jnp.zeros_like(low))
    spread = jnp.where(one_hot[:, :, None], low[:, None, :], jnp.zeros((), BF16))
    term = jnp.dot(
        spread.reshape(rows, entries * rank), up.reshape(entries * rank, columns), preferred_element_type=F32
    )
    return (base + term).astype(BF16)


def solution(mesh):
    in_specs = (
        P(("groups", "dp"), "tensor"),
        P(None, "tensor"),
        P("dp", "tensor", None),
        P("dp", None, "tensor"),
        P("groups"),
        P(("groups", "dp"), None),
        P(("groups", "dp")),
        P(),
    )
    out_specs = P(("groups", "dp"), "tensor")
    return jax.shard_map(local, mesh=mesh, in_specs=in_specs, out_specs=out_specs, check_vma=False)
```

```python
import functools

import jax
import jax.numpy as jnp
from jax import lax
from jax.experimental import pallas as pl
from jax.experimental.pallas import tpu as pltpu
from jax.sharding import PartitionSpec as P

PARAMS = pltpu.CompilerParams(vmem_limit_bytes=48 * 2**20)
TAIL_PARAMS = pltpu.CompilerParams(vmem_limit_bytes=24 * 2**20)
F32 = jnp.float32
BF16 = jnp.bfloat16


def start_pages(places, blocks, length, targets, sems, rows_of):
    for e, target in enumerate(targets):
        for j, block in enumerate(blocks):

            @pl.when(places[e] // length == j)
            def _():
                pltpu.make_async_copy(rows_of(block.at[lax.rem(places[e], length)]), target, sems[e]).start()


def join_downs_kernel(places, upper, *refs):
    *blocks, out, other, held, sems = refs
    length, rank_part, _ = blocks[0].shape
    shards, slots, width = held.shape
    entries = places.shape[0]
    step = pl.program_id(0)

    def targets(t):
        return [held.at[t, pl.ds(e * rank_part, rank_part)] for e in range(entries)]

    @pl.when(step == 0)
    def _():
        for t in range(shards):
            semaphores = [sems.at[t, e] for e in range(entries)]
            start_pages(
                places, blocks, length, targets(t), semaphores, lambda page: page.at[:, pl.ds(t * width, width)]
            )
            held[t, entries * rank_part:] = jnp.zeros((slots - entries * rank_part, width), BF16)

    for t in range(shards):

        @pl.when(step == t)
        def _():
            for e, target in enumerate(targets(t)):
                source = blocks[0].at[0, :, pl.ds(t * width, width)]
                pltpu.make_async_copy(source, target, sems.at[t, e]).wait()
            joined = held[t].T
            out[...] = joined
            half = shards // 2

            @pl.when((upper[0] != 0) == (t < half))
            def _():
                other[t % half * width:(t % half + 1) * width] = joined


def join_downs(places, upper, blocks, shards):
    entries = places.shape[0]
    _, rank_part, features = blocks[0].shape
    width, slots = features // shards, -(-entries * rank_part // 128) * 128
    return pl.pallas_call(
        join_downs_kernel,
        out_shape=[jax.ShapeDtypeStruct((a, slots), BF16) for a in (features, features // 2)],
        grid=(shards,),
        in_specs=[pl.BlockSpec(memory_space=pltpu.SMEM)] * 2
        + [pl.BlockSpec(memory_space=pltpu.HBM)] * len(blocks),
        out_specs=[
            pl.BlockSpec((width, slots), lambda t: (t, 0)),
            pl.BlockSpec((features // 2, slots), lambda t: (0, 0)),
        ],
        scratch_shapes=[pltpu.VMEM((shards, slots, width), BF16), pltpu.SemaphoreType.DMA((shards, entries))],
        compiler_params=TAIL_PARAMS,
        cost_estimate=pl.CostEstimate(flops=0, bytes_accessed=4 * features * slots, transcendentals=0),
    )(places, upper, *blocks)


RESIDENT = pl.BlockSpec(memory_space=pltpu.VMEM)
IN_HBM = pl.BlockSpec(memory_space=pltpu.HBM)


def fold_entry(low, slot, rank_part):
    lane = lax.broadcasted_iota(jnp.int32, low.shape, 1)
    own = jnp.where(lane // rank_part == slot, low, 0.0)
    shape = (low.shape[1], rank_part)
    fold = lax.rem(lax.broadcasted_iota(jnp.int32, shape, 0), rank_part) == lax.broadcasted_iota(jnp.int32, shape, 1)
    return jnp.dot(own, fold.astype(F32), precision=lax.Precision.HIGHEST, preferred_element_type=F32)


def shards_kernel(with_low, start, valid, *refs):
    refs = list(refs)
    xs = [refs.pop(0) for _ in range(valid.shape[0])]
    weight = refs.pop(0)
    if with_low:
        down, slot, base, low, acc = refs
    else:
        base_in, base = refs
    step = pl.program_id(0)

    @pl.when(step == 0)
    def _():
        base[...] = jnp.zeros_like(base) if with_low else base_in[...]
        if with_low:
            acc[...] = jnp.zeros_like(acc)

    for i, x in enumerate(xs):

        @pl.when((step // 2 == i) & (valid[i] != 0))
        def _():
            part = min(base.shape[1], 512)
            for n in range(0, base.shape[1], part):
                base[:, n:n + part] += jnp.dot(x[...], weight[:, n:n + part], preferred_element_type=F32)
            if with_low:
                acc[...] += jnp.dot(x[...], down[...], preferred_element_type=F32)

    if with_low:

        @pl.when(step == pl.num_programs(0) - 1)
        def _():
            low[...] = fold_entry(acc[...], slot[...], low.shape[1])


def plan_shards(source, n_tensor):
    there = (source >= 0) & (source < n_tensor)
    start = 2 * jnp.clip(source, 0, n_tensor - 1)[:, None] + jnp.arange(2)[None, :]
    idle = jnp.concatenate([start[1:2, :1], start[:-1, 1:]], axis=0)
    start = jnp.where(there[:, None], start, idle).reshape(-1).astype(jnp.int32)
    return start, there.astype(jnp.int32)


def add_shards(base, xs, plan, weight, down=None, slot=None, rank_part=0):
    rows, width = xs[0].shape
    half = width // 2
    columns = weight.shape[1]
    steps = 2 * len(xs)

    def whole(a):
        return pl.BlockSpec((rows, a), lambda s, *_: (0, 0))

    def walked(a):
        return pl.BlockSpec((half, a.shape[1]), lambda s, start, valid: (start[s], 0))

    in_specs = [
        pl.BlockSpec((rows, half), lambda s, *_, i=i: (0, jnp.clip(s - 2 * i, 0, 1))) for i in range(len(xs))
    ] + [walked(weight)]
    out_shape = [jax.ShapeDtypeStruct((rows, columns), F32)]
    scratch = []
    slots = 0
    if base is None:
        slots = down.shape[1]
        in_specs += [walked(down), whole(1)]
        out_shape += [jax.ShapeDtypeStruct((rows, rank_part), F32)]
        scratch = [pltpu.VMEM((rows, slots), F32)]
        rest = (down, slot)
    else:
        in_specs += [whole(columns)]
        rest = (base,)
    return pl.pallas_call(
        functools.partial(shards_kernel, base is None),
        out_shape=out_shape,
        grid_spec=pltpu.PrefetchScalarGridSpec(
            num_scalar_prefetch=2,
            grid=(steps,),
            in_specs=in_specs,
            out_specs=[whole(a.shape[1]) for a in out_shape],
            scratch_shapes=scratch,
        ),
        compiler_params=PARAMS,
        cost_estimate=pl.CostEstimate(
            flops=2 * steps * half * rows * (columns + slots),
            bytes_accessed=2 * steps * half * (rows + columns + slots) + 8 * rows * columns,
            transcendentals=0,
        ),
    )(*plan, *xs, weight, *rest)


def half_kernel(start, valid, x, weight, base_in, base):
    step = pl.program_id(0)

    @pl.when(step == 0)
    def _():
        base[...] = base_in[...]

    @pl.when(valid[0] != 0)
    def _():
        part = min(base.shape[1], 512)
        for n in range(0, base.shape[1], part):
            base[:, n:n + part] += jnp.dot(x[...], weight[:, n:n + part], preferred_element_type=F32)


def add_half(base, x, valid, source, weight):
    rows, half = x.shape
    columns = weight.shape[1]
    step = half // 2
    whole = pl.BlockSpec((rows, columns), lambda s, *_: (0, 0))
    return pl.pallas_call(
        half_kernel,
        out_shape=jax.ShapeDtypeStruct((rows, columns), F32),
        grid_spec=pltpu.PrefetchScalarGridSpec(
            num_scalar_prefetch=2,
            grid=(2,),
            in_specs=[
                pl.BlockSpec((rows, step), lambda s, *_: (0, s)),
                pl.BlockSpec((step, columns), lambda s, source, valid: (source[0] * 4 + s, 0)),
                whole,
            ],
            out_specs=whole,
        ),
        compiler_params=PARAMS,
        cost_estimate=pl.CostEstimate(
            flops=2 * half * rows * columns,
            bytes_accessed=2 * half * (rows + columns) + 8 * rows * columns,
            transcendentals=0,
        ),
    )(source[None], valid[None], x, weight, base)


def far_low_kernel(
    facts, left_1, left_2, right_1, right_2, down, other_down, slot, row_rank, low, other_low,
    out, near_x, far_x, rows_of, other_rows, sems
):
    me, end, source, upper = facts[0], facts[1], facts[2], facts[3]
    width = far_x.shape[1]
    rank_part = low.shape[1]
    start = pl.multiple_of(source * width, width)

    @pl.when(upper != 0)
    def _():
        pltpu.make_async_copy(left_2, far_x, sems.at[0]).start()
        pltpu.make_async_copy(left_1, near_x, sems.at[1]).start()

    @pl.when(upper == 0)
    def _():
        pltpu.make_async_copy(right_2, far_x, sems.at[0]).start()
        pltpu.make_async_copy(right_1, near_x, sems.at[1]).start()

    copies = [
        pltpu.make_async_copy(down.at[pl.ds(start, width)], rows_of, sems.at[2]),
        pltpu.make_async_copy(other_down, other_rows, sems.at[3]),
    ]
    for copy in copies:
        copy.start()
    pltpu.make_async_copy(left_2, far_x, sems.at[0]).wait()

    def finished(total, sums, place):
        sums = total[...] + fold_entry(sums, slot[...], rank_part)
        k = lax.broadcasted_iota(jnp.int32, sums.shape, 1) + place * rank_part
        return jnp.where(k < row_rank[...], sums, 0.0)

    copies[0].wait()
    own = finished(low, jnp.dot(far_x[...], rows_of[...], preferred_element_type=F32), me)
    pltpu.make_async_copy(left_1, near_x, sems.at[1]).wait()
    copies[1].wait()
    far_rows = other_rows[pl.ds(pl.multiple_of((1 - upper) * width, width), width)]
    near_rows = other_rows[pl.ds(pl.multiple_of(upper * width, width), width)]
    sums = jnp.dot(far_x[...], far_rows, preferred_element_type=F32)
    sums += jnp.dot(near_x[...], near_rows, preferred_element_type=F32)
    other = finished(other_low, sums, end)
    at_left = jnp.concatenate([other, own], axis=1)
    at_right = jnp.concatenate([own, other], axis=1)
    out[...] = jnp.where(upper != 0, at_right, at_left).astype(BF16)


def far_low(facts, left_1, left_2, right_1, right_2, down, other_down, slot, row_rank, low, other_low):
    rows, width = left_1.shape
    slots = down.shape[1]
    return pl.pallas_call(
        far_low_kernel,
        out_shape=jax.ShapeDtypeStruct((rows, 2 * low.shape[1]), BF16),
        in_specs=[pl.BlockSpec(memory_space=pltpu.SMEM)] + [IN_HBM] * 6 + [RESIDENT] * 4,
        out_specs=RESIDENT,
        scratch_shapes=[
            pltpu.VMEM((rows, width), BF16),
            pltpu.VMEM((rows, width), BF16),
            pltpu.VMEM((width, slots), BF16),
            pltpu.VMEM((2 * width, slots), BF16),
            pltpu.SemaphoreType.DMA((4,)),
        ],
        compiler_params=TAIL_PARAMS,
        cost_estimate=pl.CostEstimate(
            flops=6 * width * rows * slots, bytes_accessed=2 * width * (2 * rows + 3 * slots), transcendentals=0
        ),
    )(facts, left_1, left_2, right_1, right_2, down, other_down, slot, row_rank, low, other_low)


def prepare_kernel(facts, places, base, sent, received, weight, *refs):
    *blocks, slot, total, last_rows, mid, mid_rows, up, spread, sems = refs
    mid_width, last_width = mid_rows.shape[0], last_rows.shape[0]
    width = mid_width + last_width
    length, rank, _ = blocks[0].shape
    count = up.shape[0] // rank
    which, start = facts[0], facts[1] * 2 * width + width
    part = min(total.shape[1], 512)

    def rows_at(first, length):
        return weight.at[pl.ds(pl.multiple_of(start + first, length), length)]

    to_total = pltpu.make_async_copy(base, total, sems.at[0])
    to_mid_rows = pltpu.make_async_copy(rows_at(0, mid_width), mid_rows, sems.at[1])
    to_last = pltpu.make_async_copy(rows_at(mid_width, last_width), last_rows, sems.at[2])
    pages = [up.at[pl.ds(e * rank, rank)] for e in range(count)]
    page_sems = [sems.at[4 + e] for e in range(count)]

    @pl.when(which == 0)
    def _():
        pltpu.make_async_copy(sent, mid, sems.at[3]).start()

    @pl.when(which != 0)
    def _():
        pltpu.make_async_copy(received, mid, sems.at[3]).start()

    to_total.start()
    start_pages(places, blocks, length, pages, page_sems, lambda page: page)

    @pl.when(which != 0)
    def _():
        to_mid_rows.start()
        to_last.start()

    pltpu.make_async_copy(sent, mid, sems.at[3]).wait()
    for e in range(count):
        spread[:, e * rank:(e + 1) * rank] = jnp.where(
            slot[...] == e, mid[:, mid_width:].astype(F32), 0.0
        ).astype(BF16)
    for page, sem in zip(pages, page_sems):
        pltpu.make_async_copy(blocks[0].at[0], page, sem).wait()
    to_total.wait()
    for n in range(0, total.shape[1], part):
        cut = slice(n, n + part)
        total[:, cut] += jnp.dot(spread[...], up[:, cut], preferred_element_type=F32)

    @pl.when(which != 0)
    def _():
        to_mid_rows.wait()
        for n in range(0, total.shape[1], part):
            cut = slice(n, n + part)
            total[:, cut] += jnp.dot(mid[:, :mid_width], mid_rows[:, cut], preferred_element_type=F32)
        to_last.wait()


def prepare(facts, places, base, sent, received, weight, blocks, slot):
    rows, columns = base.shape
    rank = blocks[0].shape[1]
    entries = places.shape[0]
    mid_width = sent.shape[1] - rank
    last_width = mid_width
    return pl.pallas_call(
        prepare_kernel,
        out_shape=[pltpu.VMEM((rows, columns), F32), pltpu.VMEM((last_width, columns), BF16)],
        in_specs=[pl.BlockSpec(memory_space=pltpu.SMEM)] * 2 + [IN_HBM] * (4 + len(blocks)) + [RESIDENT],
        out_specs=[RESIDENT] * 2,
        scratch_shapes=[
            pltpu.VMEM(sent.shape, BF16),
            pltpu.VMEM((mid_width, columns), BF16),
            pltpu.VMEM((entries * rank, columns), BF16),
            pltpu.VMEM((rows, entries * rank), BF16),
            pltpu.SemaphoreType.DMA((4 + entries,)),
        ],
        compiler_params=TAIL_PARAMS,
        cost_estimate=pl.CostEstimate(
            flops=2 * (mid_width + entries * rank) * rows * columns,
            bytes_accessed=2 * (columns + entries * rank + 2 * rows) * columns,
            transcendentals=0,
        ),
    )(facts, places, base, sent, received, weight, *blocks, slot)


def last_kernel(facts, total, weight, x, out):
    part = out.shape[1]
    cut = pl.ds(pl.multiple_of(pl.program_id(0) * part, part), part)

    @pl.when(facts[0] != 0)
    def _():
        out[...] = (total[:, cut] + jnp.dot(x[...], weight[:, cut], preferred_element_type=F32)).astype(BF16)

    @pl.when(facts[0] == 0)
    def _():
        out[...] = total[:, cut].astype(BF16)


def add_last(facts, total, weight, x):
    rows, columns = total.shape
    part = min(columns, 512)
    return pl.pallas_call(
        last_kernel,
        out_shape=jax.ShapeDtypeStruct((rows, columns), BF16),
        grid=(columns // part,),
        in_specs=[pl.BlockSpec(memory_space=pltpu.SMEM), RESIDENT, RESIDENT, pl.BlockSpec(x.shape, lambda n: (0, 0))],
        out_specs=pl.BlockSpec((rows, part), lambda n: (0, n)),
        compiler_params=TAIL_PARAMS,
        cost_estimate=pl.CostEstimate(
            flops=2 * x.shape[1] * rows * columns, bytes_accessed=2 * rows * columns, transcendentals=0
        ),
    )(facts, total, weight, x)


def after(value, *earlier):
    return lax.optimization_barrier((value,) + earlier)[0]


def looked_up(table, ids):
    hit = ids[:, None] == jnp.arange(table.shape[0])[None, :]
    return jnp.sum(jnp.where(hit, table[None, :], 0), axis=1)


def local(
    attention_result,
    output_weight,
    adapter_down_weight,
    adapter_up_weight,
    adapter_page_row,
    requests,
    row_request_entry,
    ranks,
):
    n_dp = lax.axis_size("dp")
    n_tensor = lax.axis_size("tensor")
    me = lax.axis_index("tensor")
    rows, width = attention_result.shape
    holder_length, rank_part, _ = adapter_down_weight.shape
    rank, columns = adapter_up_weight.shape[1:]
    own_list = requests[0]
    entries = own_list.shape[0]
    one_hot = row_request_entry[:, None] == jnp.arange(entries)[None, :]
    row_rank = jnp.sum(jnp.where(one_hot, looked_up(ranks, own_list)[None, :], 0), axis=1)
    pages = looked_up(adapter_page_row, own_list)
    places = ((pages // holder_length) ^ lax.axis_index("dp")) * holder_length + pages % holder_length
    if n_tensor != 4 or n_dp != 4 or width % 512 or columns != width or rank_part % 16 or entries * rank_part > 256:
        return plain(
            attention_result, output_weight, adapter_down_weight, adapter_up_weight, places, one_hot, row_rank
        )


    def across(x, distance):
        return lax.ppermute(x, "dp", [(i, i ^ distance) for i in range(n_dp)])

    right = [(i, i + 1) for i in range(n_tensor - 1)]
    left = [(i + 1, i) for i in range(n_tensor - 1)]
    upper = me >= n_tensor // 2
    ends = me * (n_tensor - 1 - me) == 0
    slot = row_request_entry[:, None]
    farthest = jnp.where(upper, 0, n_tensor - 1)
    end = jnp.where(upper, n_tensor - 1, 0)
    source = jnp.where(upper, me - 2, me + 2)
    facts = jnp.stack([ends.astype(jnp.int32), farthest]).astype(jnp.int32)
    far_facts = jnp.stack([me, end, source, upper.astype(jnp.int32)]).astype(jnp.int32)
    near = plan_shards(me + jnp.array([0, -1, 1], jnp.int32), n_tensor)
    far = plan_shards(me + jnp.array([-2, 2], jnp.int32), n_tensor)

    right_1 = lax.ppermute(attention_result, "tensor", right)
    left_1 = lax.ppermute(attention_result, "tensor", left)
    far_down = across(adapter_down_weight, 2)
    far_up = across(adapter_up_weight, 2)
    near_down = across(adapter_down_weight, 1)

    right_1, left_1, places, slot, live, facts, far_facts, near, far = lax.optimization_barrier(
        (right_1, left_1, places, slot, row_rank[:, None], facts, far_facts, near, far)
    )
    right_2 = lax.ppermute(right_1, "tensor", right[1:])
    left_2 = lax.ppermute(left_1, "tensor", left[:-1])
    downs = (adapter_down_weight, near_down, far_down, across(after(far_down, right_1, left_1), 1))
    down, other_down = join_downs(places, far_facts[3:], downs, n_tensor)
    other_down = lax.ppermute(other_down, "tensor", [(0, 1), (3, 2)])

    base, low = add_shards(
        None, [attention_result, right_1, left_1], near, output_weight, down, slot, rank_part
    )
    other_low = lax.ppermute(low, "tensor", [(0, 1), (3, 2)])

    right_2, left_2 = lax.optimization_barrier((base, right_2, left_2))[1:]
    third = right[-1:] + left[:1]
    cuts = (0, width // 2, width // 4 * 3, width)

    def piece(i):
        cut = slice(cuts[i], cuts[i + 1])
        return jnp.where(upper, right_2[:, cut], left_2[:, cut])

    first_2 = piece(0)
    first_3 = lax.ppermute(first_2, "tensor", third)
    right_2, left_2, other_down, other_low = lax.optimization_barrier(
        (first_2, right_2, left_2, other_down, other_low)
    )[1:]
    pair = far_low(
        far_facts, right_1, right_2, left_1, left_2, down, other_down, slot, live, low, other_low
    )
    from_middle = lax.ppermute(pair, "tensor", [(1, 2), (2, 1)])
    base, = add_shards(after(base, pair), [right_2, left_2], far, output_weight)
    low = jnp.where(upper, jnp.concatenate([from_middle, pair], axis=1), jnp.concatenate([pair, from_middle], axis=1))
    second_2 = jnp.concatenate([piece(1), low], axis=1)
    second_3 = lax.ppermute(second_2, "tensor", third)
    right_2, left_2 = lax.optimization_barrier((second_2, right_2, left_2))[1:]
    last_3 = lax.ppermute(piece(2), "tensor", third)
    ups = (adapter_up_weight, across(after(adapter_up_weight, far_down), 1), far_up, across(after(far_up, first_2), 1))
    base = add_half(base, first_3, facts[0], facts[1], output_weight)
    total, rows_of = prepare(facts, places, base, second_2, second_3, output_weight, ups, slot)
    total, rows_of, last_3 = lax.optimization_barrier((total, rows_of, last_3))
    return add_last(facts, total, rows_of, last_3)


def gather_pages(block, n_dp):
    return [block] + [
        lax.ppermute(block, "dp", [(i, i ^ j) for i in range(n_dp)]) for j in range(1, n_dp)
    ]


def plain(x, output_weight, down_weight, up_weight, places, one_hot, row_rank):
    n_dp = lax.axis_size("dp")
    rows = x.shape[0]
    rank, columns = up_weight.shape[1:]
    entries = one_hot.shape[1]

    def requested(block):
        blocks = jnp.concatenate(gather_pages(block, n_dp), axis=0)
        return jnp.concatenate(
            [lax.dynamic_slice_in_dim(blocks, places[e], 1, 0) for e in range(entries)], axis=0
        )

    down, up = requested(down_weight), requested(up_weight)
    x = lax.all_gather(x, "tensor", axis=1, tiled=True)
    base = jnp.dot(x, output_weight, preferred_element_type=F32)
    low = jnp.einsum("rd,ekd->rek", x, down, preferred_element_type=F32)
    low = jnp.sum(jnp.where(one_hot[:, :, None], low, 0.0), axis=1).astype(BF16)
    low = lax.all_gather(low, "tensor", axis=1, tiled=True)
    low = jnp.where(jnp.arange(rank)[None, :] < row_rank[:, None], low, jnp.zeros_like(low))
    spread = jnp.where(one_hot[:, :, None], low[:, None, :], jnp.zeros((), BF16))
    term = jnp.dot(
        spread.reshape(rows, entries * rank), up.reshape(entries * rank, columns), preferred_element_type=F32
    )
    return (base + term).astype(BF16)


def solution(mesh):
    in_specs = (
        P(("groups", "dp"), "tensor"),
        P(None, "tensor"),
        P("dp", "tensor", None),
        P("dp", None, "tensor"),
        P("groups"),
        P(("groups", "dp"), None),
        P(("groups", "dp")),
        P(),
    )
    out_specs = P(("groups", "dp"), "tensor")
    return jax.shard_map(local, mesh=mesh, in_specs=in_specs, out_specs=out_specs, check_vma=False)
```

```python
import functools

import jax
import jax.numpy as jnp
from jax import lax
from jax.experimental import pallas as pl
from jax.experimental.pallas import tpu as pltpu
from jax.sharding import PartitionSpec as P

PARAMS = pltpu.CompilerParams(vmem_limit_bytes=48 * 2**20)
TAIL_PARAMS = pltpu.CompilerParams(vmem_limit_bytes=24 * 2**20)
F32 = jnp.float32
BF16 = jnp.bfloat16


def start_pages(places, blocks, length, targets, sems, rows_of):
    for e, target in enumerate(targets):
        for j, block in enumerate(blocks):

            @pl.when(places[e] // length == j)
            def _():
                pltpu.make_async_copy(rows_of(block.at[lax.rem(places[e], length)]), target, sems[e]).start()


def join_downs_kernel(places, upper, *refs):
    *blocks, out, other, held, sems = refs
    length, rank_part, _ = blocks[0].shape
    shards, slots, width = held.shape
    entries = places.shape[0]
    step = pl.program_id(0)

    def targets(t):
        return [held.at[t, pl.ds(e * rank_part, rank_part)] for e in range(entries)]

    @pl.when(step == 0)
    def _():
        for t in range(shards):
            semaphores = [sems.at[t, e] for e in range(entries)]
            start_pages(
                places, blocks, length, targets(t), semaphores, lambda page: page.at[:, pl.ds(t * width, width)]
            )
            held[t, entries * rank_part:] = jnp.zeros((slots - entries * rank_part, width), BF16)

    for t in range(shards):

        @pl.when(step == t)
        def _():
            for e, target in enumerate(targets(t)):
                source = blocks[0].at[0, :, pl.ds(t * width, width)]
                pltpu.make_async_copy(source, target, sems.at[t, e]).wait()
            joined = held[t].T
            out[...] = joined
            half = shards // 2

            @pl.when((upper[0] != 0) == (t < half))
            def _():
                other[:, t % half * width:(t % half + 1) * width] = held[t, :entries * rank_part]


def join_downs(places, upper, blocks, shards):
    entries = places.shape[0]
    _, rank_part, features = blocks[0].shape
    width, slots = features // shards, -(-entries * rank_part // 128) * 128
    return pl.pallas_call(
        join_downs_kernel,
        out_shape=[
            jax.ShapeDtypeStruct((features, slots), BF16),
            jax.ShapeDtypeStruct((entries * rank_part, features // 2), BF16),
        ],
        grid=(shards,),
        in_specs=[pl.BlockSpec(memory_space=pltpu.SMEM)] * 2
        + [pl.BlockSpec(memory_space=pltpu.HBM)] * len(blocks),
        out_specs=[
            pl.BlockSpec((width, slots), lambda t: (t, 0)),
            pl.BlockSpec((entries * rank_part, features // 2), lambda t: (0, 0)),
        ],
        scratch_shapes=[pltpu.VMEM((shards, slots, width), BF16), pltpu.SemaphoreType.DMA((shards, entries))],
        compiler_params=TAIL_PARAMS,
        cost_estimate=pl.CostEstimate(flops=0, bytes_accessed=4 * features * slots, transcendentals=0),
    )(places, upper, *blocks)


RESIDENT = pl.BlockSpec(memory_space=pltpu.VMEM)


def in_hbm(a):
    return pltpu.with_memory_space_constraint(a, pltpu.HBM)


IN_HBM = pl.BlockSpec(memory_space=pltpu.HBM)


def fold_entry(low, slot, rank_part):
    lane = lax.broadcasted_iota(jnp.int32, low.shape, 1)
    own = jnp.where(lane // rank_part == slot, low, 0.0)
    shape = (low.shape[1], rank_part)
    fold = lax.rem(lax.broadcasted_iota(jnp.int32, shape, 0), rank_part) == lax.broadcasted_iota(jnp.int32, shape, 1)
    return jnp.dot(own, fold.astype(F32), precision=lax.Precision.HIGHEST, preferred_element_type=F32)


def shards_kernel(with_low, start, valid, *refs):
    refs = list(refs)
    xs = [refs.pop(0) for _ in range(valid.shape[0])]
    weight = refs.pop(0)
    if with_low:
        down, slot, base, low, acc = refs
    else:
        base_in, base = refs
    step = pl.program_id(0)

    @pl.when(step == 0)
    def _():
        base[...] = jnp.zeros_like(base) if with_low else base_in[...]
        if with_low:
            acc[...] = jnp.zeros_like(acc)

    for i, x in enumerate(xs):

        @pl.when((step // 2 == i) & (valid[i] != 0))
        def _():
            part = min(base.shape[1], 512)
            for n in range(0, base.shape[1], part):
                base[:, n:n + part] += jnp.dot(x[...], weight[:, n:n + part], preferred_element_type=F32)
            if with_low:
                acc[...] += jnp.dot(x[...], down[...], preferred_element_type=F32)

    if with_low:

        @pl.when(step == pl.num_programs(0) - 1)
        def _():
            low[...] = fold_entry(acc[...], slot[...], low.shape[1])


def plan_shards(source, n_tensor):
    there = (source >= 0) & (source < n_tensor)
    start = 2 * jnp.clip(source, 0, n_tensor - 1)[:, None] + jnp.arange(2)[None, :]
    idle = jnp.concatenate([start[1:2, :1], start[:-1, 1:]], axis=0)
    start = jnp.where(there[:, None], start, idle).reshape(-1).astype(jnp.int32)
    return start, there.astype(jnp.int32)


def add_shards(base, xs, plan, weight, down=None, slot=None, rank_part=0):
    rows, width = xs[0].shape
    half = width // 2
    columns = weight.shape[1]
    steps = 2 * len(xs)

    def whole(a):
        return pl.BlockSpec((rows, a), lambda s, *_: (0, 0))

    def walked(a):
        return pl.BlockSpec((half, a.shape[1]), lambda s, start, valid: (start[s], 0))

    in_specs = [
        pl.BlockSpec((rows, half), lambda s, *_, i=i: (0, jnp.clip(s - 2 * i, 0, 1))) for i in range(len(xs))
    ] + [walked(weight)]
    out_shape = [jax.ShapeDtypeStruct((rows, columns), F32)]
    scratch = []
    slots = 0
    if base is None:
        slots = down.shape[1]
        in_specs += [walked(down), whole(1)]
        out_shape += [jax.ShapeDtypeStruct((rows, rank_part), F32)]
        scratch = [pltpu.VMEM((rows, slots), F32)]
        rest = (down, slot)
    else:
        in_specs += [whole(columns)]
        rest = (base,)
    return pl.pallas_call(
        functools.partial(shards_kernel, base is None),
        out_shape=out_shape,
        grid_spec=pltpu.PrefetchScalarGridSpec(
            num_scalar_prefetch=2,
            grid=(steps,),
            in_specs=in_specs,
            out_specs=[whole(a.shape[1]) for a in out_shape],
            scratch_shapes=scratch,
        ),
        compiler_params=PARAMS,
        cost_estimate=pl.CostEstimate(
            flops=2 * steps * half * rows * (columns + slots),
            bytes_accessed=2 * steps * half * (rows + columns + slots) + 8 * rows * columns,
            transcendentals=0,
        ),
    )(*plan, *xs, weight, *rest)


def half_kernel(start, valid, x, weight, base_in, base):
    step = pl.program_id(0)

    @pl.when(step == 0)
    def _():
        base[...] = base_in[...]

    @pl.when(valid[0] != 0)
    def _():
        part = min(base.shape[1], 512)
        for n in range(0, base.shape[1], part):
            base[:, n:n + part] += jnp.dot(x[...], weight[:, n:n + part], preferred_element_type=F32)


def add_half(base, x, valid, source, weight):
    rows, half = x.shape
    columns = weight.shape[1]
    step = half // 2
    whole = pl.BlockSpec((rows, columns), lambda s, *_: (0, 0))
    return pl.pallas_call(
        half_kernel,
        out_shape=jax.ShapeDtypeStruct((rows, columns), F32),
        grid_spec=pltpu.PrefetchScalarGridSpec(
            num_scalar_prefetch=2,
            grid=(2,),
            in_specs=[
                pl.BlockSpec((rows, step), lambda s, *_: (0, s)),
                pl.BlockSpec((step, columns), lambda s, source, valid: (source[0] * 4 + s, 0)),
                whole,
            ],
            out_specs=whole,
        ),
        compiler_params=PARAMS,
        cost_estimate=pl.CostEstimate(
            flops=2 * half * rows * columns,
            bytes_accessed=2 * half * (rows + columns) + 8 * rows * columns,
            transcendentals=0,
        ),
    )(source[None], valid[None], x, weight, base)


def far_low_kernel(
    facts, left_1, left_2, right_1, right_2, down, other_down, slot, row_rank, low, other_low,
    out, near_x, far_x, rows_of, other_rows, sems
):
    me, end, source, upper = facts[0], facts[1], facts[2], facts[3]
    width = far_x.shape[1]
    rank_part = low.shape[1]
    start = pl.multiple_of(source * width, width)

    @pl.when(upper != 0)
    def _():
        pltpu.make_async_copy(left_2, far_x, sems.at[0]).start()
        pltpu.make_async_copy(left_1, near_x, sems.at[1]).start()

    @pl.when(upper == 0)
    def _():
        pltpu.make_async_copy(right_2, far_x, sems.at[0]).start()
        pltpu.make_async_copy(right_1, near_x, sems.at[1]).start()

    copies = [
        pltpu.make_async_copy(down.at[pl.ds(start, width)], rows_of, sems.at[2]),
        pltpu.make_async_copy(other_down, other_rows, sems.at[3]),
    ]
    for copy in copies:
        copy.start()
    pltpu.make_async_copy(left_2, far_x, sems.at[0]).wait()

    def finished(total, sums, place):
        sums = total[...] + fold_entry(sums, slot[...], rank_part)
        k = lax.broadcasted_iota(jnp.int32, sums.shape, 1) + place * rank_part
        return jnp.where(k < row_rank[...], sums, 0.0)

    copies[0].wait()
    own = finished(low, jnp.dot(far_x[...], rows_of[...], preferred_element_type=F32), me)
    pltpu.make_async_copy(left_1, near_x, sems.at[1]).wait()
    copies[1].wait()
    sums = jnp.zeros((far_x.shape[0], other_rows.shape[0]), F32)
    for x, place in ((far_x, 1 - upper), (near_x, upper)):
        rows = other_rows[:, pl.ds(pl.multiple_of(place * width, width), width)]
        sums += lax.dot_general(x[...], rows, (((1,), (1,)), ((), ())), preferred_element_type=F32)
    other = finished(other_low, sums, end)
    at_left = jnp.concatenate([other, own], axis=1)
    at_right = jnp.concatenate([own, other], axis=1)
    out[...] = jnp.where(upper != 0, at_right, at_left).astype(BF16)


def far_low(facts, left_1, left_2, right_1, right_2, down, other_down, slot, row_rank, low, other_low):
    rows, width = left_1.shape
    slots = down.shape[1]
    return pl.pallas_call(
        far_low_kernel,
        out_shape=jax.ShapeDtypeStruct((rows, 2 * low.shape[1]), BF16),
        in_specs=[pl.BlockSpec(memory_space=pltpu.SMEM)] + [IN_HBM] * 6 + [RESIDENT] * 4,
        out_specs=RESIDENT,
        scratch_shapes=[
            pltpu.VMEM((rows, width), BF16),
            pltpu.VMEM((rows, width), BF16),
            pltpu.VMEM((width, slots), BF16),
            pltpu.VMEM(other_down.shape, BF16),
            pltpu.SemaphoreType.DMA((4,)),
        ],
        compiler_params=TAIL_PARAMS,
        cost_estimate=pl.CostEstimate(
            flops=6 * width * rows * slots, bytes_accessed=2 * width * (2 * rows + 3 * slots), transcendentals=0
        ),
    )(facts, left_1, left_2, right_1, right_2, in_hbm(down), other_down, slot, row_rank, low, other_low)


def prepare_kernel(facts, places, base, sent, received, weight, *refs):
    *blocks, slot, total, last_rows, mid, mid_rows, up, spread, sems = refs
    mid_width, last_width = mid_rows.shape[0], last_rows.shape[0]
    width = mid_width + last_width
    length, rank, _ = blocks[0].shape
    count = up.shape[0] // rank
    which, start = facts[0], facts[1] * 2 * width + width
    part = min(total.shape[1], 512)

    def rows_at(first, length):
        return weight.at[pl.ds(pl.multiple_of(start + first, length), length)]

    to_total = pltpu.make_async_copy(base, total, sems.at[0])
    to_mid_rows = pltpu.make_async_copy(rows_at(0, mid_width), mid_rows, sems.at[1])
    to_last = pltpu.make_async_copy(rows_at(mid_width, last_width), last_rows, sems.at[2])
    pages = [up.at[pl.ds(e * rank, rank)] for e in range(count)]
    page_sems = [sems.at[4 + e] for e in range(count)]

    @pl.when(which == 0)
    def _():
        pltpu.make_async_copy(sent, mid, sems.at[3]).start()

    @pl.when(which != 0)
    def _():
        pltpu.make_async_copy(received, mid, sems.at[3]).start()

    to_total.start()
    start_pages(places, blocks, length, pages, page_sems, lambda page: page)

    @pl.when(which != 0)
    def _():
        to_mid_rows.start()
        to_last.start()

    pltpu.make_async_copy(sent, mid, sems.at[3]).wait()
    for e in range(count):
        spread[:, e * rank:(e + 1) * rank] = jnp.where(
            slot[...] == e, mid[:, mid_width:].astype(F32), 0.0
        ).astype(BF16)
    for page, sem in zip(pages, page_sems):
        pltpu.make_async_copy(blocks[0].at[0], page, sem).wait()
    to_total.wait()
    for n in range(0, total.shape[1], part):
        cut = slice(n, n + part)
        total[:, cut] += jnp.dot(spread[...], up[:, cut], preferred_element_type=F32)

    @pl.when(which != 0)
    def _():
        to_mid_rows.wait()
        for n in range(0, total.shape[1], part):
            cut = slice(n, n + part)
            total[:, cut] += jnp.dot(mid[:, :mid_width], mid_rows[:, cut], preferred_element_type=F32)
        to_last.wait()


def prepare(facts, places, base, sent, received, weight, blocks, slot):
    rows, columns = base.shape
    rank = blocks[0].shape[1]
    entries = places.shape[0]
    mid_width = sent.shape[1] - rank
    last_width = mid_width
    return pl.pallas_call(
        prepare_kernel,
        out_shape=[pltpu.VMEM((rows, columns), F32), pltpu.VMEM((last_width, columns), BF16)],
        in_specs=[pl.BlockSpec(memory_space=pltpu.SMEM)] * 2 + [IN_HBM] * (4 + len(blocks)) + [RESIDENT],
        out_specs=[RESIDENT] * 2,
        scratch_shapes=[
            pltpu.VMEM(sent.shape, BF16),
            pltpu.VMEM((mid_width, columns), BF16),
            pltpu.VMEM((entries * rank, columns), BF16),
            pltpu.VMEM((rows, entries * rank), BF16),
            pltpu.SemaphoreType.DMA((4 + entries,)),
        ],
        compiler_params=TAIL_PARAMS,
        cost_estimate=pl.CostEstimate(
            flops=2 * (mid_width + entries * rank) * rows * columns,
            bytes_accessed=2 * (columns + entries * rank + 2 * rows) * columns,
            transcendentals=0,
        ),
    )(facts, places, base, sent, received, weight, in_hbm(blocks[0]), *blocks[1:], slot)


def last_kernel(facts, total, weight, x, out):
    part = out.shape[1]
    cut = pl.ds(pl.multiple_of(pl.program_id(0) * part, part), part)

    @pl.when(facts[0] != 0)
    def _():
        out[...] = (total[:, cut] + jnp.dot(x[...], weight[:, cut], preferred_element_type=F32)).astype(BF16)

    @pl.when(facts[0] == 0)
    def _():
        out[...] = total[:, cut].astype(BF16)


def add_last(facts, total, weight, x):
    rows, columns = total.shape
    part = min(columns, 512)
    return pl.pallas_call(
        last_kernel,
        out_shape=jax.ShapeDtypeStruct((rows, columns), BF16),
        grid=(columns // part,),
        in_specs=[pl.BlockSpec(memory_space=pltpu.SMEM), RESIDENT, RESIDENT, pl.BlockSpec(x.shape, lambda n: (0, 0))],
        out_specs=pl.BlockSpec((rows, part), lambda n: (0, n)),
        compiler_params=TAIL_PARAMS,
        cost_estimate=pl.CostEstimate(
            flops=2 * x.shape[1] * rows * columns, bytes_accessed=2 * rows * columns, transcendentals=0
        ),
    )(facts, total, weight, x)


def after(value, *earlier):
    return lax.optimization_barrier((value,) + earlier)[0]


def looked_up(table, ids):
    hit = ids[:, None] == jnp.arange(table.shape[0])[None, :]
    return jnp.sum(jnp.where(hit, table[None, :], 0), axis=1)


def local(
    attention_result,
    output_weight,
    adapter_down_weight,
    adapter_up_weight,
    adapter_page_row,
    requests,
    row_request_entry,
    ranks,
):
    n_dp = lax.axis_size("dp")
    n_tensor = lax.axis_size("tensor")
    me = lax.axis_index("tensor")
    rows, width = attention_result.shape
    holder_length, rank_part, _ = adapter_down_weight.shape
    rank, columns = adapter_up_weight.shape[1:]
    own_list = requests[0]
    entries = own_list.shape[0]
    one_hot = row_request_entry[:, None] == jnp.arange(entries)[None, :]
    row_rank = jnp.sum(jnp.where(one_hot, looked_up(ranks, own_list)[None, :], 0), axis=1)
    pages = looked_up(adapter_page_row, own_list)
    places = ((pages // holder_length) ^ lax.axis_index("dp")) * holder_length + pages % holder_length
    if n_tensor != 4 or n_dp != 4 or width % 512 or columns != width or rank_part % 16 or entries * rank_part > 256:
        return plain(
            attention_result, output_weight, adapter_down_weight, adapter_up_weight, places, one_hot, row_rank
        )


    def across(x, distance):
        return lax.ppermute(x, "dp", [(i, i ^ distance) for i in range(n_dp)])

    right = [(i, i + 1) for i in range(n_tensor - 1)]
    left = [(i + 1, i) for i in range(n_tensor - 1)]
    upper = me >= n_tensor // 2
    ends = me * (n_tensor - 1 - me) == 0
    slot = row_request_entry[:, None]
    farthest = jnp.where(upper, 0, n_tensor - 1)
    end = jnp.where(upper, n_tensor - 1, 0)
    source = jnp.where(upper, me - 2, me + 2)
    facts = jnp.stack([ends.astype(jnp.int32), farthest]).astype(jnp.int32)
    far_facts = jnp.stack([me, end, source, upper.astype(jnp.int32)]).astype(jnp.int32)
    near = plan_shards(me + jnp.array([0, -1, 1], jnp.int32), n_tensor)
    far = plan_shards(me + jnp.array([-2, 2], jnp.int32), n_tensor)

    right_1 = lax.ppermute(attention_result, "tensor", right)
    left_1 = lax.ppermute(attention_result, "tensor", left)
    far_down = across(adapter_down_weight, 2)
    far_up = across(adapter_up_weight, 2)
    near_down = across(adapter_down_weight, 1)

    right_1, left_1, places, slot, live, facts, far_facts, near, far = lax.optimization_barrier(
        (right_1, left_1, places, slot, row_rank[:, None], facts, far_facts, near, far)
    )
    right_2 = lax.ppermute(right_1, "tensor", right[1:])
    left_2 = lax.ppermute(left_1, "tensor", left[:-1])
    downs = (adapter_down_weight, near_down, far_down, across(after(far_down, right_1, left_1), 1))
    down, other_down = join_downs(places, far_facts[3:], downs, n_tensor)
    other_down = lax.ppermute(other_down, "tensor", [(0, 1), (3, 2)])

    base, low = add_shards(
        None, [attention_result, right_1, left_1], near, output_weight, down, slot, rank_part
    )
    other_low = lax.ppermute(low, "tensor", [(0, 1), (3, 2)])

    right_2, left_2 = lax.optimization_barrier((base, right_2, left_2))[1:]
    third = right[-1:] + left[:1]
    cuts = (0, width // 2, width // 4 * 3, width)

    def piece(i):
        cut = slice(cuts[i], cuts[i + 1])
        return jnp.where(upper, right_2[:, cut], left_2[:, cut])

    first_2 = piece(0)
    first_3 = lax.ppermute(first_2, "tensor", third)
    right_2, left_2, other_down, other_low = lax.optimization_barrier(
        (first_2, right_2, left_2, other_down, other_low)
    )[1:]
    pair = far_low(
        far_facts, right_1, right_2, left_1, left_2, down, other_down, slot, live, low, other_low
    )
    from_middle = lax.ppermute(pair, "tensor", [(1, 2), (2, 1)])
    base, = add_shards(after(base, pair), [right_2, left_2], far, output_weight)
    low = jnp.where(upper, jnp.concatenate([from_middle, pair], axis=1), jnp.concatenate([pair, from_middle], axis=1))
    second_2 = jnp.concatenate([piece(1), low], axis=1)
    second_3 = lax.ppermute(second_2, "tensor", third)
    right_2, left_2 = lax.optimization_barrier((second_2, right_2, left_2))[1:]
    last_3 = lax.ppermute(piece(2), "tensor", third)
    ups = (adapter_up_weight, across(after(adapter_up_weight, far_down), 1), far_up, across(after(far_up, first_2), 1))
    base = add_half(base, first_3, facts[0], facts[1], output_weight)
    total, rows_of = prepare(facts, places, base, second_2, second_3, output_weight, ups, slot)
    total, rows_of, last_3 = lax.optimization_barrier((total, rows_of, last_3))
    return add_last(facts, total, rows_of, last_3)


def gather_pages(block, n_dp):
    return [block] + [
        lax.ppermute(block, "dp", [(i, i ^ j) for i in range(n_dp)]) for j in range(1, n_dp)
    ]


def plain(x, output_weight, down_weight, up_weight, places, one_hot, row_rank):
    n_dp = lax.axis_size("dp")
    rows = x.shape[0]
    rank, columns = up_weight.shape[1:]
    entries = one_hot.shape[1]

    def requested(block):
        blocks = jnp.concatenate(gather_pages(block, n_dp), axis=0)
        return jnp.concatenate(
            [lax.dynamic_slice_in_dim(blocks, places[e], 1, 0) for e in range(entries)], axis=0
        )

    down, up = requested(down_weight), requested(up_weight)
    x = lax.all_gather(x, "tensor", axis=1, tiled=True)
    base = jnp.dot(x, output_weight, preferred_element_type=F32)
    low = jnp.einsum("rd,ekd->rek", x, down, preferred_element_type=F32)
    low = jnp.sum(jnp.where(one_hot[:, :, None], low, 0.0), axis=1).astype(BF16)
    low = lax.all_gather(low, "tensor", axis=1, tiled=True)
    low = jnp.where(jnp.arange(rank)[None, :] < row_rank[:, None], low, jnp.zeros_like(low))
    spread = jnp.where(one_hot[:, :, None], low[:, None, :], jnp.zeros((), BF16))
    term = jnp.dot(
        spread.reshape(rows, entries * rank), up.reshape(entries * rank, columns), preferred_element_type=F32
    )
    return (base + term).astype(BF16)


def solution(mesh):
    in_specs = (
        P(("groups", "dp"), "tensor"),
        P(None, "tensor"),
        P("dp", "tensor", None),
        P("dp", None, "tensor"),
        P("groups"),
        P(("groups", "dp"), None),
        P(("groups", "dp")),
        P(),
    )
    out_specs = P(("groups", "dp"), "tensor")
    return jax.shard_map(local, mesh=mesh, in_specs=in_specs, out_specs=out_specs, check_vma=False)
```

```python
import functools

import jax
import jax.numpy as jnp
from jax import lax
from jax.experimental import pallas as pl
from jax.experimental.pallas import tpu as pltpu
from jax.sharding import PartitionSpec as P

PARAMS = pltpu.CompilerParams(vmem_limit_bytes=48 * 2**20)
TAIL_PARAMS = pltpu.CompilerParams(vmem_limit_bytes=24 * 2**20)
F32 = jnp.float32
BF16 = jnp.bfloat16


def start_pages(places, blocks, length, targets, sems, rows_of):
    for e, target in enumerate(targets):
        for j, block in enumerate(blocks):

            @pl.when(places[e] // length == j)
            def _():
                pltpu.make_async_copy(rows_of(block.at[lax.rem(places[e], length)]), target, sems[e]).start()


def join_downs_kernel(places, upper, *refs):
    *blocks, out, other, held, sems = refs
    length, rank_part, _ = blocks[0].shape
    shards, slots, width = held.shape
    entries = places.shape[0]
    step = pl.program_id(0)

    def targets(t):
        return [held.at[t, pl.ds(e * rank_part, rank_part)] for e in range(entries)]

    @pl.when(step == 0)
    def _():
        for t in range(shards):
            semaphores = [sems.at[t, e] for e in range(entries)]
            start_pages(
                places, blocks, length, targets(t), semaphores, lambda page: page.at[:, pl.ds(t * width, width)]
            )
            held[t, entries * rank_part:] = jnp.zeros((slots - entries * rank_part, width), BF16)

    for t in range(shards):

        @pl.when(step == t)
        def _():
            for e, target in enumerate(targets(t)):
                source = blocks[0].at[0, :, pl.ds(t * width, width)]
                pltpu.make_async_copy(source, target, sems.at[t, e]).wait()
            joined = held[t].T
            out[...] = joined
            half = shards // 2

            @pl.when((upper[0] != 0) == (t < half))
            def _():
                other[:, t % half * width:(t % half + 1) * width] = held[t, :entries * rank_part]


def join_downs(places, upper, blocks, shards):
    entries = places.shape[0]
    _, rank_part, features = blocks[0].shape
    width, slots = features // shards, -(-entries * rank_part // 128) * 128
    return pl.pallas_call(
        join_downs_kernel,
        out_shape=[
            jax.ShapeDtypeStruct((features, slots), BF16),
            jax.ShapeDtypeStruct((entries * rank_part, features // 2), BF16),
        ],
        grid=(shards,),
        in_specs=[pl.BlockSpec(memory_space=pltpu.SMEM)] * 2
        + [pl.BlockSpec(memory_space=pltpu.HBM)] * len(blocks),
        out_specs=[
            pl.BlockSpec((width, slots), lambda t: (t, 0)),
            pl.BlockSpec((entries * rank_part, features // 2), lambda t: (0, 0)),
        ],
        scratch_shapes=[pltpu.VMEM((shards, slots, width), BF16), pltpu.SemaphoreType.DMA((shards, entries))],
        compiler_params=TAIL_PARAMS,
        cost_estimate=pl.CostEstimate(flops=0, bytes_accessed=4 * features * slots, transcendentals=0),
    )(places, upper, *blocks)


RESIDENT = pl.BlockSpec(memory_space=pltpu.VMEM)


def in_hbm(a):
    return pltpu.with_memory_space_constraint(a, pltpu.HBM)


IN_HBM = pl.BlockSpec(memory_space=pltpu.HBM)


def fold_entry(low, slot, rank_part):
    lane = lax.broadcasted_iota(jnp.int32, low.shape, 1)
    own = jnp.where(lane // rank_part == slot, low, 0.0)
    shape = (low.shape[1], rank_part)
    fold = lax.rem(lax.broadcasted_iota(jnp.int32, shape, 0), rank_part) == lax.broadcasted_iota(jnp.int32, shape, 1)
    return jnp.dot(own, fold.astype(F32), precision=lax.Precision.HIGHEST, preferred_element_type=F32)


def shards_kernel(with_low, start, valid, *refs):
    refs = list(refs)
    xs = [refs.pop(0) for _ in range(valid.shape[0])]
    weight = refs.pop(0)
    if with_low:
        down, slot, base, low, acc = refs
    else:
        base_in, base = refs
    step = pl.program_id(0)

    @pl.when(step == 0)
    def _():
        base[...] = jnp.zeros_like(base) if with_low else base_in[...]
        if with_low:
            acc[...] = jnp.zeros_like(acc)

    for i, x in enumerate(xs):

        @pl.when((step // 2 == i) & (valid[i] != 0))
        def _():
            part = min(base.shape[1], 512)
            for n in range(0, base.shape[1], part):
                base[:, n:n + part] += jnp.dot(x[...], weight[:, n:n + part], preferred_element_type=F32)
            if with_low:
                acc[...] += jnp.dot(x[...], down[...], preferred_element_type=F32)

    if with_low:

        @pl.when(step == pl.num_programs(0) - 1)
        def _():
            low[...] = fold_entry(acc[...], slot[...], low.shape[1])


def plan_shards(source, n_tensor):
    there = (source >= 0) & (source < n_tensor)
    start = 2 * jnp.clip(source, 0, n_tensor - 1)[:, None] + jnp.arange(2)[None, :]
    idle = jnp.concatenate([start[1:2, :1], start[:-1, 1:]], axis=0)
    start = jnp.where(there[:, None], start, idle).reshape(-1).astype(jnp.int32)
    return start, there.astype(jnp.int32)


def add_shards(base, xs, plan, weight, down=None, slot=None, rank_part=0):
    rows, width = xs[0].shape
    half = width // 2
    columns = weight.shape[1]
    steps = 2 * len(xs)

    def whole(a):
        return pl.BlockSpec((rows, a), lambda s, *_: (0, 0))

    def walked(a):
        return pl.BlockSpec((half, a.shape[1]), lambda s, start, valid: (start[s], 0))

    in_specs = [
        pl.BlockSpec((rows, half), lambda s, *_, i=i: (0, jnp.clip(s - 2 * i, 0, 1))) for i in range(len(xs))
    ] + [walked(weight)]
    out_shape = [jax.ShapeDtypeStruct((rows, columns), F32)]
    scratch = []
    slots = 0
    if base is None:
        slots = down.shape[1]
        in_specs += [walked(down), whole(1)]
        out_shape += [jax.ShapeDtypeStruct((rows, rank_part), F32)]
        scratch = [pltpu.VMEM((rows, slots), F32)]
        rest = (down, slot)
    else:
        in_specs += [whole(columns)]
        rest = (base,)
    return pl.pallas_call(
        functools.partial(shards_kernel, base is None),
        out_shape=out_shape,
        grid_spec=pltpu.PrefetchScalarGridSpec(
            num_scalar_prefetch=2,
            grid=(steps,),
            in_specs=in_specs,
            out_specs=[whole(a.shape[1]) for a in out_shape],
            scratch_shapes=scratch,
        ),
        compiler_params=PARAMS,
        cost_estimate=pl.CostEstimate(
            flops=2 * steps * half * rows * (columns + slots),
            bytes_accessed=2 * steps * half * (rows + columns + slots) + 8 * rows * columns,
            transcendentals=0,
        ),
    )(*plan, *xs, weight, *rest)


def half_kernel(start, valid, x, weight, base_in, base):
    step = pl.program_id(0)

    @pl.when(step == 0)
    def _():
        base[...] = base_in[...]

    @pl.when(valid[0] != 0)
    def _():
        part = min(base.shape[1], 512)
        for n in range(0, base.shape[1], part):
            base[:, n:n + part] += jnp.dot(x[...], weight[:, n:n + part], preferred_element_type=F32)


def add_half(base, x, valid, source, weight):
    rows, half = x.shape
    columns = weight.shape[1]
    step = half // 2
    whole = pl.BlockSpec((rows, columns), lambda s, *_: (0, 0))
    return pl.pallas_call(
        half_kernel,
        out_shape=jax.ShapeDtypeStruct((rows, columns), F32),
        grid_spec=pltpu.PrefetchScalarGridSpec(
            num_scalar_prefetch=2,
            grid=(2,),
            in_specs=[
                pl.BlockSpec((rows, step), lambda s, *_: (0, s)),
                pl.BlockSpec((step, columns), lambda s, source, valid: (source[0] * 4 + s, 0)),
                whole,
            ],
            out_specs=whole,
        ),
        compiler_params=PARAMS,
        cost_estimate=pl.CostEstimate(
            flops=2 * half * rows * columns,
            bytes_accessed=2 * half * (rows + columns) + 8 * rows * columns,
            transcendentals=0,
        ),
    )(source, valid, x, weight, base)


def far_low_kernel(
    facts, left_1, left_2, right_1, right_2, down, other_down, slot, row_rank, low, other_low,
    out, near_x, far_x, rows_of, other_rows, sems
):
    me, end, source, upper = facts[0], facts[1], facts[2], facts[3]
    width = far_x.shape[1]
    rank_part = low.shape[1]
    start = pl.multiple_of(source * width, width)

    @pl.when(upper != 0)
    def _():
        pltpu.make_async_copy(left_2, far_x, sems.at[0]).start()
        pltpu.make_async_copy(left_1, near_x, sems.at[1]).start()

    @pl.when(upper == 0)
    def _():
        pltpu.make_async_copy(right_2, far_x, sems.at[0]).start()
        pltpu.make_async_copy(right_1, near_x, sems.at[1]).start()

    copies = [
        pltpu.make_async_copy(down.at[pl.ds(start, width)], rows_of, sems.at[2]),
        pltpu.make_async_copy(other_down, other_rows, sems.at[3]),
    ]
    for copy in copies:
        copy.start()
    pltpu.make_async_copy(left_2, far_x, sems.at[0]).wait()

    def finished(total, sums, place):
        sums = total[...] + fold_entry(sums, slot[...], rank_part)
        k = lax.broadcasted_iota(jnp.int32, sums.shape, 1) + place * rank_part
        return jnp.where(k < row_rank[...], sums, 0.0)

    copies[0].wait()
    own = finished(low, jnp.dot(far_x[...], rows_of[...], preferred_element_type=F32), me)
    pltpu.make_async_copy(left_1, near_x, sems.at[1]).wait()
    copies[1].wait()
    sums = jnp.zeros((far_x.shape[0], other_rows.shape[0]), F32)
    for x, place in ((far_x, 1 - upper), (near_x, upper)):
        rows = other_rows[:, pl.ds(pl.multiple_of(place * width, width), width)]
        sums += lax.dot_general(x[...], rows, (((1,), (1,)), ((), ())), preferred_element_type=F32)
    other = finished(other_low, sums, end)
    at_left = jnp.concatenate([other, own], axis=1)
    at_right = jnp.concatenate([own, other], axis=1)
    out[...] = jnp.where(upper != 0, at_right, at_left).astype(BF16)


def far_low(facts, left_1, left_2, right_1, right_2, down, other_down, slot, row_rank, low, other_low):
    rows, width = left_1.shape
    slots = down.shape[1]
    return pl.pallas_call(
        far_low_kernel,
        out_shape=jax.ShapeDtypeStruct((rows, 2 * low.shape[1]), BF16),
        in_specs=[pl.BlockSpec(memory_space=pltpu.SMEM)] + [IN_HBM] * 6 + [RESIDENT] * 4,
        out_specs=RESIDENT,
        scratch_shapes=[
            pltpu.VMEM((rows, width), BF16),
            pltpu.VMEM((rows, width), BF16),
            pltpu.VMEM((width, slots), BF16),
            pltpu.VMEM(other_down.shape, BF16),
            pltpu.SemaphoreType.DMA((4,)),
        ],
        compiler_params=TAIL_PARAMS,
        cost_estimate=pl.CostEstimate(
            flops=6 * width * rows * slots, bytes_accessed=2 * width * (2 * rows + 3 * slots), transcendentals=0
        ),
    )(facts, left_1, left_2, right_1, right_2, in_hbm(down), other_down, slot, row_rank, low, other_low)


def prepare_kernel(facts, places, base, sent, received, weight, *refs):
    *blocks, slot, total, last_rows, mid, mid_rows, up, spread, sems = refs
    mid_width, last_width = mid_rows.shape[0], last_rows.shape[0]
    width = mid_width + last_width
    length, rank, _ = blocks[0].shape
    count = up.shape[0] // rank
    which, start = facts[0], facts[1] * 2 * width + width
    part = min(total.shape[1], 512)

    def rows_at(first, length):
        return weight.at[pl.ds(pl.multiple_of(start + first, length), length)]

    to_total = pltpu.make_async_copy(base, total, sems.at[0])
    to_mid_rows = pltpu.make_async_copy(rows_at(0, mid_width), mid_rows, sems.at[1])
    to_last = pltpu.make_async_copy(rows_at(mid_width, last_width), last_rows, sems.at[2])
    pages = [up.at[pl.ds(e * rank, rank)] for e in range(count)]
    page_sems = [sems.at[4 + e] for e in range(count)]

    @pl.when(which == 0)
    def _():
        pltpu.make_async_copy(sent, mid, sems.at[3]).start()

    @pl.when(which != 0)
    def _():
        pltpu.make_async_copy(received, mid, sems.at[3]).start()

    to_total.start()
    start_pages(places, blocks, length, pages, page_sems, lambda page: page)

    @pl.when(which != 0)
    def _():
        to_mid_rows.start()
        to_last.start()

    pltpu.make_async_copy(sent, mid, sems.at[3]).wait()
    for e in range(count):
        spread[:, e * rank:(e + 1) * rank] = jnp.where(
            slot[...] == e, mid[:, mid_width:].astype(F32), 0.0
        ).astype(BF16)
    for page, sem in zip(pages, page_sems):
        pltpu.make_async_copy(blocks[0].at[0], page, sem).wait()
    to_total.wait()
    for n in range(0, total.shape[1], part):
        cut = slice(n, n + part)
        total[:, cut] += jnp.dot(spread[...], up[:, cut], preferred_element_type=F32)

    @pl.when(which != 0)
    def _():
        to_mid_rows.wait()
        for n in range(0, total.shape[1], part):
            cut = slice(n, n + part)
            total[:, cut] += jnp.dot(mid[:, :mid_width], mid_rows[:, cut], preferred_element_type=F32)
        to_last.wait()


def prepare(facts, places, base, sent, received, weight, blocks, slot):
    rows, columns = base.shape
    rank = blocks[0].shape[1]
    entries = places.shape[0]
    mid_width = sent.shape[1] - rank
    last_width = mid_width
    return pl.pallas_call(
        prepare_kernel,
        out_shape=[pltpu.VMEM((rows, columns), F32), pltpu.VMEM((last_width, columns), BF16)],
        in_specs=[pl.BlockSpec(memory_space=pltpu.SMEM)] * 2 + [IN_HBM] * (4 + len(blocks)) + [RESIDENT],
        out_specs=[RESIDENT] * 2,
        scratch_shapes=[
            pltpu.VMEM(sent.shape, BF16),
            pltpu.VMEM((mid_width, columns), BF16),
            pltpu.VMEM((entries * rank, columns), BF16),
            pltpu.VMEM((rows, entries * rank), BF16),
            pltpu.SemaphoreType.DMA((4 + entries,)),
        ],
        compiler_params=TAIL_PARAMS,
        cost_estimate=pl.CostEstimate(
            flops=2 * (mid_width + entries * rank) * rows * columns,
            bytes_accessed=2 * (columns + entries * rank + 2 * rows) * columns,
            transcendentals=0,
        ),
    )(facts, places, base, sent, received, weight, in_hbm(blocks[0]), *blocks[1:], slot)


def last_kernel(facts, total, weight, x, out):
    part = out.shape[1]
    cut = pl.ds(pl.multiple_of(pl.program_id(0) * part, part), part)

    @pl.when(facts[0] != 0)
    def _():
        out[...] = (total[:, cut] + jnp.dot(x[...], weight[:, cut], preferred_element_type=F32)).astype(BF16)

    @pl.when(facts[0] == 0)
    def _():
        out[...] = total[:, cut].astype(BF16)


def add_last(facts, total, weight, x):
    rows, columns = total.shape
    part = min(columns, 512)
    return pl.pallas_call(
        last_kernel,
        out_shape=jax.ShapeDtypeStruct((rows, columns), BF16),
        grid=(columns // part,),
        in_specs=[pl.BlockSpec(memory_space=pltpu.SMEM), RESIDENT, RESIDENT, pl.BlockSpec(x.shape, lambda n: (0, 0))],
        out_specs=pl.BlockSpec((rows, part), lambda n: (0, n)),
        compiler_params=TAIL_PARAMS,
        cost_estimate=pl.CostEstimate(
            flops=2 * x.shape[1] * rows * columns, bytes_accessed=2 * rows * columns, transcendentals=0
        ),
    )(facts, total, weight, x)


def after(value, *earlier):
    return lax.optimization_barrier((value,) + earlier)[0]


def looked_up(table, ids):
    hit = ids[:, None] == jnp.arange(table.shape[0])[None, :]
    return jnp.sum(jnp.where(hit, table[None, :], 0), axis=1)


def local(
    attention_result,
    output_weight,
    adapter_down_weight,
    adapter_up_weight,
    adapter_page_row,
    requests,
    row_request_entry,
    ranks,
):
    n_dp = lax.axis_size("dp")
    n_tensor = lax.axis_size("tensor")
    me = lax.axis_index("tensor")
    rows, width = attention_result.shape
    holder_length, rank_part, _ = adapter_down_weight.shape
    rank, columns = adapter_up_weight.shape[1:]
    own_list = requests[0]
    entries = own_list.shape[0]
    one_hot = row_request_entry[:, None] == jnp.arange(entries)[None, :]
    row_rank = jnp.sum(jnp.where(one_hot, looked_up(ranks, own_list)[None, :], 0), axis=1)
    pages = looked_up(adapter_page_row, own_list)
    places = ((pages // holder_length) ^ lax.axis_index("dp")) * holder_length + pages % holder_length
    if n_tensor != 4 or n_dp != 4 or width % 512 or columns != width or rank_part % 16 or entries * rank_part > 256:
        return plain(
            attention_result, output_weight, adapter_down_weight, adapter_up_weight, places, one_hot, row_rank
        )


    def across(x, distance):
        return lax.ppermute(x, "dp", [(i, i ^ distance) for i in range(n_dp)])

    right = [(i, i + 1) for i in range(n_tensor - 1)]
    left = [(i + 1, i) for i in range(n_tensor - 1)]
    upper = me >= n_tensor // 2
    ends = me * (n_tensor - 1 - me) == 0
    slot = row_request_entry[:, None]
    farthest = jnp.where(upper, 0, n_tensor - 1)
    end = jnp.where(upper, n_tensor - 1, 0)
    source = jnp.where(upper, me - 2, me + 2)
    facts = jnp.stack([ends.astype(jnp.int32), farthest]).astype(jnp.int32)
    far_facts = jnp.stack([me, end, source, upper.astype(jnp.int32)]).astype(jnp.int32)
    near = plan_shards(me + jnp.array([0, -1, 1], jnp.int32), n_tensor)
    far = plan_shards(me + jnp.array([-2, 2], jnp.int32), n_tensor)

    right_1 = lax.ppermute(attention_result, "tensor", right)
    left_1 = lax.ppermute(after(attention_result, facts), "tensor", left)
    far_down = across(adapter_down_weight, 2)
    far_up = across(adapter_up_weight, 2)
    near_down = across(adapter_down_weight, 1)

    right_1, left_1, places, slot, live, facts, far_facts, near, far, ended, started, is_upper = lax.optimization_barrier(
        (
            right_1, left_1, places, slot, row_rank[:, None], facts, far_facts, near, far,
            ends.astype(jnp.int32)[None], farthest.astype(jnp.int32)[None], upper.astype(jnp.int32)[None],
        )
    )
    right_2 = lax.ppermute(right_1, "tensor", right[1:])
    left_2 = lax.ppermute(left_1, "tensor", left[:-1])
    downs = (adapter_down_weight, near_down, far_down, across(after(far_down, right_1, left_1), 1))
    down, other_down = join_downs(places, is_upper, downs, n_tensor)
    other_down = lax.ppermute(other_down, "tensor", [(0, 1), (3, 2)])

    base, low = add_shards(
        None, [attention_result, right_1, left_1], near, output_weight, down, slot, rank_part
    )
    other_low = lax.ppermute(low, "tensor", [(0, 1), (3, 2)])

    near_up = across(after(adapter_up_weight, far_down), 1)
    near_up, right_2, left_2 = lax.optimization_barrier((base, near_up, right_2, left_2))[1:]
    third = right[-1:] + left[:1]
    cuts = (0, width // 2, width // 4 * 3, width)

    def piece(i):
        cut = slice(cuts[i], cuts[i + 1])
        return jnp.where(upper, right_2[:, cut], left_2[:, cut])

    first_2 = piece(0)
    first_3 = lax.ppermute(first_2, "tensor", third)
    right_2, left_2, other_down, other_low = lax.optimization_barrier(
        (first_2, right_2, left_2, other_down, other_low)
    )[1:]
    pair = far_low(
        far_facts, right_1, right_2, left_1, left_2, down, other_down, slot, live, low, other_low
    )
    from_middle = lax.ppermute(pair, "tensor", [(1, 2), (2, 1)])
    base, = add_shards(after(base, pair), [right_2, left_2], far, output_weight)
    low = jnp.where(upper, jnp.concatenate([from_middle, pair], axis=1), jnp.concatenate([pair, from_middle], axis=1))
    second_2 = jnp.concatenate([piece(1), low], axis=1)
    second_3 = lax.ppermute(second_2, "tensor", third)
    right_2, left_2 = lax.optimization_barrier((second_2, right_2, left_2))[1:]
    last_3 = lax.ppermute(piece(2), "tensor", third)
    ups = (adapter_up_weight, near_up, far_up, across(after(far_up, first_2), 1))
    base = add_half(base, first_3, ended, started, output_weight)
    total, rows_of = prepare(facts, places, base, second_2, second_3, output_weight, ups, slot)
    total, rows_of, last_3 = lax.optimization_barrier((total, rows_of, last_3))
    return add_last(facts, total, rows_of, last_3)


def gather_pages(block, n_dp):
    return [block] + [
        lax.ppermute(block, "dp", [(i, i ^ j) for i in range(n_dp)]) for j in range(1, n_dp)
    ]


def plain(x, output_weight, down_weight, up_weight, places, one_hot, row_rank):
    n_dp = lax.axis_size("dp")
    rows = x.shape[0]
    rank, columns = up_weight.shape[1:]
    entries = one_hot.shape[1]

    def requested(block):
        blocks = jnp.concatenate(gather_pages(block, n_dp), axis=0)
        return jnp.concatenate(
            [lax.dynamic_slice_in_dim(blocks, places[e], 1, 0) for e in range(entries)], axis=0
        )

    down, up = requested(down_weight), requested(up_weight)
    x = lax.all_gather(x, "tensor", axis=1, tiled=True)
    base = jnp.dot(x, output_weight, preferred_element_type=F32)
    low = jnp.einsum("rd,ekd->rek", x, down, preferred_element_type=F32)
    low = jnp.sum(jnp.where(one_hot[:, :, None], low, 0.0), axis=1).astype(BF16)
    low = lax.all_gather(low, "tensor", axis=1, tiled=True)
    low = jnp.where(jnp.arange(rank)[None, :] < row_rank[:, None], low, jnp.zeros_like(low))
    spread = jnp.where(one_hot[:, :, None], low[:, None, :], jnp.zeros((), BF16))
    term = jnp.dot(
        spread.reshape(rows, entries * rank), up.reshape(entries * rank, columns), preferred_element_type=F32
    )
    return (base + term).astype(BF16)


def solution(mesh):
    in_specs = (
        P(("groups", "dp"), "tensor"),
        P(None, "tensor"),
        P("dp", "tensor", None),
        P("dp", None, "tensor"),
        P("groups"),
        P(("groups", "dp"), None),
        P(("groups", "dp")),
        P(),
    )
    out_specs = P(("groups", "dp"), "tensor")
    return jax.shard_map(local, mesh=mesh, in_specs=in_specs, out_specs=out_specs, check_vma=False)
```

```python
import functools

import jax
import jax.numpy as jnp
from jax import lax
from jax.experimental import pallas as pl
from jax.experimental.pallas import tpu as pltpu
from jax.sharding import PartitionSpec as P

PARAMS = pltpu.CompilerParams(vmem_limit_bytes=48 * 2**20)
TAIL_PARAMS = pltpu.CompilerParams(vmem_limit_bytes=24 * 2**20)
F32 = jnp.float32
BF16 = jnp.bfloat16
PIECES = 2


def start_pages(places, blocks, targets, sems, rows_of):
    for e, target in enumerate(targets):
        first = 0
        for block in blocks:
            past = first + block.shape[0]

            @pl.when((places[e] >= first) & (places[e] < past))
            def _():
                pltpu.make_async_copy(rows_of(block.at[places[e] - first]), target, sems[e]).start()

            first = past


def join_downs_kernel(places, upper, *refs):
    *blocks, out, other, held, sems = refs
    _, rank_part, _ = blocks[0].shape
    shards, slots, width = held.shape
    entries = places.shape[0]
    step = pl.program_id(0)

    def targets(t):
        return [held.at[t, pl.ds(e * rank_part, rank_part)] for e in range(entries)]

    @pl.when(step == 0)
    def _():
        for t in range(shards):
            semaphores = [sems.at[t, e] for e in range(entries)]
            start_pages(
                places, blocks, targets(t), semaphores, lambda page: page.at[:, pl.ds(t * width, width)]
            )
            held[t, entries * rank_part:] = jnp.zeros((slots - entries * rank_part, width), BF16)

    for t in range(shards):

        @pl.when(step == t)
        def _():
            for e, target in enumerate(targets(t)):
                source = blocks[0].at[0, :, pl.ds(t * width, width)]
                pltpu.make_async_copy(source, target, sems.at[t, e]).wait()
            joined = held[t].T
            out[...] = joined
            half = shards // 2

            @pl.when((upper[0] != 0) == (t < half))
            def _():
                other[:, t % half * width:(t % half + 1) * width] = held[t, :entries * rank_part]


def join_downs(places, upper, blocks, shards):
    entries = places.shape[0]
    _, rank_part, features = blocks[0].shape
    width, slots = features // shards, -(-entries * rank_part // 128) * 128
    return pl.pallas_call(
        join_downs_kernel,
        out_shape=[
            jax.ShapeDtypeStruct((features, slots), BF16),
            jax.ShapeDtypeStruct((entries * rank_part, features // 2), BF16),
        ],
        grid=(shards,),
        in_specs=[pl.BlockSpec(memory_space=pltpu.SMEM)] * 2
        + [pl.BlockSpec(memory_space=pltpu.HBM)] * len(blocks),
        out_specs=[
            pl.BlockSpec((width, slots), lambda t: (t, 0)),
            pl.BlockSpec((entries * rank_part, features // 2), lambda t: (0, 0)),
        ],
        scratch_shapes=[pltpu.VMEM((shards, slots, width), BF16), pltpu.SemaphoreType.DMA((shards, entries))],
        compiler_params=TAIL_PARAMS,
        cost_estimate=pl.CostEstimate(flops=1, bytes_accessed=1, transcendentals=0),
    )(places, upper, *blocks)


RESIDENT = pl.BlockSpec(memory_space=pltpu.VMEM)


def in_hbm(a):
    return pltpu.with_memory_space_constraint(a, pltpu.HBM)


IN_HBM = pl.BlockSpec(memory_space=pltpu.HBM)


def fold_entry(low, slot, rank_part):
    lane = lax.broadcasted_iota(jnp.int32, low.shape, 1)
    own = jnp.where(lane // rank_part == slot, low, 0.0)
    shape = (low.shape[1], rank_part)
    fold = lax.rem(lax.broadcasted_iota(jnp.int32, shape, 0), rank_part) == lax.broadcasted_iota(jnp.int32, shape, 1)
    return jnp.dot(own, fold.astype(F32), precision=lax.Precision.HIGHEST, preferred_element_type=F32)


def shards_kernel(with_low, start, valid, *refs):
    refs = list(refs)
    xs = [refs.pop(0) for _ in range(valid.shape[0])]
    weight = refs.pop(0)
    if with_low:
        down, slot, base, low, acc = refs
    else:
        base_in, base = refs
    step = pl.program_id(0)

    @pl.when(step == 0)
    def _():
        base[...] = jnp.zeros_like(base) if with_low else base_in[...]
        if with_low:
            acc[...] = jnp.zeros_like(acc)

    for i, x in enumerate(xs):

        @pl.when((step // 2 == i) & (valid[i] != 0))
        def _():
            part = min(base.shape[1], 512)
            for n in range(0, base.shape[1], part):
                base[:, n:n + part] += jnp.dot(x[...], weight[:, n:n + part], preferred_element_type=F32)
            if with_low:
                acc[...] += jnp.dot(x[...], down[...], preferred_element_type=F32)

    if with_low:

        @pl.when(step == pl.num_programs(0) - 1)
        def _():
            low[...] = fold_entry(acc[...], slot[...], low.shape[1])


def plan_shards(source, n_tensor):
    there = (source >= 0) & (source < n_tensor)
    start = 2 * jnp.clip(source, 0, n_tensor - 1)[:, None] + jnp.arange(2)[None, :]
    idle = jnp.concatenate([start[1:2, :1], start[:-1, 1:]], axis=0)
    start = jnp.where(there[:, None], start, idle).reshape(-1).astype(jnp.int32)
    return start, there.astype(jnp.int32)


def add_shards(base, xs, plan, weight, down=None, slot=None, rank_part=0):
    rows, width = xs[0].shape
    half = width // 2
    columns = weight.shape[1]
    steps = 2 * len(xs)

    def whole(a):
        return pl.BlockSpec((rows, a), lambda s, *_: (0, 0))

    def walked(a):
        return pl.BlockSpec((half, a.shape[1]), lambda s, start, valid: (start[s], 0))

    in_specs = [
        pl.BlockSpec((rows, half), lambda s, *_, i=i: (0, jnp.clip(s - 2 * i, 0, 1))) for i in range(len(xs))
    ] + [walked(weight)]
    out_shape = [jax.ShapeDtypeStruct((rows, columns), F32)]
    scratch = []
    slots = 0
    if base is None:
        slots = down.shape[1]
        in_specs += [walked(down), whole(1)]
        out_shape += [jax.ShapeDtypeStruct((rows, rank_part), F32)]
        scratch = [pltpu.VMEM((rows, slots), F32)]
        rest = (down, slot)
    else:
        in_specs += [whole(columns)]
        rest = (base,)
    return pl.pallas_call(
        functools.partial(shards_kernel, base is None),
        out_shape=out_shape,
        grid_spec=pltpu.PrefetchScalarGridSpec(
            num_scalar_prefetch=2,
            grid=(steps,),
            in_specs=in_specs,
            out_specs=[whole(a.shape[1]) for a in out_shape],
            scratch_shapes=scratch,
        ),
        compiler_params=PARAMS,
        cost_estimate=pl.CostEstimate(flops=1, bytes_accessed=1, transcendentals=0),
    )(*plan, *xs, weight, *rest)


def half_kernel(start, valid, x, weight, base_in, base):
    step = pl.program_id(0)

    @pl.when(step == 0)
    def _():
        base[...] = base_in[...]

    @pl.when(valid[0] != 0)
    def _():
        part = min(base.shape[1], 512)
        for n in range(0, base.shape[1], part):
            base[:, n:n + part] += jnp.dot(x[...], weight[:, n:n + part], preferred_element_type=F32)


def add_half(base, x, valid, source, weight):
    rows, half = x.shape
    columns = weight.shape[1]
    step = half // 2
    whole = pl.BlockSpec((rows, columns), lambda s, *_: (0, 0))
    return pl.pallas_call(
        half_kernel,
        out_shape=jax.ShapeDtypeStruct((rows, columns), F32),
        grid_spec=pltpu.PrefetchScalarGridSpec(
            num_scalar_prefetch=2,
            grid=(2,),
            in_specs=[
                pl.BlockSpec((rows, step), lambda s, *_: (0, s)),
                pl.BlockSpec((step, columns), lambda s, source, valid: (source[0] * 4 + s, 0)),
                whole,
            ],
            out_specs=whole,
        ),
        compiler_params=PARAMS,
        cost_estimate=pl.CostEstimate(flops=1, bytes_accessed=1, transcendentals=0),
    )(source, valid, x, weight, base)


def far_low_kernel(
    facts, left_1, left_2, right_1, right_2, down, other_down, slot, row_rank, low, other_low,
    out, near_x, far_x, rows_of, other_rows, sems
):
    me, end, source, upper = facts[0], facts[1], facts[2], facts[3]
    width = far_x.shape[1]
    rank_part = low.shape[1]
    start = pl.multiple_of(source * width, width)

    @pl.when(upper != 0)
    def _():
        pltpu.make_async_copy(left_2, far_x, sems.at[0]).start()
        pltpu.make_async_copy(left_1, near_x, sems.at[1]).start()

    @pl.when(upper == 0)
    def _():
        pltpu.make_async_copy(right_2, far_x, sems.at[0]).start()
        pltpu.make_async_copy(right_1, near_x, sems.at[1]).start()

    copies = [
        pltpu.make_async_copy(down.at[pl.ds(start, width)], rows_of, sems.at[2]),
        pltpu.make_async_copy(other_down, other_rows, sems.at[3]),
    ]
    for copy in copies:
        copy.start()
    pltpu.make_async_copy(left_2, far_x, sems.at[0]).wait()

    def finished(total, sums, place):
        sums = total[...] + fold_entry(sums, slot[...], rank_part)
        k = lax.broadcasted_iota(jnp.int32, sums.shape, 1) + place * rank_part
        return jnp.where(k < row_rank[...], sums, 0.0)

    copies[0].wait()
    own = finished(low, jnp.dot(far_x[...], rows_of[...], preferred_element_type=F32), me)
    pltpu.make_async_copy(left_1, near_x, sems.at[1]).wait()
    copies[1].wait()
    sums = jnp.zeros((far_x.shape[0], other_rows.shape[0]), F32)
    for x, place in ((far_x, 1 - upper), (near_x, upper)):
        rows = other_rows[:, pl.ds(pl.multiple_of(place * width, width), width)]
        sums += lax.dot_general(x[...], rows, (((1,), (1,)), ((), ())), preferred_element_type=F32)
    other = finished(other_low, sums, end)
    at_left = jnp.concatenate([other, own], axis=1)
    at_right = jnp.concatenate([own, other], axis=1)
    out[...] = jnp.where(upper != 0, at_right, at_left).astype(BF16)


def far_low(facts, left_1, left_2, right_1, right_2, down, other_down, slot, row_rank, low, other_low):
    rows, width = left_1.shape
    slots = down.shape[1]
    return pl.pallas_call(
        far_low_kernel,
        out_shape=jax.ShapeDtypeStruct((rows, 2 * low.shape[1]), BF16),
        in_specs=[pl.BlockSpec(memory_space=pltpu.SMEM)] + [IN_HBM] * 6 + [RESIDENT] * 4,
        out_specs=RESIDENT,
        scratch_shapes=[
            pltpu.VMEM((rows, width), BF16),
            pltpu.VMEM((rows, width), BF16),
            pltpu.VMEM((width, slots), BF16),
            pltpu.VMEM(other_down.shape, BF16),
            pltpu.SemaphoreType.DMA((4,)),
        ],
        compiler_params=TAIL_PARAMS,
        cost_estimate=pl.CostEstimate(flops=1, bytes_accessed=1, transcendentals=0),
    )(facts, left_1, left_2, right_1, right_2, in_hbm(down), other_down, slot, row_rank, low, other_low)


def prepare_kernel(facts, places, base, sent, received, weight, *refs):
    *blocks, slot, total, last_rows, mid, mid_rows, up, spread, sems = refs
    mid_width, last_width = mid_rows.shape[0], last_rows.shape[0]
    width = mid_width + last_width
    _, rank, _ = blocks[0].shape
    count = up.shape[0] // rank
    which, start = facts[0], facts[1] * 2 * width + width
    part = min(total.shape[1], 512)

    def rows_at(first, length):
        return weight.at[pl.ds(pl.multiple_of(start + first, length), length)]

    to_total = pltpu.make_async_copy(base, total, sems.at[0])
    to_mid_rows = pltpu.make_async_copy(rows_at(0, mid_width), mid_rows, sems.at[1])
    to_last = pltpu.make_async_copy(rows_at(mid_width, last_width), last_rows, sems.at[2])
    pages = [up.at[pl.ds(e * rank, rank)] for e in range(count)]
    page_sems = [sems.at[4 + e] for e in range(count)]

    @pl.when(which == 0)
    def _():
        pltpu.make_async_copy(sent, mid, sems.at[3]).start()

    @pl.when(which != 0)
    def _():
        pltpu.make_async_copy(received, mid, sems.at[3]).start()

    to_total.start()
    start_pages(places, blocks, pages, page_sems, lambda page: page)

    @pl.when(which != 0)
    def _():
        to_mid_rows.start()
        to_last.start()

    pltpu.make_async_copy(sent, mid, sems.at[3]).wait()
    for e in range(count):
        spread[:, e * rank:(e + 1) * rank] = jnp.where(
            slot[...] == e, mid[:, mid_width:].astype(F32), 0.0
        ).astype(BF16)
    for page, sem in zip(pages, page_sems):
        pltpu.make_async_copy(blocks[0].at[0], page, sem).wait()
    to_total.wait()
    for n in range(0, total.shape[1], part):
        cut = slice(n, n + part)
        total[:, cut] += jnp.dot(spread[...], up[:, cut], preferred_element_type=F32)

    @pl.when(which != 0)
    def _():
        to_mid_rows.wait()
        for n in range(0, total.shape[1], part):
            cut = slice(n, n + part)
            total[:, cut] += jnp.dot(mid[:, :mid_width], mid_rows[:, cut], preferred_element_type=F32)
        to_last.wait()


def prepare(facts, places, base, sent, received, weight, blocks, slot):
    rows, columns = base.shape
    rank = blocks[0].shape[1]
    entries = places.shape[0]
    mid_width = sent.shape[1] - rank
    last_width = mid_width
    return pl.pallas_call(
        prepare_kernel,
        out_shape=[pltpu.VMEM((rows, columns), F32), pltpu.VMEM((last_width, columns), BF16)],
        in_specs=[pl.BlockSpec(memory_space=pltpu.SMEM)] * 2 + [IN_HBM] * (4 + len(blocks)) + [RESIDENT],
        out_specs=[RESIDENT] * 2,
        scratch_shapes=[
            pltpu.VMEM(sent.shape, BF16),
            pltpu.VMEM((mid_width, columns), BF16),
            pltpu.VMEM((entries * rank, columns), BF16),
            pltpu.VMEM((rows, entries * rank), BF16),
            pltpu.SemaphoreType.DMA((4 + entries,)),
        ],
        compiler_params=TAIL_PARAMS,
        cost_estimate=pl.CostEstimate(flops=1, bytes_accessed=1, transcendentals=0),
    )(facts, places, base, sent, received, weight, in_hbm(blocks[0]), *blocks[1:], slot)


def last_kernel(facts, total, weight, x, out):
    part = out.shape[1]
    cut = pl.ds(pl.multiple_of(pl.program_id(0) * part, part), part)

    @pl.when(facts[0] != 0)
    def _():
        out[...] = (total[:, cut] + jnp.dot(x[...], weight[:, cut], preferred_element_type=F32)).astype(BF16)

    @pl.when(facts[0] == 0)
    def _():
        out[...] = total[:, cut].astype(BF16)


def add_last(facts, total, weight, x):
    rows, columns = total.shape
    part = min(columns, 512)
    return pl.pallas_call(
        last_kernel,
        out_shape=jax.ShapeDtypeStruct((rows, columns), BF16),
        grid=(columns // part,),
        in_specs=[pl.BlockSpec(memory_space=pltpu.SMEM), RESIDENT, RESIDENT, pl.BlockSpec(x.shape, lambda n: (0, 0))],
        out_specs=pl.BlockSpec((rows, part), lambda n: (0, n)),
        compiler_params=TAIL_PARAMS,
        cost_estimate=pl.CostEstimate(flops=1, bytes_accessed=1, transcendentals=0),
    )(facts, total, weight, x)


def after(value, *earlier):
    return lax.optimization_barrier((value,) + earlier)[0]


def looked_up(table, ids):
    hit = ids[:, None] == jnp.arange(table.shape[0])[None, :]
    return jnp.sum(jnp.where(hit, table[None, :], 0), axis=1)


def local(
    attention_result,
    output_weight,
    adapter_down_weight,
    adapter_up_weight,
    adapter_page_row,
    requests,
    row_request_entry,
    ranks,
):
    n_dp = lax.axis_size("dp")
    n_tensor = lax.axis_size("tensor")
    me = lax.axis_index("tensor")
    rows, width = attention_result.shape
    holder_length, rank_part, _ = adapter_down_weight.shape
    rank, columns = adapter_up_weight.shape[1:]
    own_list = requests[0]
    entries = own_list.shape[0]
    one_hot = row_request_entry[:, None] == jnp.arange(entries)[None, :]
    row_rank = jnp.sum(jnp.where(one_hot, looked_up(ranks, own_list)[None, :], 0), axis=1)
    pages = looked_up(adapter_page_row, own_list)
    places = ((pages // holder_length) ^ lax.axis_index("dp")) * holder_length + pages % holder_length
    if n_tensor != 4 or n_dp != 4 or width % 512 or columns != width or rank_part % 16 or entries * rank_part > 256:
        return plain(
            attention_result, output_weight, adapter_down_weight, adapter_up_weight, places, one_hot, row_rank
        )


    def across(x, distance):
        return lax.ppermute(x, "dp", [(i, i ^ distance) for i in range(n_dp)])

    right = [(i, i + 1) for i in range(n_tensor - 1)]
    left = [(i + 1, i) for i in range(n_tensor - 1)]
    upper = me >= n_tensor // 2
    ends = me * (n_tensor - 1 - me) == 0
    slot = row_request_entry[:, None]
    farthest = jnp.where(upper, 0, n_tensor - 1)
    end = jnp.where(upper, n_tensor - 1, 0)
    source = jnp.where(upper, me - 2, me + 2)
    facts = jnp.stack([ends.astype(jnp.int32), farthest]).astype(jnp.int32)
    far_facts = jnp.stack([me, end, source, upper.astype(jnp.int32)]).astype(jnp.int32)
    near = plan_shards(me + jnp.array([0, -1, 1], jnp.int32), n_tensor)
    far = plan_shards(me + jnp.array([-2, 2], jnp.int32), n_tensor)

    right_1 = lax.ppermute(attention_result, "tensor", right)
    left_1 = lax.ppermute(attention_result, "tensor", left)
    far_down = across(adapter_down_weight, 2)
    far_up = across(adapter_up_weight, 2)
    near_down = across(adapter_down_weight, 1)

    right_1, left_1, places, slot, live, facts, far_facts, near, far, ended, started, is_upper = lax.optimization_barrier(
        (
            right_1, left_1, places, slot, row_rank[:, None], facts, far_facts, near, far,
            ends.astype(jnp.int32)[None], farthest.astype(jnp.int32)[None], upper.astype(jnp.int32)[None],
        )
    )
    right_2 = lax.ppermute(right_1, "tensor", right[1:])
    left_2 = lax.ppermute(left_1, "tensor", left[:-1])
    came = after(far_down, right_1, left_1)
    cuts = range(0, holder_length, max(holder_length // PIECES, 1))
    swapped = [across(came[i:i + cuts.step], 1) for i in cuts]
    downs = (adapter_down_weight, near_down, far_down, *swapped)
    down, other_down = join_downs(places, is_upper, downs, n_tensor)
    other_down = lax.ppermute(other_down, "tensor", [(0, 1), (3, 2)])

    base, low = add_shards(
        None, [attention_result, right_1, left_1], near, output_weight, down, slot, rank_part
    )
    other_low = lax.ppermute(low, "tensor", [(0, 1), (3, 2)])

    right_2, left_2 = lax.optimization_barrier((base, right_2, left_2))[1:]
    third = right[-1:] + left[:1]
    cuts = (0, width // 2, width // 4 * 3, width)

    def piece(i):
        cut = slice(cuts[i], cuts[i + 1])
        return jnp.where(upper, right_2[:, cut], left_2[:, cut])

    first_2 = piece(0)
    first_3 = lax.ppermute(first_2, "tensor", third)
    right_2, left_2, other_down, other_low = lax.optimization_barrier(
        (first_2, right_2, left_2, other_down, other_low)
    )[1:]
    pair = far_low(
        far_facts, right_1, right_2, left_1, left_2, down, other_down, slot, live, low, other_low
    )
    from_middle = lax.ppermute(pair, "tensor", [(1, 2), (2, 1)])
    base, = add_shards(after(base, pair), [right_2, left_2], far, output_weight)
    low = jnp.where(upper, jnp.concatenate([from_middle, pair], axis=1), jnp.concatenate([pair, from_middle], axis=1))
    second_2 = jnp.concatenate([piece(1), low], axis=1)
    second_3 = lax.ppermute(second_2, "tensor", third)
    right_2, left_2 = lax.optimization_barrier((second_2, right_2, left_2))[1:]
    last_3 = lax.ppermute(piece(2), "tensor", third)
    ups = (adapter_up_weight, across(after(adapter_up_weight, far_down), 1), far_up, across(after(far_up, first_2), 1))
    base = add_half(base, first_3, ended, started, output_weight)
    total, rows_of = prepare(facts, places, base, second_2, second_3, output_weight, ups, slot)
    total, rows_of, last_3 = lax.optimization_barrier((total, rows_of, last_3))
    return add_last(facts, total, rows_of, last_3)


def gather_pages(block, n_dp):
    return [block] + [
        lax.ppermute(block, "dp", [(i, i ^ j) for i in range(n_dp)]) for j in range(1, n_dp)
    ]


def plain(x, output_weight, down_weight, up_weight, places, one_hot, row_rank):
    n_dp = lax.axis_size("dp")
    rows = x.shape[0]
    rank, columns = up_weight.shape[1:]
    entries = one_hot.shape[1]

    def requested(block):
        blocks = jnp.concatenate(gather_pages(block, n_dp), axis=0)
        return jnp.concatenate(
            [lax.dynamic_slice_in_dim(blocks, places[e], 1, 0) for e in range(entries)], axis=0
        )

    down, up = requested(down_weight), requested(up_weight)
    x = lax.all_gather(x, "tensor", axis=1, tiled=True)
    base = jnp.dot(x, output_weight, preferred_element_type=F32)
    low = jnp.einsum("rd,ekd->rek", x, down, preferred_element_type=F32)
    low = jnp.sum(jnp.where(one_hot[:, :, None], low, 0.0), axis=1).astype(BF16)
    low = lax.all_gather(low, "tensor", axis=1, tiled=True)
    low = jnp.where(jnp.arange(rank)[None, :] < row_rank[:, None], low, jnp.zeros_like(low))
    spread = jnp.where(one_hot[:, :, None], low[:, None, :], jnp.zeros((), BF16))
    term = jnp.dot(
        spread.reshape(rows, entries * rank), up.reshape(entries * rank, columns), preferred_element_type=F32
    )
    return (base + term).astype(BF16)


def solution(mesh):
    in_specs = (
        P(("groups", "dp"), "tensor"),
        P(None, "tensor"),
        P("dp", "tensor", None),
        P("dp", None, "tensor"),
        P("groups"),
        P(("groups", "dp"), None),
        P(("groups", "dp")),
        P(),
    )
    out_specs = P(("groups", "dp"), "tensor")
    return jax.shard_map(local, mesh=mesh, in_specs=in_specs, out_specs=out_specs, check_vma=False)
```

```python
import functools

import jax
import jax.numpy as jnp
from jax import lax
from jax.experimental import pallas as pl
from jax.experimental.pallas import tpu as pltpu
from jax.sharding import PartitionSpec as P

PARAMS = pltpu.CompilerParams(vmem_limit_bytes=48 * 2**20)
TAIL_PARAMS = pltpu.CompilerParams(vmem_limit_bytes=24 * 2**20)
F32 = jnp.float32
BF16 = jnp.bfloat16
PIECES = 2


def start_pages(places, blocks, targets, sems, rows_of):
    for e, target in enumerate(targets):
        first = 0
        for block in blocks:
            past = first + block.shape[0]

            @pl.when((places[e] >= first) & (places[e] < past))
            def _():
                pltpu.make_async_copy(rows_of(block.at[places[e] - first]), target, sems[e]).start()

            first = past


def join_downs_kernel(places, upper, *refs):
    *blocks, out, other, held, sems = refs
    _, rank_part, _ = blocks[0].shape
    shards, slots, width = held.shape
    entries = places.shape[0]
    step = pl.program_id(0)

    def targets(t):
        return [held.at[t, pl.ds(e * rank_part, rank_part)] for e in range(entries)]

    @pl.when(step == 0)
    def _():
        for t in range(shards):
            semaphores = [sems.at[t, e] for e in range(entries)]
            start_pages(
                places, blocks, targets(t), semaphores, lambda page: page.at[:, pl.ds(t * width, width)]
            )
            held[t, entries * rank_part:] = jnp.zeros((slots - entries * rank_part, width), BF16)

    for t in range(shards):

        @pl.when(step == t)
        def _():
            for e, target in enumerate(targets(t)):
                source = blocks[0].at[0, :, pl.ds(t * width, width)]
                pltpu.make_async_copy(source, target, sems.at[t, e]).wait()
            joined = held[t].T
            out[...] = joined
            half = shards // 2

            @pl.when((upper[0] != 0) == (t < half))
            def _():
                other[:, t % half * width:(t % half + 1) * width] = held[t, :entries * rank_part]


def join_downs(places, upper, blocks, shards):
    entries = places.shape[0]
    _, rank_part, features = blocks[0].shape
    width, slots = features // shards, -(-entries * rank_part // 128) * 128
    return pl.pallas_call(
        join_downs_kernel,
        out_shape=[
            jax.ShapeDtypeStruct((features, slots), BF16),
            jax.ShapeDtypeStruct((entries * rank_part, features // 2), BF16),
        ],
        grid=(shards,),
        in_specs=[pl.BlockSpec(memory_space=pltpu.SMEM)] * 2
        + [pl.BlockSpec(memory_space=pltpu.HBM)] * len(blocks),
        out_specs=[
            pl.BlockSpec((width, slots), lambda t: (t, 0)),
            pl.BlockSpec((entries * rank_part, features // 2), lambda t: (0, 0)),
        ],
        scratch_shapes=[pltpu.VMEM((shards, slots, width), BF16), pltpu.SemaphoreType.DMA((shards, entries))],
        compiler_params=TAIL_PARAMS,
        cost_estimate=pl.CostEstimate(flops=1, bytes_accessed=1, transcendentals=0),
    )(places, upper, *blocks)


RESIDENT = pl.BlockSpec(memory_space=pltpu.VMEM)


def in_hbm(a):
    return pltpu.with_memory_space_constraint(a, pltpu.HBM)


IN_HBM = pl.BlockSpec(memory_space=pltpu.HBM)


def fold_entry(low, slot, rank_part):
    lane = lax.broadcasted_iota(jnp.int32, low.shape, 1)
    own = jnp.where(lane // rank_part == slot, low, 0.0)
    shape = (low.shape[1], rank_part)
    fold = lax.rem(lax.broadcasted_iota(jnp.int32, shape, 0), rank_part) == lax.broadcasted_iota(jnp.int32, shape, 1)
    return jnp.dot(own, fold.astype(F32), precision=lax.Precision.HIGHEST, preferred_element_type=F32)


def shards_kernel(with_low, start, valid, *refs):
    refs = list(refs)
    xs = [refs.pop(0) for _ in range(valid.shape[0])]
    weight = refs.pop(0)
    if with_low:
        down, slot, base, low, acc = refs
    else:
        base_in, base = refs
    step = pl.program_id(0)

    @pl.when(step == 0)
    def _():
        base[...] = jnp.zeros_like(base) if with_low else base_in[...]
        if with_low:
            acc[...] = jnp.zeros_like(acc)

    for i, x in enumerate(xs):

        @pl.when((step // 2 == i) & (valid[i] != 0))
        def _():
            part = min(base.shape[1], 512)
            for n in range(0, base.shape[1], part):
                base[:, n:n + part] += jnp.dot(x[...], weight[:, n:n + part], preferred_element_type=F32)
            if with_low:
                acc[...] += jnp.dot(x[...], down[...], preferred_element_type=F32)

    if with_low:

        @pl.when(step == pl.num_programs(0) - 1)
        def _():
            low[...] = fold_entry(acc[...], slot[...], low.shape[1])


def plan_shards(source, n_tensor):
    there = (source >= 0) & (source < n_tensor)
    start = 2 * jnp.clip(source, 0, n_tensor - 1)[:, None] + jnp.arange(2)[None, :]
    idle = jnp.concatenate([start[1:2, :1], start[:-1, 1:]], axis=0)
    start = jnp.where(there[:, None], start, idle).reshape(-1).astype(jnp.int32)
    return start, there.astype(jnp.int32)


def add_shards(base, xs, plan, weight, down=None, slot=None, rank_part=0):
    rows, width = xs[0].shape
    half = width // 2
    columns = weight.shape[1]
    steps = 2 * len(xs)

    def whole(a):
        return pl.BlockSpec((rows, a), lambda s, *_: (0, 0))

    def walked(a):
        return pl.BlockSpec((half, a.shape[1]), lambda s, start, valid: (start[s], 0))

    in_specs = [
        pl.BlockSpec((rows, half), lambda s, *_, i=i: (0, jnp.clip(s - 2 * i, 0, 1))) for i in range(len(xs))
    ] + [walked(weight)]
    out_shape = [jax.ShapeDtypeStruct((rows, columns), F32)]
    scratch = []
    slots = 0
    if base is None:
        slots = down.shape[1]
        in_specs += [walked(down), whole(1)]
        out_shape += [jax.ShapeDtypeStruct((rows, rank_part), F32)]
        scratch = [pltpu.VMEM((rows, slots), F32)]
        rest = (down, slot)
    else:
        in_specs += [whole(columns)]
        rest = (base,)
    return pl.pallas_call(
        functools.partial(shards_kernel, base is None),
        out_shape=out_shape,
        grid_spec=pltpu.PrefetchScalarGridSpec(
            num_scalar_prefetch=2,
            grid=(steps,),
            in_specs=in_specs,
            out_specs=[whole(a.shape[1]) for a in out_shape],
            scratch_shapes=scratch,
        ),
        compiler_params=PARAMS,
        cost_estimate=pl.CostEstimate(flops=1, bytes_accessed=1, transcendentals=0),
    )(*plan, *xs, weight, *rest)


def half_kernel(start, valid, x, weight, base_in, base):
    step = pl.program_id(0)

    @pl.when(step == 0)
    def _():
        base[...] = base_in[...]

    @pl.when(valid[0] != 0)
    def _():
        part = min(base.shape[1], 512)
        for n in range(0, base.shape[1], part):
            base[:, n:n + part] += jnp.dot(x[...], weight[:, n:n + part], preferred_element_type=F32)


def add_half(base, x, valid, source, weight):
    rows, half = x.shape
    columns = weight.shape[1]
    step = half // 5
    whole = pl.BlockSpec((rows, columns), lambda s, *_: (0, 0))
    return pl.pallas_call(
        half_kernel,
        out_shape=jax.ShapeDtypeStruct((rows, columns), F32),
        grid_spec=pltpu.PrefetchScalarGridSpec(
            num_scalar_prefetch=2,
            grid=(half // step,),
            in_specs=[
                pl.BlockSpec((rows, step), lambda s, *_: (0, s)),
                pl.BlockSpec((step, columns), lambda s, source, valid: (source[0] * (columns // step) + s, 0)),
                whole,
            ],
            out_specs=whole,
        ),
        compiler_params=PARAMS,
        cost_estimate=pl.CostEstimate(flops=1, bytes_accessed=1, transcendentals=0),
    )(source, valid, x, weight, base)


def far_low_kernel(
    facts, left_1, left_2, right_1, right_2, down, other_down, slot, row_rank, low, other_low,
    out, near_x, far_x, rows_of, other_rows, sems
):
    me, end, source, upper = facts[0], facts[1], facts[2], facts[3]
    width = far_x.shape[1]
    rank_part = low.shape[1]
    start = pl.multiple_of(source * width, width)

    @pl.when(upper != 0)
    def _():
        pltpu.make_async_copy(left_2, far_x, sems.at[0]).start()
        pltpu.make_async_copy(left_1, near_x, sems.at[1]).start()

    @pl.when(upper == 0)
    def _():
        pltpu.make_async_copy(right_2, far_x, sems.at[0]).start()
        pltpu.make_async_copy(right_1, near_x, sems.at[1]).start()

    copies = [
        pltpu.make_async_copy(down.at[pl.ds(start, width)], rows_of, sems.at[2]),
        pltpu.make_async_copy(other_down, other_rows, sems.at[3]),
    ]
    for copy in copies:
        copy.start()
    pltpu.make_async_copy(left_2, far_x, sems.at[0]).wait()

    def finished(total, sums, place):
        sums = total[...] + fold_entry(sums, slot[...], rank_part)
        k = lax.broadcasted_iota(jnp.int32, sums.shape, 1) + place * rank_part
        return jnp.where(k < row_rank[...], sums, 0.0)

    copies[0].wait()
    own = finished(low, jnp.dot(far_x[...], rows_of[...], preferred_element_type=F32), me)
    pltpu.make_async_copy(left_1, near_x, sems.at[1]).wait()
    copies[1].wait()
    sums = jnp.zeros((far_x.shape[0], other_rows.shape[0]), F32)
    for x, place in ((far_x, 1 - upper), (near_x, upper)):
        rows = other_rows[:, pl.ds(pl.multiple_of(place * width, width), width)]
        sums += lax.dot_general(x[...], rows, (((1,), (1,)), ((), ())), preferred_element_type=F32)
    other = finished(other_low, sums, end)
    at_left = jnp.concatenate([other, own], axis=1)
    at_right = jnp.concatenate([own, other], axis=1)
    out[...] = jnp.where(upper != 0, at_right, at_left).astype(BF16)


def far_low(facts, left_1, left_2, right_1, right_2, down, other_down, slot, row_rank, low, other_low):
    rows, width = left_1.shape
    slots = down.shape[1]
    return pl.pallas_call(
        far_low_kernel,
        out_shape=jax.ShapeDtypeStruct((rows, 2 * low.shape[1]), BF16),
        in_specs=[pl.BlockSpec(memory_space=pltpu.SMEM)] + [IN_HBM] * 6 + [RESIDENT] * 4,
        out_specs=RESIDENT,
        scratch_shapes=[
            pltpu.VMEM((rows, width), BF16),
            pltpu.VMEM((rows, width), BF16),
            pltpu.VMEM((width, slots), BF16),
            pltpu.VMEM(other_down.shape, BF16),
            pltpu.SemaphoreType.DMA((4,)),
        ],
        compiler_params=TAIL_PARAMS,
        cost_estimate=pl.CostEstimate(flops=1, bytes_accessed=1, transcendentals=0),
    )(facts, left_1, left_2, right_1, right_2, in_hbm(down), other_down, slot, row_rank, low, other_low)


def prepare_kernel(facts, places, base, sent, received, weight, *refs):
    *blocks, slot, total, last_rows, mid, mid_rows, up, spread, sems = refs
    mid_width, last_width = mid_rows.shape[0], last_rows.shape[0]
    shard = total.shape[1]
    _, rank, _ = blocks[0].shape
    count = up.shape[0] // rank
    which, start = facts[0], (facts[1] + 1) * shard - mid_width - last_width
    part = min(total.shape[1], 512)

    def rows_at(first, length):
        return weight.at[pl.ds(pl.multiple_of(start + first, last_width), length)]

    to_total = pltpu.make_async_copy(base, total, sems.at[0])
    to_mid_rows = pltpu.make_async_copy(rows_at(0, mid_width), mid_rows, sems.at[1])
    to_last = pltpu.make_async_copy(rows_at(mid_width, last_width), last_rows, sems.at[2])
    pages = [up.at[pl.ds(e * rank, rank)] for e in range(count)]
    page_sems = [sems.at[4 + e] for e in range(count)]

    @pl.when(which == 0)
    def _():
        pltpu.make_async_copy(sent, mid, sems.at[3]).start()

    @pl.when(which != 0)
    def _():
        pltpu.make_async_copy(received, mid, sems.at[3]).start()

    to_total.start()
    start_pages(places, blocks, pages, page_sems, lambda page: page)

    @pl.when(which != 0)
    def _():
        to_mid_rows.start()
        to_last.start()

    pltpu.make_async_copy(sent, mid, sems.at[3]).wait()
    for e in range(count):
        spread[:, e * rank:(e + 1) * rank] = jnp.where(
            slot[...] == e, mid[:, mid_width:].astype(F32), 0.0
        ).astype(BF16)
    for page, sem in zip(pages, page_sems):
        pltpu.make_async_copy(blocks[0].at[0], page, sem).wait()
    to_total.wait()
    for n in range(0, total.shape[1], part):
        cut = slice(n, n + part)
        total[:, cut] += jnp.dot(spread[...], up[:, cut], preferred_element_type=F32)

    @pl.when(which != 0)
    def _():
        to_mid_rows.wait()
        for n in range(0, total.shape[1], part):
            cut = slice(n, n + part)
            total[:, cut] += jnp.dot(mid[:, :mid_width], mid_rows[:, cut], preferred_element_type=F32)
        to_last.wait()


def prepare(facts, places, base, sent, received, last_width, weight, blocks, slot):
    rows, columns = base.shape
    rank = blocks[0].shape[1]
    entries = places.shape[0]
    mid_width = sent.shape[1] - rank
    return pl.pallas_call(
        prepare_kernel,
        out_shape=[pltpu.VMEM((rows, columns), F32), pltpu.VMEM((last_width, columns), BF16)],
        in_specs=[pl.BlockSpec(memory_space=pltpu.SMEM)] * 2 + [IN_HBM] * (4 + len(blocks)) + [RESIDENT],
        out_specs=[RESIDENT] * 2,
        scratch_shapes=[
            pltpu.VMEM(sent.shape, BF16),
            pltpu.VMEM((mid_width, columns), BF16),
            pltpu.VMEM((entries * rank, columns), BF16),
            pltpu.VMEM((rows, entries * rank), BF16),
            pltpu.SemaphoreType.DMA((4 + entries,)),
        ],
        compiler_params=TAIL_PARAMS,
        cost_estimate=pl.CostEstimate(flops=1, bytes_accessed=1, transcendentals=0),
    )(facts, places, base, sent, received, weight, in_hbm(blocks[0]), *blocks[1:], slot)


def last_kernel(facts, total, weight, x, out):
    part = out.shape[1]
    cut = pl.ds(pl.multiple_of(pl.program_id(0) * part, part), part)

    @pl.when(facts[0] != 0)
    def _():
        out[...] = (total[:, cut] + jnp.dot(x[...], weight[:, cut], preferred_element_type=F32)).astype(BF16)

    @pl.when(facts[0] == 0)
    def _():
        out[...] = total[:, cut].astype(BF16)


def add_last(facts, total, weight, x):
    rows, columns = total.shape
    part = min(columns, 512)
    return pl.pallas_call(
        last_kernel,
        out_shape=jax.ShapeDtypeStruct((rows, columns), BF16),
        grid=(columns // part,),
        in_specs=[pl.BlockSpec(memory_space=pltpu.SMEM), RESIDENT, RESIDENT, pl.BlockSpec(x.shape, lambda n: (0, 0))],
        out_specs=pl.BlockSpec((rows, part), lambda n: (0, n)),
        compiler_params=TAIL_PARAMS,
        cost_estimate=pl.CostEstimate(flops=1, bytes_accessed=1, transcendentals=0),
    )(facts, total, weight, x)


def after(value, *earlier):
    return lax.optimization_barrier((value,) + earlier)[0]


def looked_up(table, ids):
    hit = ids[:, None] == jnp.arange(table.shape[0])[None, :]
    return jnp.sum(jnp.where(hit, table[None, :], 0), axis=1)


def local(
    attention_result,
    output_weight,
    adapter_down_weight,
    adapter_up_weight,
    adapter_page_row,
    requests,
    row_request_entry,
    ranks,
):
    n_dp = lax.axis_size("dp")
    n_tensor = lax.axis_size("tensor")
    me = lax.axis_index("tensor")
    rows, width = attention_result.shape
    holder_length, rank_part, _ = adapter_down_weight.shape
    rank, columns = adapter_up_weight.shape[1:]
    own_list = requests[0]
    entries = own_list.shape[0]
    one_hot = row_request_entry[:, None] == jnp.arange(entries)[None, :]
    row_rank = jnp.sum(jnp.where(one_hot, looked_up(ranks, own_list)[None, :], 0), axis=1)
    pages = looked_up(adapter_page_row, own_list)
    places = ((pages // holder_length) ^ lax.axis_index("dp")) * holder_length + pages % holder_length
    if n_tensor != 4 or n_dp != 4 or width % 512 or columns != width or rank_part % 16 or entries * rank_part > 256:
        return plain(
            attention_result, output_weight, adapter_down_weight, adapter_up_weight, places, one_hot, row_rank
        )


    def across(x, distance):
        return lax.ppermute(x, "dp", [(i, i ^ distance) for i in range(n_dp)])

    right = [(i, i + 1) for i in range(n_tensor - 1)]
    left = [(i + 1, i) for i in range(n_tensor - 1)]
    upper = me >= n_tensor // 2
    ends = me * (n_tensor - 1 - me) == 0
    slot = row_request_entry[:, None]
    farthest = jnp.where(upper, 0, n_tensor - 1)
    end = jnp.where(upper, n_tensor - 1, 0)
    source = jnp.where(upper, me - 2, me + 2)
    facts = jnp.stack([ends.astype(jnp.int32), farthest]).astype(jnp.int32)
    far_facts = jnp.stack([me, end, source, upper.astype(jnp.int32)]).astype(jnp.int32)
    near = plan_shards(me + jnp.array([0, -1, 1], jnp.int32), n_tensor)
    far = plan_shards(me + jnp.array([-2, 2], jnp.int32), n_tensor)

    right_1 = lax.ppermute(attention_result, "tensor", right)
    left_1 = lax.ppermute(attention_result, "tensor", left)
    far_down = across(adapter_down_weight, 2)
    far_up = across(adapter_up_weight, 2)
    near_down = across(adapter_down_weight, 1)

    right_1, left_1, places, slot, live, facts, far_facts, near, far, ended, started, is_upper = lax.optimization_barrier(
        (
            right_1, left_1, places, slot, row_rank[:, None], facts, far_facts, near, far,
            ends.astype(jnp.int32)[None], farthest.astype(jnp.int32)[None], upper.astype(jnp.int32)[None],
        )
    )
    right_2 = lax.ppermute(right_1, "tensor", right[1:])
    left_2 = lax.ppermute(left_1, "tensor", left[:-1])
    came = after(far_down, right_1, left_1)
    cuts = range(0, holder_length, max(holder_length // PIECES, 1))
    swapped = [across(came[i:i + cuts.step], 1) for i in cuts]
    downs = (adapter_down_weight, near_down, far_down, *swapped)
    down, other_down = join_downs(places, is_upper, downs, n_tensor)
    other_down = lax.ppermute(other_down, "tensor", [(0, 1), (3, 2)])

    base, low = add_shards(
        None, [attention_result, right_1, left_1], near, output_weight, down, slot, rank_part
    )
    other_low = lax.ppermute(low, "tensor", [(0, 1), (3, 2)])

    right_2, left_2 = lax.optimization_barrier((base, right_2, left_2))[1:]
    third = right[-1:] + left[:1]
    cuts = (0, width // 8 * 5, width // 8 * 7, width)

    def piece(i):
        cut = slice(cuts[i], cuts[i + 1])
        return jnp.where(upper, right_2[:, cut], left_2[:, cut])

    first_2 = piece(0)
    first_3 = lax.ppermute(first_2, "tensor", third)
    right_2, left_2, other_down, other_low = lax.optimization_barrier(
        (first_2, right_2, left_2, other_down, other_low)
    )[1:]
    pair = far_low(
        far_facts, right_1, right_2, left_1, left_2, down, other_down, slot, live, low, other_low
    )
    from_middle = lax.ppermute(pair, "tensor", [(1, 2), (2, 1)])
    base, = add_shards(after(base, pair), [right_2, left_2], far, output_weight)
    low = jnp.where(upper, jnp.concatenate([from_middle, pair], axis=1), jnp.concatenate([pair, from_middle], axis=1))
    second_2 = jnp.concatenate([piece(1), low], axis=1)
    second_3 = lax.ppermute(second_2, "tensor", third)
    right_2, left_2 = lax.optimization_barrier((second_2, right_2, left_2))[1:]
    last_3 = lax.ppermute(piece(2), "tensor", third)
    ups = (adapter_up_weight, across(after(adapter_up_weight, far_down), 1), far_up, across(after(far_up, first_2), 1))
    base = add_half(base, first_3, ended, started, output_weight)
    total, rows_of = prepare(facts, places, base, second_2, second_3, width - cuts[2], output_weight, ups, slot)
    total, rows_of, last_3 = lax.optimization_barrier((total, rows_of, last_3))
    return add_last(facts, total, rows_of, last_3)


def gather_pages(block, n_dp):
    return [block] + [
        lax.ppermute(block, "dp", [(i, i ^ j) for i in range(n_dp)]) for j in range(1, n_dp)
    ]


def plain(x, output_weight, down_weight, up_weight, places, one_hot, row_rank):
    n_dp = lax.axis_size("dp")
    rows = x.shape[0]
    rank, columns = up_weight.shape[1:]
    entries = one_hot.shape[1]

    def requested(block):
        blocks = jnp.concatenate(gather_pages(block, n_dp), axis=0)
        return jnp.concatenate(
            [lax.dynamic_slice_in_dim(blocks, places[e], 1, 0) for e in range(entries)], axis=0
        )

    down, up = requested(down_weight), requested(up_weight)
    x = lax.all_gather(x, "tensor", axis=1, tiled=True)
    base = jnp.dot(x, output_weight, preferred_element_type=F32)
    low = jnp.einsum("rd,ekd->rek", x, down, preferred_element_type=F32)
    low = jnp.sum(jnp.where(one_hot[:, :, None], low, 0.0), axis=1).astype(BF16)
    low = lax.all_gather(low, "tensor", axis=1, tiled=True)
    low = jnp.where(jnp.arange(rank)[None, :] < row_rank[:, None], low, jnp.zeros_like(low))
    spread = jnp.where(one_hot[:, :, None], low[:, None, :], jnp.zeros((), BF16))
    term = jnp.dot(
        spread.reshape(rows, entries * rank), up.reshape(entries * rank, columns), preferred_element_type=F32
    )
    return (base + term).astype(BF16)


def solution(mesh):
    in_specs = (
        P(("groups", "dp"), "tensor"),
        P(None, "tensor"),
        P("dp", "tensor", None),
        P("dp", None, "tensor"),
        P("groups"),
        P(("groups", "dp"), None),
        P(("groups", "dp")),
        P(),
    )
    out_specs = P(("groups", "dp"), "tensor")
    return jax.shard_map(local, mesh=mesh, in_specs=in_specs, out_specs=out_specs, check_vma=False)
```

```python
import functools

import jax
import jax.numpy as jnp
from jax import lax
from jax.experimental import pallas as pl
from jax.experimental.pallas import tpu as pltpu
from jax.sharding import PartitionSpec as P

PARAMS = pltpu.CompilerParams(vmem_limit_bytes=48 * 2**20)
TAIL_PARAMS = pltpu.CompilerParams(vmem_limit_bytes=24 * 2**20)
F32 = jnp.float32
BF16 = jnp.bfloat16
PIECES = 2


def start_pages(places, blocks, targets, sems, rows_of):
    for e, target in enumerate(targets):
        first = 0
        for block in blocks:
            past = first + block.shape[0]

            @pl.when((places[e] >= first) & (places[e] < past))
            def _():
                pltpu.make_async_copy(rows_of(block.at[places[e] - first]), target, sems[e]).start()

            first = past


def join_downs_kernel(places, upper, *refs):
    *blocks, out, other, held, sems = refs
    _, rank_part, _ = blocks[0].shape
    shards, slots, width = held.shape
    entries = places.shape[0]
    step = pl.program_id(0)

    def targets(t):
        return [held.at[t, pl.ds(e * rank_part, rank_part)] for e in range(entries)]

    @pl.when(step == 0)
    def _():
        for t in range(shards):
            semaphores = [sems.at[t, e] for e in range(entries)]
            start_pages(
                places, blocks, targets(t), semaphores, lambda page: page.at[:, pl.ds(t * width, width)]
            )
            held[t, entries * rank_part:] = jnp.zeros((slots - entries * rank_part, width), BF16)

    for t in range(shards):

        @pl.when(step == t)
        def _():
            for e, target in enumerate(targets(t)):
                source = blocks[0].at[0, :, pl.ds(t * width, width)]
                pltpu.make_async_copy(source, target, sems.at[t, e]).wait()
            joined = held[t].T
            out[...] = joined
            half = shards // 2

            @pl.when((upper[0] != 0) == (t < half))
            def _():
                other[:, t % half * width:(t % half + 1) * width] = held[t, :entries * rank_part]


def join_downs(places, upper, blocks, shards):
    entries = places.shape[0]
    _, rank_part, features = blocks[0].shape
    width, slots = features // shards, -(-entries * rank_part // 128) * 128
    return pl.pallas_call(
        join_downs_kernel,
        out_shape=[
            jax.ShapeDtypeStruct((features, slots), BF16),
            jax.ShapeDtypeStruct((entries * rank_part, features // 2), BF16),
        ],
        grid=(shards,),
        in_specs=[pl.BlockSpec(memory_space=pltpu.SMEM)] * 2
        + [pl.BlockSpec(memory_space=pltpu.HBM)] * len(blocks),
        out_specs=[
            pl.BlockSpec((width, slots), lambda t: (t, 0)),
            pl.BlockSpec((entries * rank_part, features // 2), lambda t: (0, 0)),
        ],
        scratch_shapes=[pltpu.VMEM((shards, slots, width), BF16), pltpu.SemaphoreType.DMA((shards, entries))],
        compiler_params=TAIL_PARAMS,
        cost_estimate=pl.CostEstimate(flops=1, bytes_accessed=1, transcendentals=0),
    )(places, upper, *blocks)


RESIDENT = pl.BlockSpec(memory_space=pltpu.VMEM)


def in_hbm(a):
    return pltpu.with_memory_space_constraint(a, pltpu.HBM)


IN_HBM = pl.BlockSpec(memory_space=pltpu.HBM)


def fold_entry(low, slot, rank_part):
    lane = lax.broadcasted_iota(jnp.int32, low.shape, 1)
    own = jnp.where(lane // rank_part == slot, low, 0.0)
    shape = (low.shape[1], rank_part)
    fold = lax.rem(lax.broadcasted_iota(jnp.int32, shape, 0), rank_part) == lax.broadcasted_iota(jnp.int32, shape, 1)
    return jnp.dot(own, fold.astype(F32), precision=lax.Precision.HIGHEST, preferred_element_type=F32)


def shards_kernel(with_low, halves, start, valid, *refs):
    refs = list(refs)
    xs = [refs.pop(0) for _ in range(valid.shape[0])]
    weight = refs.pop(0)
    if with_low:
        down, slot, base, low, acc = refs
    else:
        base_in, base = refs
    step = pl.program_id(0)

    @pl.when(step == 0)
    def _():
        base[...] = jnp.zeros_like(base) if with_low else base_in[...]
        if with_low:
            acc[...] = jnp.zeros_like(acc)

    for i, x in enumerate(xs):

        @pl.when((step // halves == i) & (valid[i] != 0))
        def _():
            part = min(base.shape[1], 512)
            for n in range(0, base.shape[1], part):
                base[:, n:n + part] += jnp.dot(x[...], weight[:, n:n + part], preferred_element_type=F32)
            if with_low:
                acc[...] += jnp.dot(x[...], down[...], preferred_element_type=F32)

    if with_low:

        @pl.when(step == pl.num_programs(0) - 1)
        def _():
            low[...] = fold_entry(acc[...], slot[...], low.shape[1])


def plan_shards(source, n_tensor):
    there = (source >= 0) & (source < n_tensor)
    start = 2 * jnp.clip(source, 0, n_tensor - 1)[:, None] + jnp.arange(2)[None, :]
    idle = jnp.concatenate([start[1:2, :1], start[:-1, 1:]], axis=0)
    start = jnp.where(there[:, None], start, idle).reshape(-1).astype(jnp.int32)
    return start, there.astype(jnp.int32)


def add_shards(base, xs, plan, weight, down=None, slot=None, rank_part=0, only=None):
    rows, width = xs[0].shape
    half = width // 2
    columns = weight.shape[1]
    halves = 2 if only is None else 1
    steps = halves * len(xs)
    if only is not None:
        start = plan[0].reshape(-1, 2)[:, only]
        plan = (jnp.where(plan[1] != 0, start, start[::-1]), plan[1])

    def whole(a):
        return pl.BlockSpec((rows, a), lambda s, *_: (0, 0))

    def walked(a):
        return pl.BlockSpec((half, a.shape[1]), lambda s, start, valid: (start[s], 0))

    in_specs = [
        pl.BlockSpec((rows, half), lambda s, *_, i=i: (0, jnp.clip(s - 2 * i, 0, 1) if only is None else only))
        for i in range(len(xs))
    ] + [walked(weight)]
    out_shape = [jax.ShapeDtypeStruct((rows, columns), F32)]
    scratch = []
    slots = 0
    if base is None:
        slots = down.shape[1]
        in_specs += [walked(down), whole(1)]
        out_shape += [jax.ShapeDtypeStruct((rows, rank_part), F32)]
        scratch = [pltpu.VMEM((rows, slots), F32)]
        rest = (down, slot)
    else:
        in_specs += [whole(columns)]
        rest = (base,)
    return pl.pallas_call(
        functools.partial(shards_kernel, base is None, halves),
        out_shape=out_shape,
        grid_spec=pltpu.PrefetchScalarGridSpec(
            num_scalar_prefetch=2,
            grid=(steps,),
            in_specs=in_specs,
            out_specs=[whole(a.shape[1]) for a in out_shape],
            scratch_shapes=scratch,
        ),
        compiler_params=PARAMS,
        cost_estimate=pl.CostEstimate(flops=1, bytes_accessed=1, transcendentals=0),
    )(*plan, *xs, weight, *rest)


def half_kernel(start, valid, x, weight, base_in, base):
    step = pl.program_id(0)

    @pl.when(step == 0)
    def _():
        base[...] = base_in[...]

    @pl.when(valid[0] != 0)
    def _():
        part = min(base.shape[1], 512)
        for n in range(0, base.shape[1], part):
            base[:, n:n + part] += jnp.dot(x[...], weight[:, n:n + part], preferred_element_type=F32)


def add_half(base, x, valid, source, weight):
    rows, half = x.shape
    columns = weight.shape[1]
    step = half // 5
    whole = pl.BlockSpec((rows, columns), lambda s, *_: (0, 0))
    return pl.pallas_call(
        half_kernel,
        out_shape=jax.ShapeDtypeStruct((rows, columns), F32),
        grid_spec=pltpu.PrefetchScalarGridSpec(
            num_scalar_prefetch=2,
            grid=(half // step,),
            in_specs=[
                pl.BlockSpec((rows, step), lambda s, *_: (0, s)),
                pl.BlockSpec((step, columns), lambda s, source, valid: (source[0] * (columns // step) + s, 0)),
                whole,
            ],
            out_specs=whole,
        ),
        compiler_params=PARAMS,
        cost_estimate=pl.CostEstimate(flops=1, bytes_accessed=1, transcendentals=0),
    )(source, valid, x, weight, base)


def far_low_kernel(
    facts, left_1, left_2, right_1, right_2, down, other_down, slot, row_rank, low, other_low,
    out, near_x, far_x, rows_of, other_rows, sems
):
    me, end, source, upper = facts[0], facts[1], facts[2], facts[3]
    width = far_x.shape[1]
    rank_part = low.shape[1]
    start = pl.multiple_of(source * width, width)

    @pl.when(upper != 0)
    def _():
        pltpu.make_async_copy(left_2, far_x, sems.at[0]).start()
        pltpu.make_async_copy(left_1, near_x, sems.at[1]).start()

    @pl.when(upper == 0)
    def _():
        pltpu.make_async_copy(right_2, far_x, sems.at[0]).start()
        pltpu.make_async_copy(right_1, near_x, sems.at[1]).start()

    copies = [
        pltpu.make_async_copy(down.at[pl.ds(start, width)], rows_of, sems.at[2]),
        pltpu.make_async_copy(other_down, other_rows, sems.at[3]),
    ]
    for copy in copies:
        copy.start()
    pltpu.make_async_copy(left_2, far_x, sems.at[0]).wait()

    def finished(total, sums, place):
        sums = total[...] + fold_entry(sums, slot[...], rank_part)
        k = lax.broadcasted_iota(jnp.int32, sums.shape, 1) + place * rank_part
        return jnp.where(k < row_rank[...], sums, 0.0)

    copies[0].wait()
    own = finished(low, jnp.dot(far_x[...], rows_of[...], preferred_element_type=F32), me)
    pltpu.make_async_copy(left_1, near_x, sems.at[1]).wait()
    copies[1].wait()
    sums = jnp.zeros((far_x.shape[0], other_rows.shape[0]), F32)
    for x, place in ((far_x, 1 - upper), (near_x, upper)):
        rows = other_rows[:, pl.ds(pl.multiple_of(place * width, width), width)]
        sums += lax.dot_general(x[...], rows, (((1,), (1,)), ((), ())), preferred_element_type=F32)
    other = finished(other_low, sums, end)
    at_left = jnp.concatenate([other, own], axis=1)
    at_right = jnp.concatenate([own, other], axis=1)
    out[...] = jnp.where(upper != 0, at_right, at_left).astype(BF16)


def far_low(facts, left_1, left_2, right_1, right_2, down, other_down, slot, row_rank, low, other_low):
    rows, width = left_1.shape
    slots = down.shape[1]
    return pl.pallas_call(
        far_low_kernel,
        out_shape=jax.ShapeDtypeStruct((rows, 2 * low.shape[1]), BF16),
        in_specs=[pl.BlockSpec(memory_space=pltpu.SMEM)] + [IN_HBM] * 6 + [RESIDENT] * 4,
        out_specs=RESIDENT,
        scratch_shapes=[
            pltpu.VMEM((rows, width), BF16),
            pltpu.VMEM((rows, width), BF16),
            pltpu.VMEM((width, slots), BF16),
            pltpu.VMEM(other_down.shape, BF16),
            pltpu.SemaphoreType.DMA((4,)),
        ],
        compiler_params=TAIL_PARAMS,
        cost_estimate=pl.CostEstimate(flops=1, bytes_accessed=1, transcendentals=0),
    )(facts, left_1, left_2, right_1, right_2, in_hbm(down), other_down, slot, row_rank, low, other_low)


def prepare_kernel(facts, places, base, sent, received, weight, *refs):
    *blocks, slot, total, last_rows, mid, mid_rows, up, spread, sems = refs
    mid_width, last_width = mid_rows.shape[0], last_rows.shape[0]
    shard = total.shape[1]
    _, rank, _ = blocks[0].shape
    count = up.shape[0] // rank
    which, start = facts[0], (facts[1] + 1) * shard - mid_width - last_width
    part = min(total.shape[1], 512)

    def rows_at(first, length):
        return weight.at[pl.ds(pl.multiple_of(start + first, last_width), length)]

    to_total = pltpu.make_async_copy(base, total, sems.at[0])
    to_mid_rows = pltpu.make_async_copy(rows_at(0, mid_width), mid_rows, sems.at[1])
    to_last = pltpu.make_async_copy(rows_at(mid_width, last_width), last_rows, sems.at[2])
    pages = [up.at[pl.ds(e * rank, rank)] for e in range(count)]
    page_sems = [sems.at[4 + e] for e in range(count)]

    @pl.when(which == 0)
    def _():
        pltpu.make_async_copy(sent, mid, sems.at[3]).start()

    @pl.when(which != 0)
    def _():
        pltpu.make_async_copy(received, mid, sems.at[3]).start()

    to_total.start()
    start_pages(places, blocks, pages, page_sems, lambda page: page)

    @pl.when(which != 0)
    def _():
        to_mid_rows.start()
        to_last.start()

    pltpu.make_async_copy(sent, mid, sems.at[3]).wait()
    for e in range(count):
        spread[:, e * rank:(e + 1) * rank] = jnp.where(
            slot[...] == e, mid[:, mid_width:].astype(F32), 0.0
        ).astype(BF16)
    for page, sem in zip(pages, page_sems):
        pltpu.make_async_copy(blocks[0].at[0], page, sem).wait()
    to_total.wait()
    for n in range(0, total.shape[1], part):
        cut = slice(n, n + part)
        total[:, cut] += jnp.dot(spread[...], up[:, cut], preferred_element_type=F32)

    @pl.when(which != 0)
    def _():
        to_mid_rows.wait()
        for n in range(0, total.shape[1], part):
            cut = slice(n, n + part)
            total[:, cut] += jnp.dot(mid[:, :mid_width], mid_rows[:, cut], preferred_element_type=F32)
        to_last.wait()


def prepare(facts, places, base, sent, received, last_width, weight, blocks, slot):
    rows, columns = base.shape
    rank = blocks[0].shape[1]
    entries = places.shape[0]
    mid_width = sent.shape[1] - rank
    return pl.pallas_call(
        prepare_kernel,
        out_shape=[pltpu.VMEM((rows, columns), F32), pltpu.VMEM((last_width, columns), BF16)],
        in_specs=[pl.BlockSpec(memory_space=pltpu.SMEM)] * 2 + [IN_HBM] * (4 + len(blocks)) + [RESIDENT],
        out_specs=[RESIDENT] * 2,
        scratch_shapes=[
            pltpu.VMEM(sent.shape, BF16),
            pltpu.VMEM((mid_width, columns), BF16),
            pltpu.VMEM((entries * rank, columns), BF16),
            pltpu.VMEM((rows, entries * rank), BF16),
            pltpu.SemaphoreType.DMA((4 + entries,)),
        ],
        compiler_params=TAIL_PARAMS,
        cost_estimate=pl.CostEstimate(flops=1, bytes_accessed=1, transcendentals=0),
    )(facts, places, base, sent, received, weight, in_hbm(blocks[0]), *blocks[1:], slot)


def last_kernel(facts, total, weight, x, out):
    part = out.shape[1]
    cut = pl.ds(pl.multiple_of(pl.program_id(0) * part, part), part)

    @pl.when(facts[0] != 0)
    def _():
        out[...] = (total[:, cut] + jnp.dot(x[...], weight[:, cut], preferred_element_type=F32)).astype(BF16)

    @pl.when(facts[0] == 0)
    def _():
        out[...] = total[:, cut].astype(BF16)


def add_last(facts, total, weight, x):
    rows, columns = total.shape
    part = min(columns, 512)
    return pl.pallas_call(
        last_kernel,
        out_shape=jax.ShapeDtypeStruct((rows, columns), BF16),
        grid=(columns // part,),
        in_specs=[pl.BlockSpec(memory_space=pltpu.SMEM), RESIDENT, RESIDENT, pl.BlockSpec(x.shape, lambda n: (0, 0))],
        out_specs=pl.BlockSpec((rows, part), lambda n: (0, n)),
        compiler_params=TAIL_PARAMS,
        cost_estimate=pl.CostEstimate(flops=1, bytes_accessed=1, transcendentals=0),
    )(facts, total, weight, x)


def after(value, *earlier):
    return lax.optimization_barrier((value,) + earlier)[0]


def looked_up(table, ids):
    hit = ids[:, None] == jnp.arange(table.shape[0])[None, :]
    return jnp.sum(jnp.where(hit, table[None, :], 0), axis=1)


def local(
    attention_result,
    output_weight,
    adapter_down_weight,
    adapter_up_weight,
    adapter_page_row,
    requests,
    row_request_entry,
    ranks,
):
    n_dp = lax.axis_size("dp")
    n_tensor = lax.axis_size("tensor")
    me = lax.axis_index("tensor")
    rows, width = attention_result.shape
    holder_length, rank_part, _ = adapter_down_weight.shape
    rank, columns = adapter_up_weight.shape[1:]
    own_list = requests[0]
    entries = own_list.shape[0]
    one_hot = row_request_entry[:, None] == jnp.arange(entries)[None, :]
    row_rank = jnp.sum(jnp.where(one_hot, looked_up(ranks, own_list)[None, :], 0), axis=1)
    pages = looked_up(adapter_page_row, own_list)
    places = ((pages // holder_length) ^ lax.axis_index("dp")) * holder_length + pages % holder_length
    if n_tensor != 4 or n_dp != 4 or width % 512 or columns != width or rank_part % 16 or entries * rank_part > 256:
        return plain(
            attention_result, output_weight, adapter_down_weight, adapter_up_weight, places, one_hot, row_rank
        )


    def across(x, distance):
        return lax.ppermute(x, "dp", [(i, i ^ distance) for i in range(n_dp)])

    right = [(i, i + 1) for i in range(n_tensor - 1)]
    left = [(i + 1, i) for i in range(n_tensor - 1)]
    upper = me >= n_tensor // 2
    ends = me * (n_tensor - 1 - me) == 0
    slot = row_request_entry[:, None]
    farthest = jnp.where(upper, 0, n_tensor - 1)
    end = jnp.where(upper, n_tensor - 1, 0)
    source = jnp.where(upper, me - 2, me + 2)
    facts = jnp.stack([ends.astype(jnp.int32), farthest]).astype(jnp.int32)
    far_facts = jnp.stack([me, end, source, upper.astype(jnp.int32)]).astype(jnp.int32)
    near = plan_shards(me + jnp.array([0, -1, 1], jnp.int32), n_tensor)
    far = plan_shards(me + jnp.array([-2, 2], jnp.int32), n_tensor)

    right_1 = lax.ppermute(attention_result, "tensor", right)
    left_1 = lax.ppermute(attention_result, "tensor", left)
    far_down = across(adapter_down_weight, 2)
    far_up = across(adapter_up_weight, 2)
    near_down = across(adapter_down_weight, 1)

    right_1, left_1, places, slot, live, facts, far_facts, near, far, ended, started, is_upper = lax.optimization_barrier(
        (
            right_1, left_1, places, slot, row_rank[:, None], facts, far_facts, near, far,
            ends.astype(jnp.int32)[None], farthest.astype(jnp.int32)[None], upper.astype(jnp.int32)[None],
        )
    )
    right_2 = lax.ppermute(right_1, "tensor", right[1:])
    left_2 = lax.ppermute(left_1, "tensor", left[:-1])
    came = after(far_down, right_1, left_1)
    cuts = range(0, holder_length, max(holder_length // PIECES, 1))
    swapped = [across(came[i:i + cuts.step], 1) for i in cuts]
    downs = (adapter_down_weight, near_down, far_down, *swapped)
    down, other_down = join_downs(places, is_upper, downs, n_tensor)
    other_down = lax.ppermute(other_down, "tensor", [(0, 1), (3, 2)])

    base, low = add_shards(
        None, [attention_result, right_1, left_1], near, output_weight, down, slot, rank_part
    )
    right_2, left_2 = lax.optimization_barrier((base, right_2, left_2))[1:]
    third = right[-1:] + left[:1]
    cuts = (0, width // 8 * 5, width // 8 * 7, width)

    def piece(i):
        cut = slice(cuts[i], cuts[i + 1])
        return jnp.where(upper, right_2[:, cut], left_2[:, cut])

    first_2 = piece(0)
    first_3 = lax.ppermute(first_2, "tensor", third)
    right_2, left_2 = lax.optimization_barrier((first_2, right_2, left_2))[1:]
    middle = piece(1)
    other_low = lax.ppermute(after(low, middle), "tensor", [(0, 1), (3, 2)])
    base, = add_shards(base, [right_2, left_2], far, output_weight, only=0)
    right_2, left_2, other_down, other_low = lax.optimization_barrier(
        (base, right_2, left_2, other_down, other_low)
    )[1:]
    pair = far_low(
        far_facts, right_1, right_2, left_1, left_2, down, other_down, slot, live, low, other_low
    )
    from_middle = lax.ppermute(pair, "tensor", [(1, 2), (2, 1)])
    base, = add_shards(after(base, pair), [right_2, left_2], far, output_weight, only=1)
    low = jnp.where(upper, jnp.concatenate([from_middle, pair], axis=1), jnp.concatenate([pair, from_middle], axis=1))
    second_2 = jnp.concatenate([middle, low], axis=1)
    second_3 = lax.ppermute(second_2, "tensor", third)
    right_2, left_2 = lax.optimization_barrier((second_2, right_2, left_2))[1:]
    last_3 = lax.ppermute(piece(2), "tensor", third)
    ups = (adapter_up_weight, across(after(adapter_up_weight, far_down), 1), far_up, across(after(far_up, first_2), 1))
    base = add_half(base, first_3, ended, started, output_weight)
    total, rows_of = prepare(facts, places, base, second_2, second_3, width - cuts[2], output_weight, ups, slot)
    total, rows_of, last_3 = lax.optimization_barrier((total, rows_of, last_3))
    return add_last(facts, total, rows_of, last_3)


def gather_pages(block, n_dp):
    return [block] + [
        lax.ppermute(block, "dp", [(i, i ^ j) for i in range(n_dp)]) for j in range(1, n_dp)
    ]


def plain(x, output_weight, down_weight, up_weight, places, one_hot, row_rank):
    n_dp = lax.axis_size("dp")
    rows = x.shape[0]
    rank, columns = up_weight.shape[1:]
    entries = one_hot.shape[1]

    def requested(block):
        blocks = jnp.concatenate(gather_pages(block, n_dp), axis=0)
        return jnp.concatenate(
            [lax.dynamic_slice_in_dim(blocks, places[e], 1, 0) for e in range(entries)], axis=0
        )

    down, up = requested(down_weight), requested(up_weight)
    x = lax.all_gather(x, "tensor", axis=1, tiled=True)
    base = jnp.dot(x, output_weight, preferred_element_type=F32)
    low = jnp.einsum("rd,ekd->rek", x, down, preferred_element_type=F32)
    low = jnp.sum(jnp.where(one_hot[:, :, None], low, 0.0), axis=1).astype(BF16)
    low = lax.all_gather(low, "tensor", axis=1, tiled=True)
    low = jnp.where(jnp.arange(rank)[None, :] < row_rank[:, None], low, jnp.zeros_like(low))
    spread = jnp.where(one_hot[:, :, None], low[:, None, :], jnp.zeros((), BF16))
    term = jnp.dot(
        spread.reshape(rows, entries * rank), up.reshape(entries * rank, columns), preferred_element_type=F32
    )
    return (base + term).astype(BF16)


def solution(mesh):
    in_specs = (
        P(("groups", "dp"), "tensor"),
        P(None, "tensor"),
        P("dp", "tensor", None),
        P("dp", None, "tensor"),
        P("groups"),
        P(("groups", "dp"), None),
        P(("groups", "dp")),
        P(),
    )
    out_specs = P(("groups", "dp"), "tensor")
    return jax.shard_map(local, mesh=mesh, in_specs=in_specs, out_specs=out_specs, check_vma=False)
```

```python
import functools

import jax
import jax.numpy as jnp
from jax import lax
from jax.experimental import pallas as pl
from jax.experimental.pallas import tpu as pltpu
from jax.sharding import PartitionSpec as P

PARAMS = pltpu.CompilerParams(vmem_limit_bytes=48 * 2**20)
TAIL_PARAMS = pltpu.CompilerParams(vmem_limit_bytes=24 * 2**20)
F32 = jnp.float32
BF16 = jnp.bfloat16
PIECES = 2


def start_pages(places, blocks, targets, sems, rows_of):
    for e, target in enumerate(targets):
        first = 0
        for block in blocks:
            past = first + block.shape[0]

            @pl.when((places[e] >= first) & (places[e] < past))
            def _():
                pltpu.make_async_copy(rows_of(block.at[places[e] - first]), target, sems[e]).start()

            first = past


def join_downs_kernel(places, upper, *refs):
    *blocks, out, other, held, sems = refs
    _, rank_part, _ = blocks[0].shape
    shards, slots, width = held.shape
    entries = places.shape[0]
    step = pl.program_id(0)

    def targets(t):
        return [held.at[t, pl.ds(e * rank_part, rank_part)] for e in range(entries)]

    @pl.when(step == 0)
    def _():
        for t in range(shards):
            semaphores = [sems.at[t, e] for e in range(entries)]
            start_pages(
                places, blocks, targets(t), semaphores, lambda page: page.at[:, pl.ds(t * width, width)]
            )
            held[t, entries * rank_part:] = jnp.zeros((slots - entries * rank_part, width), BF16)

    for t in range(shards):

        @pl.when(step == t)
        def _():
            for e, target in enumerate(targets(t)):
                source = blocks[0].at[0, :, pl.ds(t * width, width)]
                pltpu.make_async_copy(source, target, sems.at[t, e]).wait()
            joined = held[t].T
            out[...] = joined
            half = shards // 2

            @pl.when((upper[0] != 0) == (t < half))
            def _():
                other[:, t % half * width:(t % half + 1) * width] = held[t, :entries * rank_part]


def join_downs(places, upper, blocks, shards):
    entries = places.shape[0]
    _, rank_part, features = blocks[0].shape
    width, slots = features // shards, -(-entries * rank_part // 128) * 128
    return pl.pallas_call(
        join_downs_kernel,
        out_shape=[
            jax.ShapeDtypeStruct((features, slots), BF16),
            jax.ShapeDtypeStruct((entries * rank_part, features // 2), BF16),
        ],
        grid=(shards,),
        in_specs=[pl.BlockSpec(memory_space=pltpu.SMEM)] * 2
        + [pl.BlockSpec(memory_space=pltpu.HBM)] * len(blocks),
        out_specs=[
            pl.BlockSpec((width, slots), lambda t: (t, 0)),
            pl.BlockSpec((entries * rank_part, features // 2), lambda t: (0, 0)),
        ],
        scratch_shapes=[pltpu.VMEM((shards, slots, width), BF16), pltpu.SemaphoreType.DMA((shards, entries))],
        compiler_params=TAIL_PARAMS,
        cost_estimate=pl.CostEstimate(flops=1, bytes_accessed=1, transcendentals=0),
    )(places, upper, *blocks)


RESIDENT = pl.BlockSpec(memory_space=pltpu.VMEM)


def in_hbm(a):
    return pltpu.with_memory_space_constraint(a, pltpu.HBM)


IN_HBM = pl.BlockSpec(memory_space=pltpu.HBM)


def fold_entry(low, slot, rank_part):
    lane = lax.broadcasted_iota(jnp.int32, low.shape, 1)
    own = jnp.where(lane // rank_part == slot, low, 0.0)
    shape = (low.shape[1], rank_part)
    fold = lax.rem(lax.broadcasted_iota(jnp.int32, shape, 0), rank_part) == lax.broadcasted_iota(jnp.int32, shape, 1)
    return jnp.dot(own, fold.astype(F32), precision=lax.Precision.HIGHEST, preferred_element_type=F32)


def shards_kernel(with_low, start, valid, *refs):
    refs = list(refs)
    xs = [refs.pop(0) for _ in range(valid.shape[0])]
    weight = refs.pop(0)
    if with_low:
        down, slot, base, low, acc = refs
    else:
        base_in, base = refs
    step = pl.program_id(0)

    @pl.when(step == 0)
    def _():
        base[...] = jnp.zeros_like(base) if with_low else base_in[...]
        if with_low:
            acc[...] = jnp.zeros_like(acc)

    for i, x in enumerate(xs):

        @pl.when((step // 2 == i) & (valid[i] != 0))
        def _():
            part = min(base.shape[1], 512)
            for n in range(0, base.shape[1], part):
                base[:, n:n + part] += jnp.dot(x[...], weight[:, n:n + part], preferred_element_type=F32)
            if with_low:
                acc[...] += jnp.dot(x[...], down[...], preferred_element_type=F32)

    if with_low:

        @pl.when(step == pl.num_programs(0) - 1)
        def _():
            low[...] = fold_entry(acc[...], slot[...], low.shape[1])


def plan_shards(source, n_tensor):
    there = (source >= 0) & (source < n_tensor)
    start = 2 * jnp.clip(source, 0, n_tensor - 1)[:, None] + jnp.arange(2)[None, :]
    idle = jnp.concatenate([start[1:2, :1], start[:-1, 1:]], axis=0)
    start = jnp.where(there[:, None], start, idle).reshape(-1).astype(jnp.int32)
    return start, there.astype(jnp.int32)


def add_shards(base, xs, plan, weight, down=None, slot=None, rank_part=0):
    rows, width = xs[0].shape
    half = width // 2
    columns = weight.shape[1]
    steps = 2 * len(xs)

    def whole(a):
        return pl.BlockSpec((rows, a), lambda s, *_: (0, 0))

    def walked(a):
        return pl.BlockSpec((half, a.shape[1]), lambda s, start, valid: (start[s], 0))

    in_specs = [
        pl.BlockSpec((rows, half), lambda s, *_, i=i: (0, jnp.clip(s - 2 * i, 0, 1))) for i in range(len(xs))
    ] + [walked(weight)]
    out_shape = [jax.ShapeDtypeStruct((rows, columns), F32)]
    scratch = []
    slots = 0
    if base is None:
        slots = down.shape[1]
        in_specs += [walked(down), whole(1)]
        out_shape += [jax.ShapeDtypeStruct((rows, rank_part), F32)]
        scratch = [pltpu.VMEM((rows, slots), F32)]
        rest = (down, slot)
    else:
        in_specs += [whole(columns)]
        rest = (base,)
    return pl.pallas_call(
        functools.partial(shards_kernel, base is None),
        out_shape=out_shape,
        grid_spec=pltpu.PrefetchScalarGridSpec(
            num_scalar_prefetch=2,
            grid=(steps,),
            in_specs=in_specs,
            out_specs=[whole(a.shape[1]) for a in out_shape],
            scratch_shapes=scratch,
        ),
        compiler_params=PARAMS,
        cost_estimate=pl.CostEstimate(flops=1, bytes_accessed=1, transcendentals=0),
    )(*plan, *xs, weight, *rest)


def far_kernel(start, valid, third_start, third_valid, left, right, third, weight, third_rows, base_in, base):
    step = pl.program_id(0)
    part = min(base.shape[1], 512)

    def add(x, rows):
        for n in range(0, base.shape[1], part):
            base[:, n:n + part] += jnp.dot(x[...], rows[:, n:n + part], preferred_element_type=F32)

    @pl.when(step == 0)
    def _():
        base[...] = base_in[...]

    for i, x in enumerate((left, right)):

        @pl.when((step // 2 == i) & (valid[i] != 0))
        def _():
            add(x, weight)

    @pl.when((step >= 4) & (third_valid[0] != 0))
    def _():
        add(third, third_rows)


def add_far(base, left, right, plan, third, third_start, third_valid, weight):
    rows, width = left.shape
    columns = weight.shape[1]
    half, unit = width // 2, width // 8
    pieces = third.shape[1] // unit
    whole = pl.BlockSpec((rows, columns), lambda s, *_: (0, 0))

    def piece(s, third_valid):
        return jnp.clip(s - 4, 0, pieces - 1) * third_valid[0]

    return pl.pallas_call(
        far_kernel,
        out_shape=jax.ShapeDtypeStruct((rows, columns), F32),
        grid_spec=pltpu.PrefetchScalarGridSpec(
            num_scalar_prefetch=4,
            grid=(4 + pieces,),
            in_specs=[
                pl.BlockSpec((rows, half), lambda s, *_: (0, jnp.clip(s, 0, 1))),
                pl.BlockSpec((rows, half), lambda s, *_: (0, jnp.clip(s - 2, 0, 1))),
                pl.BlockSpec((rows, unit), lambda s, a, b, c, d: (0, piece(s, d))),
                pl.BlockSpec((half, columns), lambda s, a, b, c, d: (a[jnp.clip(s, 0, 3)], 0)),
                pl.BlockSpec((unit, columns), lambda s, a, b, c, d: (c[0] * 8 + piece(s, d), 0)),
                whole,
            ],
            out_specs=whole,
        ),
        compiler_params=PARAMS,
        cost_estimate=pl.CostEstimate(flops=1, bytes_accessed=1, transcendentals=0),
    )(*plan, third_start, third_valid, left, right, third, weight, weight, base)


def far_low_kernel(
    facts, left_1, left_2, right_1, right_2, down, other_down, slot, row_rank, low, other_low,
    out, near_x, far_x, rows_of, other_rows, sems
):
    me, end, source, upper = facts[0], facts[1], facts[2], facts[3]
    width = far_x.shape[1]
    rank_part = low.shape[1]
    start = pl.multiple_of(source * width, width)

    @pl.when(upper != 0)
    def _():
        pltpu.make_async_copy(left_2, far_x, sems.at[0]).start()
        pltpu.make_async_copy(left_1, near_x, sems.at[1]).start()

    @pl.when(upper == 0)
    def _():
        pltpu.make_async_copy(right_2, far_x, sems.at[0]).start()
        pltpu.make_async_copy(right_1, near_x, sems.at[1]).start()

    copies = [
        pltpu.make_async_copy(down.at[pl.ds(start, width)], rows_of, sems.at[2]),
        pltpu.make_async_copy(other_down, other_rows, sems.at[3]),
    ]
    for copy in copies:
        copy.start()
    pltpu.make_async_copy(left_2, far_x, sems.at[0]).wait()

    def finished(total, sums, place):
        sums = total[...] + fold_entry(sums, slot[...], rank_part)
        k = lax.broadcasted_iota(jnp.int32, sums.shape, 1) + place * rank_part
        return jnp.where(k < row_rank[...], sums, 0.0)

    copies[0].wait()
    own = finished(low, jnp.dot(far_x[...], rows_of[...], preferred_element_type=F32), me)
    pltpu.make_async_copy(left_1, near_x, sems.at[1]).wait()
    copies[1].wait()
    sums = jnp.zeros((far_x.shape[0], other_rows.shape[0]), F32)
    for x, place in ((far_x, 1 - upper), (near_x, upper)):
        rows = other_rows[:, pl.ds(pl.multiple_of(place * width, width), width)]
        sums += lax.dot_general(x[...], rows, (((1,), (1,)), ((), ())), preferred_element_type=F32)
    other = finished(other_low, sums, end)
    at_left = jnp.concatenate([other, own], axis=1)
    at_right = jnp.concatenate([own, other], axis=1)
    out[...] = jnp.where(upper != 0, at_right, at_left).astype(BF16)


def far_low(facts, left_1, left_2, right_1, right_2, down, other_down, slot, row_rank, low, other_low):
    rows, width = left_1.shape
    slots = down.shape[1]
    return pl.pallas_call(
        far_low_kernel,
        out_shape=jax.ShapeDtypeStruct((rows, 2 * low.shape[1]), BF16),
        in_specs=[pl.BlockSpec(memory_space=pltpu.SMEM)] + [IN_HBM] * 6 + [RESIDENT] * 4,
        out_specs=RESIDENT,
        scratch_shapes=[
            pltpu.VMEM((rows, width), BF16),
            pltpu.VMEM((rows, width), BF16),
            pltpu.VMEM((width, slots), BF16),
            pltpu.VMEM(other_down.shape, BF16),
            pltpu.SemaphoreType.DMA((4,)),
        ],
        compiler_params=TAIL_PARAMS,
        cost_estimate=pl.CostEstimate(flops=1, bytes_accessed=1, transcendentals=0),
    )(facts, left_1, left_2, right_1, right_2, in_hbm(down), other_down, slot, row_rank, low, other_low)


def prepare_kernel(facts, places, base, sent, received, weight, *refs):
    *blocks, slot, total, last_rows, mid, mid_rows, up, spread, sems = refs
    mid_width, last_width = mid_rows.shape[0], last_rows.shape[0]
    shard = total.shape[1]
    _, rank, _ = blocks[0].shape
    count = up.shape[0] // rank
    which, start = facts[0], (facts[1] + 1) * shard - mid_width - last_width
    part = min(total.shape[1], 512)

    def rows_at(first, length):
        return weight.at[pl.ds(pl.multiple_of(start + first, last_width), length)]

    to_total = pltpu.make_async_copy(base, total, sems.at[0])
    to_mid_rows = pltpu.make_async_copy(rows_at(0, mid_width), mid_rows, sems.at[1])
    to_last = pltpu.make_async_copy(rows_at(mid_width, last_width), last_rows, sems.at[2])
    pages = [up.at[pl.ds(e * rank, rank)] for e in range(count)]
    page_sems = [sems.at[4 + e] for e in range(count)]

    @pl.when(which == 0)
    def _():
        pltpu.make_async_copy(sent, mid, sems.at[3]).start()

    @pl.when(which != 0)
    def _():
        pltpu.make_async_copy(received, mid, sems.at[3]).start()

    to_total.start()
    start_pages(places, blocks, pages, page_sems, lambda page: page)

    @pl.when(which != 0)
    def _():
        to_mid_rows.start()
        to_last.start()

    pltpu.make_async_copy(sent, mid, sems.at[3]).wait()
    for e in range(count):
        spread[:, e * rank:(e + 1) * rank] = jnp.where(
            slot[...] == e, mid[:, mid_width:].astype(F32), 0.0
        ).astype(BF16)
    for page, sem in zip(pages, page_sems):
        pltpu.make_async_copy(blocks[0].at[0], page, sem).wait()
    to_total.wait()
    for n in range(0, total.shape[1], part):
        cut = slice(n, n + part)
        total[:, cut] += jnp.dot(spread[...], up[:, cut], preferred_element_type=F32)

    @pl.when(which != 0)
    def _():
        to_mid_rows.wait()
        for n in range(0, total.shape[1], part):
            cut = slice(n, n + part)
            total[:, cut] += jnp.dot(mid[:, :mid_width], mid_rows[:, cut], preferred_element_type=F32)
        to_last.wait()


def prepare(facts, places, base, sent, received, last_width, weight, blocks, slot):
    rows, columns = base.shape
    rank = blocks[0].shape[1]
    entries = places.shape[0]
    mid_width = sent.shape[1] - rank
    return pl.pallas_call(
        prepare_kernel,
        out_shape=[pltpu.VMEM((rows, columns), F32), pltpu.VMEM((last_width, columns), BF16)],
        in_specs=[pl.BlockSpec(memory_space=pltpu.SMEM)] * 2 + [IN_HBM] * (4 + len(blocks)) + [RESIDENT],
        out_specs=[RESIDENT] * 2,
        scratch_shapes=[
            pltpu.VMEM(sent.shape, BF16),
            pltpu.VMEM((mid_width, columns), BF16),
            pltpu.VMEM((entries * rank, columns), BF16),
            pltpu.VMEM((rows, entries * rank), BF16),
            pltpu.SemaphoreType.DMA((4 + entries,)),
        ],
        compiler_params=TAIL_PARAMS,
        cost_estimate=pl.CostEstimate(flops=1, bytes_accessed=1, transcendentals=0),
    )(facts, places, base, sent, received, weight, in_hbm(blocks[0]), *blocks[1:], slot)


def last_kernel(facts, total, weight, x, out):
    part = out.shape[1]
    cut = pl.ds(pl.multiple_of(pl.program_id(0) * part, part), part)

    @pl.when(facts[0] != 0)
    def _():
        out[...] = (total[:, cut] + jnp.dot(x[...], weight[:, cut], preferred_element_type=F32)).astype(BF16)

    @pl.when(facts[0] == 0)
    def _():
        out[...] = total[:, cut].astype(BF16)


def add_last(facts, total, weight, x):
    rows, columns = total.shape
    part = min(columns, 512)
    return pl.pallas_call(
        last_kernel,
        out_shape=jax.ShapeDtypeStruct((rows, columns), BF16),
        grid=(columns // part,),
        in_specs=[pl.BlockSpec(memory_space=pltpu.SMEM), RESIDENT, RESIDENT, pl.BlockSpec(x.shape, lambda n: (0, 0))],
        out_specs=pl.BlockSpec((rows, part), lambda n: (0, n)),
        compiler_params=TAIL_PARAMS,
        cost_estimate=pl.CostEstimate(flops=1, bytes_accessed=1, transcendentals=0),
    )(facts, total, weight, x)


def after(value, *earlier):
    return lax.optimization_barrier((value,) + earlier)[0]


def looked_up(table, ids):
    hit = ids[:, None] == jnp.arange(table.shape[0])[None, :]
    return jnp.sum(jnp.where(hit, table[None, :], 0), axis=1)


def local(
    attention_result,
    output_weight,
    adapter_down_weight,
    adapter_up_weight,
    adapter_page_row,
    requests,
    row_request_entry,
    ranks,
):
    n_dp = lax.axis_size("dp")
    n_tensor = lax.axis_size("tensor")
    me = lax.axis_index("tensor")
    rows, width = attention_result.shape
    holder_length, rank_part, _ = adapter_down_weight.shape
    rank, columns = adapter_up_weight.shape[1:]
    own_list = requests[0]
    entries = own_list.shape[0]
    one_hot = row_request_entry[:, None] == jnp.arange(entries)[None, :]
    row_rank = jnp.sum(jnp.where(one_hot, looked_up(ranks, own_list)[None, :], 0), axis=1)
    pages = looked_up(adapter_page_row, own_list)
    places = ((pages // holder_length) ^ lax.axis_index("dp")) * holder_length + pages % holder_length
    if n_tensor != 4 or n_dp != 4 or width % 512 or columns != width or rank_part % 16 or entries * rank_part > 256:
        return plain(
            attention_result, output_weight, adapter_down_weight, adapter_up_weight, places, one_hot, row_rank
        )


    def across(x, distance):
        return lax.ppermute(x, "dp", [(i, i ^ distance) for i in range(n_dp)])

    right = [(i, i + 1) for i in range(n_tensor - 1)]
    left = [(i + 1, i) for i in range(n_tensor - 1)]
    upper = me >= n_tensor // 2
    ends = me * (n_tensor - 1 - me) == 0
    slot = row_request_entry[:, None]
    farthest = jnp.where(upper, 0, n_tensor - 1)
    end = jnp.where(upper, n_tensor - 1, 0)
    source = jnp.where(upper, me - 2, me + 2)
    facts = jnp.stack([ends.astype(jnp.int32), farthest]).astype(jnp.int32)
    far_facts = jnp.stack([me, end, source, upper.astype(jnp.int32)]).astype(jnp.int32)
    near = plan_shards(me + jnp.array([0, -1, 1], jnp.int32), n_tensor)
    far = plan_shards(me + jnp.array([-2, 2], jnp.int32), n_tensor)

    right_1 = lax.ppermute(attention_result, "tensor", right)
    left_1 = lax.ppermute(attention_result, "tensor", left)
    far_down = across(adapter_down_weight, 2)
    far_up = across(adapter_up_weight, 2)
    near_down = across(adapter_down_weight, 1)

    right_1, left_1, places, slot, live, facts, far_facts, near, far, ended, started, is_upper = lax.optimization_barrier(
        (
            right_1, left_1, places, slot, row_rank[:, None], facts, far_facts, near, far,
            ends.astype(jnp.int32)[None], farthest.astype(jnp.int32)[None], upper.astype(jnp.int32)[None],
        )
    )
    right_2 = lax.ppermute(right_1, "tensor", right[1:])
    left_2 = lax.ppermute(left_1, "tensor", left[:-1])
    came = after(far_down, right_1, left_1)
    cuts = range(0, holder_length, max(holder_length // PIECES, 1))
    swapped = [across(came[i:i + cuts.step], 1) for i in cuts]
    downs = (adapter_down_weight, near_down, far_down, *swapped)
    down, other_down = join_downs(places, is_upper, downs, n_tensor)
    other_down = lax.ppermute(other_down, "tensor", [(0, 1), (3, 2)])

    base, low = add_shards(
        None, [attention_result, right_1, left_1], near, output_weight, down, slot, rank_part
    )
    other_low = lax.ppermute(low, "tensor", [(0, 1), (3, 2)])

    right_2, left_2 = lax.optimization_barrier((base, right_2, left_2))[1:]
    third = right[-1:] + left[:1]
    cuts = (0, width // 8 * 5, width // 8 * 7, width)

    def piece(i):
        cut = slice(cuts[i], cuts[i + 1])
        return jnp.where(upper, right_2[:, cut], left_2[:, cut])

    first_2 = piece(0)
    first_3 = lax.ppermute(first_2, "tensor", third)
    right_2, left_2, other_down, other_low = lax.optimization_barrier(
        (first_2, right_2, left_2, other_down, other_low)
    )[1:]
    pair = far_low(
        far_facts, right_1, right_2, left_1, left_2, down, other_down, slot, live, low, other_low
    )
    from_middle = lax.ppermute(pair, "tensor", [(1, 2), (2, 1)])
    low = jnp.where(upper, jnp.concatenate([from_middle, pair], axis=1), jnp.concatenate([pair, from_middle], axis=1))
    second_2 = jnp.concatenate([piece(1), low], axis=1)
    second_3 = lax.ppermute(second_2, "tensor", third)
    right_2, left_2 = lax.optimization_barrier((second_2, right_2, left_2))[1:]
    last_3 = lax.ppermute(piece(2), "tensor", third)
    ups = (adapter_up_weight, across(after(adapter_up_weight, far_down), 1), far_up, across(after(far_up, first_2), 1))
    base = add_far(after(base, pair), right_2, left_2, far, first_3, started, ended, output_weight)
    total, rows_of = prepare(facts, places, base, second_2, second_3, width - cuts[2], output_weight, ups, slot)
    total, rows_of, last_3 = lax.optimization_barrier((total, rows_of, last_3))
    return add_last(facts, total, rows_of, last_3)


def gather_pages(block, n_dp):
    return [block] + [
        lax.ppermute(block, "dp", [(i, i ^ j) for i in range(n_dp)]) for j in range(1, n_dp)
    ]


def plain(x, output_weight, down_weight, up_weight, places, one_hot, row_rank):
    n_dp = lax.axis_size("dp")
    rows = x.shape[0]
    rank, columns = up_weight.shape[1:]
    entries = one_hot.shape[1]

    def requested(block):
        blocks = jnp.concatenate(gather_pages(block, n_dp), axis=0)
        return jnp.concatenate(
            [lax.dynamic_slice_in_dim(blocks, places[e], 1, 0) for e in range(entries)], axis=0
        )

    down, up = requested(down_weight), requested(up_weight)
    x = lax.all_gather(x, "tensor", axis=1, tiled=True)
    base = jnp.dot(x, output_weight, preferred_element_type=F32)
    low = jnp.einsum("rd,ekd->rek", x, down, preferred_element_type=F32)
    low = jnp.sum(jnp.where(one_hot[:, :, None], low, 0.0), axis=1).astype(BF16)
    low = lax.all_gather(low, "tensor", axis=1, tiled=True)
    low = jnp.where(jnp.arange(rank)[None, :] < row_rank[:, None], low, jnp.zeros_like(low))
    spread = jnp.where(one_hot[:, :, None], low[:, None, :], jnp.zeros((), BF16))
    term = jnp.dot(
        spread.reshape(rows, entries * rank), up.reshape(entries * rank, columns), preferred_element_type=F32
    )
    return (base + term).astype(BF16)


def solution(mesh):
    in_specs = (
        P(("groups", "dp"), "tensor"),
        P(None, "tensor"),
        P("dp", "tensor", None),
        P("dp", None, "tensor"),
        P("groups"),
        P(("groups", "dp"), None),
        P(("groups", "dp")),
        P(),
    )
    out_specs = P(("groups", "dp"), "tensor")
    return jax.shard_map(local, mesh=mesh, in_specs=in_specs, out_specs=out_specs, check_vma=False)
```

```python
import functools

import jax
import jax.numpy as jnp
from jax import lax
from jax.experimental import pallas as pl
from jax.experimental.pallas import tpu as pltpu
from jax.sharding import PartitionSpec as P

PARAMS = pltpu.CompilerParams(vmem_limit_bytes=48 * 2**20)
TAIL_PARAMS = pltpu.CompilerParams(vmem_limit_bytes=24 * 2**20)
F32 = jnp.float32
BF16 = jnp.bfloat16
PIECES = 2


def start_pages(places, blocks, targets, sems, rows_of):
    for e, target in enumerate(targets):
        first = 0
        for block in blocks:
            past = first + block.shape[0]

            @pl.when((places[e] >= first) & (places[e] < past))
            def _():
                pltpu.make_async_copy(rows_of(block.at[places[e] - first]), target, sems[e]).start()

            first = past


def join_downs_kernel(places, upper, *refs):
    *blocks, out, other, held, sems = refs
    _, rank_part, _ = blocks[0].shape
    shards, slots, width = held.shape
    entries = places.shape[0]
    step = pl.program_id(0)

    def targets(t):
        return [held.at[t, pl.ds(e * rank_part, rank_part)] for e in range(entries)]

    @pl.when(step == 0)
    def _():
        for t in range(shards):
            semaphores = [sems.at[t, e] for e in range(entries)]
            start_pages(
                places, blocks, targets(t), semaphores, lambda page: page.at[:, pl.ds(t * width, width)]
            )
            held[t, entries * rank_part:] = jnp.zeros((slots - entries * rank_part, width), BF16)

    for t in range(shards):

        @pl.when(step == t)
        def _():
            for e, target in enumerate(targets(t)):
                source = blocks[0].at[0, :, pl.ds(t * width, width)]
                pltpu.make_async_copy(source, target, sems.at[t, e]).wait()
            joined = held[t].T
            out[...] = joined
            half = shards // 2

            @pl.when((upper[0] != 0) == (t < half))
            def _():
                other[:, t % half * width:(t % half + 1) * width] = held[t, :entries * rank_part]


def join_downs(places, upper, blocks, shards):
    entries = places.shape[0]
    _, rank_part, features = blocks[0].shape
    width, slots = features // shards, -(-entries * rank_part // 128) * 128
    return pl.pallas_call(
        join_downs_kernel,
        out_shape=[
            jax.ShapeDtypeStruct((features, slots), BF16),
            jax.ShapeDtypeStruct((entries * rank_part, features // 2), BF16),
        ],
        grid=(shards,),
        in_specs=[pl.BlockSpec(memory_space=pltpu.SMEM)] * 2
        + [pl.BlockSpec(memory_space=pltpu.HBM)] * len(blocks),
        out_specs=[
            pl.BlockSpec((width, slots), lambda t: (t, 0)),
            pl.BlockSpec((entries * rank_part, features // 2), lambda t: (0, 0)),
        ],
        scratch_shapes=[pltpu.VMEM((shards, slots, width), BF16), pltpu.SemaphoreType.DMA((shards, entries))],
        compiler_params=TAIL_PARAMS,
        cost_estimate=pl.CostEstimate(flops=1, bytes_accessed=1, transcendentals=0),
    )(places, upper, *blocks)


RESIDENT = pl.BlockSpec(memory_space=pltpu.VMEM)


def in_hbm(a):
    return pltpu.with_memory_space_constraint(a, pltpu.HBM)


IN_HBM = pl.BlockSpec(memory_space=pltpu.HBM)


def fold_entry(low, slot, rank_part):
    lane = lax.broadcasted_iota(jnp.int32, low.shape, 1)
    own = jnp.where(lane // rank_part == slot, low, 0.0)
    shape = (low.shape[1], rank_part)
    fold = lax.rem(lax.broadcasted_iota(jnp.int32, shape, 0), rank_part) == lax.broadcasted_iota(jnp.int32, shape, 1)
    return jnp.dot(own, fold.astype(F32), precision=lax.Precision.HIGHEST, preferred_element_type=F32)


def shards_kernel(with_low, start, valid, *refs):
    refs = list(refs)
    xs = [refs.pop(0) for _ in range(valid.shape[0])]
    weight = refs.pop(0)
    if with_low:
        down, slot, base, low, acc = refs
    else:
        base_in, base = refs
    step = pl.program_id(0)

    @pl.when(step == 0)
    def _():
        base[...] = jnp.zeros_like(base) if with_low else base_in[...]
        if with_low:
            acc[...] = jnp.zeros_like(acc)

    for i, x in enumerate(xs):

        @pl.when((step // 2 == i) & (valid[i] != 0))
        def _():
            part = min(base.shape[1], 512)
            for n in range(0, base.shape[1], part):
                base[:, n:n + part] += jnp.dot(x[...], weight[:, n:n + part], preferred_element_type=F32)
            if with_low:
                acc[...] += jnp.dot(x[...], down[...], preferred_element_type=F32)

    if with_low:

        @pl.when(step == pl.num_programs(0) - 1)
        def _():
            low[...] = fold_entry(acc[...], slot[...], low.shape[1])


def plan_shards(source, n_tensor):
    there = (source >= 0) & (source < n_tensor)
    start = 2 * jnp.clip(source, 0, n_tensor - 1)[:, None] + jnp.arange(2)[None, :]
    idle = jnp.concatenate([start[1:2, :1], start[:-1, 1:]], axis=0)
    start = jnp.where(there[:, None], start, idle).reshape(-1).astype(jnp.int32)
    return start, there.astype(jnp.int32)


def add_shards(base, xs, plan, weight, down=None, slot=None, rank_part=0):
    rows, width = xs[0].shape
    half = width // 2
    columns = weight.shape[1]
    steps = 2 * len(xs)

    def whole(a):
        return pl.BlockSpec((rows, a), lambda s, *_: (0, 0))

    def walked(a):
        return pl.BlockSpec((half, a.shape[1]), lambda s, start, valid: (start[s], 0))

    in_specs = [
        pl.BlockSpec((rows, half), lambda s, *_, i=i: (0, jnp.clip(s - 2 * i, 0, 1))) for i in range(len(xs))
    ] + [walked(weight)]
    out_shape = [jax.ShapeDtypeStruct((rows, columns), F32)]
    scratch = []
    slots = 0
    if base is None:
        slots = down.shape[1]
        in_specs += [walked(down), whole(1)]
        out_shape += [jax.ShapeDtypeStruct((rows, rank_part), F32)]
        scratch = [pltpu.VMEM((rows, slots), F32)]
        rest = (down, slot)
    else:
        in_specs += [whole(columns)]
        rest = (base,)
    return pl.pallas_call(
        functools.partial(shards_kernel, base is None),
        out_shape=out_shape,
        grid_spec=pltpu.PrefetchScalarGridSpec(
            num_scalar_prefetch=2,
            grid=(steps,),
            in_specs=in_specs,
            out_specs=[whole(a.shape[1]) for a in out_shape],
            scratch_shapes=scratch,
        ),
        compiler_params=PARAMS,
        cost_estimate=pl.CostEstimate(flops=1, bytes_accessed=1, transcendentals=0),
    )(*plan, *xs, weight, *rest)


def half_kernel(start, valid, x, weight, base_in, base):
    step = pl.program_id(0)

    @pl.when(step == 0)
    def _():
        base[...] = base_in[...]

    @pl.when(valid[0] != 0)
    def _():
        part = min(base.shape[1], 512)
        for n in range(0, base.shape[1], part):
            base[:, n:n + part] += jnp.dot(x[...], weight[:, n:n + part], preferred_element_type=F32)


def add_half(base, x, valid, source, weight):
    rows, half = x.shape
    columns = weight.shape[1]
    step = half // 5
    whole = pl.BlockSpec((rows, columns), lambda s, *_: (0, 0))
    return pl.pallas_call(
        half_kernel,
        out_shape=jax.ShapeDtypeStruct((rows, columns), F32),
        grid_spec=pltpu.PrefetchScalarGridSpec(
            num_scalar_prefetch=2,
            grid=(half // step,),
            in_specs=[
                pl.BlockSpec((rows, step), lambda s, source, valid: (0, s * valid[0])),
                pl.BlockSpec((step, columns), lambda s, source, valid: (source[0] * (columns // step) + s * valid[0], 0)),
                whole,
            ],
            out_specs=whole,
        ),
        compiler_params=PARAMS,
        cost_estimate=pl.CostEstimate(flops=1, bytes_accessed=1, transcendentals=0),
    )(source, valid, x, weight, base)


def far_low_kernel(
    facts, left_1, left_2, right_1, right_2, down, other_down, slot, row_rank, low, other_low,
    out, near_x, far_x, rows_of, other_rows, sems
):
    me, end, source, upper = facts[0], facts[1], facts[2], facts[3]
    width = far_x.shape[1]
    rank_part = low.shape[1]
    start = pl.multiple_of(source * width, width)

    @pl.when(upper != 0)
    def _():
        pltpu.make_async_copy(left_2, far_x, sems.at[0]).start()
        pltpu.make_async_copy(left_1, near_x, sems.at[1]).start()

    @pl.when(upper == 0)
    def _():
        pltpu.make_async_copy(right_2, far_x, sems.at[0]).start()
        pltpu.make_async_copy(right_1, near_x, sems.at[1]).start()

    copies = [
        pltpu.make_async_copy(down.at[pl.ds(start, width)], rows_of, sems.at[2]),
        pltpu.make_async_copy(other_down, other_rows, sems.at[3]),
    ]
    for copy in copies:
        copy.start()
    pltpu.make_async_copy(left_2, far_x, sems.at[0]).wait()

    def finished(total, sums, place):
        sums = total[...] + fold_entry(sums, slot[...], rank_part)
        k = lax.broadcasted_iota(jnp.int32, sums.shape, 1) + place * rank_part
        return jnp.where(k < row_rank[...], sums, 0.0)

    copies[0].wait()
    own = finished(low, jnp.dot(far_x[...], rows_of[...], preferred_element_type=F32), me)
    pltpu.make_async_copy(left_1, near_x, sems.at[1]).wait()
    copies[1].wait()
    sums = jnp.zeros((far_x.shape[0], other_rows.shape[0]), F32)
    for x, place in ((far_x, 1 - upper), (near_x, upper)):
        rows = other_rows[:, pl.ds(pl.multiple_of(place * width, width), width)]
        sums += lax.dot_general(x[...], rows, (((1,), (1,)), ((), ())), preferred_element_type=F32)
    other = finished(other_low, sums, end)
    at_left = jnp.concatenate([other, own], axis=1)
    at_right = jnp.concatenate([own, other], axis=1)
    out[...] = jnp.where(upper != 0, at_right, at_left).astype(BF16)


def far_low(facts, left_1, left_2, right_1, right_2, down, other_down, slot, row_rank, low, other_low):
    rows, width = left_1.shape
    slots = down.shape[1]
    return pl.pallas_call(
        far_low_kernel,
        out_shape=jax.ShapeDtypeStruct((rows, 2 * low.shape[1]), BF16),
        in_specs=[pl.BlockSpec(memory_space=pltpu.SMEM)] + [IN_HBM] * 6 + [RESIDENT] * 4,
        out_specs=RESIDENT,
        scratch_shapes=[
            pltpu.VMEM((rows, width), BF16),
            pltpu.VMEM((rows, width), BF16),
            pltpu.VMEM((width, slots), BF16),
            pltpu.VMEM(other_down.shape, BF16),
            pltpu.SemaphoreType.DMA((4,)),
        ],
        compiler_params=TAIL_PARAMS,
        cost_estimate=pl.CostEstimate(flops=1, bytes_accessed=1, transcendentals=0),
    )(facts, left_1, left_2, right_1, right_2, in_hbm(down), other_down, slot, row_rank, low, other_low)


def prepare_kernel(facts, places, base, sent, received, weight, *refs):
    *blocks, slot, total, last_rows, mid, mid_rows, up, spread, sems = refs
    mid_width, last_width = mid_rows.shape[0], last_rows.shape[0]
    shard = total.shape[1]
    _, rank, _ = blocks[0].shape
    count = up.shape[0] // rank
    which, start = facts[0], (facts[1] + 1) * shard - mid_width - last_width
    part = min(total.shape[1], 512)

    def rows_at(first, length):
        return weight.at[pl.ds(pl.multiple_of(start + first, last_width), length)]

    to_total = pltpu.make_async_copy(base, total, sems.at[0])
    to_mid_rows = pltpu.make_async_copy(rows_at(0, mid_width), mid_rows, sems.at[1])
    to_last = pltpu.make_async_copy(rows_at(mid_width, last_width), last_rows, sems.at[2])
    pages = [up.at[pl.ds(e * rank, rank)] for e in range(count)]
    page_sems = [sems.at[4 + e] for e in range(count)]

    @pl.when(which == 0)
    def _():
        pltpu.make_async_copy(sent, mid, sems.at[3]).start()

    @pl.when(which != 0)
    def _():
        pltpu.make_async_copy(received, mid, sems.at[3]).start()

    to_total.start()
    start_pages(places, blocks, pages, page_sems, lambda page: page)

    @pl.when(which != 0)
    def _():
        to_mid_rows.start()
        to_last.start()

    pltpu.make_async_copy(sent, mid, sems.at[3]).wait()
    for e in range(count):
        spread[:, e * rank:(e + 1) * rank] = jnp.where(
            slot[...] == e, mid[:, mid_width:].astype(F32), 0.0
        ).astype(BF16)
    for page, sem in zip(pages, page_sems):
        pltpu.make_async_copy(blocks[0].at[0], page, sem).wait()
    to_total.wait()
    for n in range(0, total.shape[1], part):
        cut = slice(n, n + part)
        total[:, cut] += jnp.dot(spread[...], up[:, cut], preferred_element_type=F32)

    @pl.when(which != 0)
    def _():
        to_mid_rows.wait()
        for n in range(0, total.shape[1], part):
            cut = slice(n, n + part)
            total[:, cut] += jnp.dot(mid[:, :mid_width], mid_rows[:, cut], preferred_element_type=F32)
        to_last.wait()


def prepare(facts, places, base, sent, received, last_width, weight, blocks, slot):
    rows, columns = base.shape
    rank = blocks[0].shape[1]
    entries = places.shape[0]
    mid_width = sent.shape[1] - rank
    return pl.pallas_call(
        prepare_kernel,
        out_shape=[pltpu.VMEM((rows, columns), F32), pltpu.VMEM((last_width, columns), BF16)],
        in_specs=[pl.BlockSpec(memory_space=pltpu.SMEM)] * 2 + [IN_HBM] * (4 + len(blocks)) + [RESIDENT],
        out_specs=[RESIDENT] * 2,
        scratch_shapes=[
            pltpu.VMEM(sent.shape, BF16),
            pltpu.VMEM((mid_width, columns), BF16),
            pltpu.VMEM((entries * rank, columns), BF16),
            pltpu.VMEM((rows, entries * rank), BF16),
            pltpu.SemaphoreType.DMA((4 + entries,)),
        ],
        compiler_params=TAIL_PARAMS,
        cost_estimate=pl.CostEstimate(flops=1, bytes_accessed=1, transcendentals=0),
    )(facts, places, base, sent, received, weight, in_hbm(blocks[0]), *blocks[1:], slot)


def last_kernel(facts, total, weight, x, out):
    part = out.shape[1]
    cut = pl.ds(pl.multiple_of(pl.program_id(0) * part, part), part)

    @pl.when(facts[0] != 0)
    def _():
        out[...] = (total[:, cut] + jnp.dot(x[...], weight[:, cut], preferred_element_type=F32)).astype(BF16)

    @pl.when(facts[0] == 0)
    def _():
        out[...] = total[:, cut].astype(BF16)


def add_last(facts, total, weight, x):
    rows, columns = total.shape
    part = min(columns, 512)
    return pl.pallas_call(
        last_kernel,
        out_shape=jax.ShapeDtypeStruct((rows, columns), BF16),
        grid=(columns // part,),
        in_specs=[pl.BlockSpec(memory_space=pltpu.SMEM), RESIDENT, RESIDENT, pl.BlockSpec(x.shape, lambda n: (0, 0))],
        out_specs=pl.BlockSpec((rows, part), lambda n: (0, n)),
        compiler_params=TAIL_PARAMS,
        cost_estimate=pl.CostEstimate(flops=1, bytes_accessed=1, transcendentals=0),
    )(facts, total, weight, x)


def after(value, *earlier):
    return lax.optimization_barrier((value,) + earlier)[0]


def looked_up(table, ids):
    hit = ids[:, None] == jnp.arange(table.shape[0])[None, :]
    return jnp.sum(jnp.where(hit, table[None, :], 0), axis=1)


def local(
    attention_result,
    output_weight,
    adapter_down_weight,
    adapter_up_weight,
    adapter_page_row,
    requests,
    row_request_entry,
    ranks,
):
    n_dp = lax.axis_size("dp")
    n_tensor = lax.axis_size("tensor")
    me = lax.axis_index("tensor")
    rows, width = attention_result.shape
    holder_length, rank_part, _ = adapter_down_weight.shape
    rank, columns = adapter_up_weight.shape[1:]
    own_list = requests[0]
    entries = own_list.shape[0]
    one_hot = row_request_entry[:, None] == jnp.arange(entries)[None, :]
    row_rank = jnp.sum(jnp.where(one_hot, looked_up(ranks, own_list)[None, :], 0), axis=1)
    pages = looked_up(adapter_page_row, own_list)
    places = ((pages // holder_length) ^ lax.axis_index("dp")) * holder_length + pages % holder_length
    if n_tensor != 4 or n_dp != 4 or width % 512 or columns != width or rank_part % 16 or entries * rank_part > 256:
        return plain(
            attention_result, output_weight, adapter_down_weight, adapter_up_weight, places, one_hot, row_rank
        )


    def across(x, distance):
        return lax.ppermute(x, "dp", [(i, i ^ distance) for i in range(n_dp)])

    right = [(i, i + 1) for i in range(n_tensor - 1)]
    left = [(i + 1, i) for i in range(n_tensor - 1)]
    upper = me >= n_tensor // 2
    ends = me * (n_tensor - 1 - me) == 0
    slot = row_request_entry[:, None]
    farthest = jnp.where(upper, 0, n_tensor - 1)
    end = jnp.where(upper, n_tensor - 1, 0)
    source = jnp.where(upper, me - 2, me + 2)
    facts = jnp.stack([ends.astype(jnp.int32), farthest]).astype(jnp.int32)
    far_facts = jnp.stack([me, end, source, upper.astype(jnp.int32)]).astype(jnp.int32)
    near = plan_shards(me + jnp.array([0, -1, 1], jnp.int32), n_tensor)
    far = plan_shards(me + jnp.array([-2, 2], jnp.int32), n_tensor)

    right_1 = lax.ppermute(attention_result, "tensor", right)
    left_1 = lax.ppermute(attention_result, "tensor", left)
    far_down = across(adapter_down_weight, 2)
    far_up = across(adapter_up_weight, 2)
    near_down = across(adapter_down_weight, 1)

    right_1, left_1, places, slot, live, facts, far_facts, near, far, ended, started, is_upper = lax.optimization_barrier(
        (
            right_1, left_1, places, slot, row_rank[:, None], facts, far_facts, near, far,
            ends.astype(jnp.int32)[None], farthest.astype(jnp.int32)[None], upper.astype(jnp.int32)[None],
        )
    )
    right_2 = lax.ppermute(right_1, "tensor", right[1:])
    left_2 = lax.ppermute(left_1, "tensor", left[:-1])
    came = after(far_down, right_1, left_1)
    cuts = range(0, holder_length, max(holder_length // PIECES, 1))
    swapped = [across(came[i:i + cuts.step], 1) for i in cuts]
    downs = (adapter_down_weight, near_down, far_down, *swapped)
    down, other_down = join_downs(places, is_upper, downs, n_tensor)
    other_down = lax.ppermute(other_down, "tensor", [(0, 1), (3, 2)])

    base, low = add_shards(
        None, [attention_result, right_1, left_1], near, output_weight, down, slot, rank_part
    )
    other_low = lax.ppermute(low, "tensor", [(0, 1), (3, 2)])

    right_2, left_2 = lax.optimization_barrier((base, right_2, left_2))[1:]
    third = right[-1:] + left[:1]
    cuts = (0, width // 8 * 5, width // 8 * 7, width)

    def piece(i):
        cut = slice(cuts[i], cuts[i + 1])
        return jnp.where(upper, right_2[:, cut], left_2[:, cut])

    first_2 = piece(0)
    first_3 = lax.ppermute(first_2, "tensor", third)
    right_2, left_2, other_down, other_low = lax.optimization_barrier(
        (first_2, right_2, left_2, other_down, other_low)
    )[1:]
    pair = far_low(
        far_facts, right_1, right_2, left_1, left_2, down, other_down, slot, live, low, other_low
    )
    from_middle = lax.ppermute(pair, "tensor", [(1, 2), (2, 1)])
    base, = add_shards(after(base, pair), [right_2, left_2], far, output_weight)
    low = jnp.where(upper, jnp.concatenate([from_middle, pair], axis=1), jnp.concatenate([pair, from_middle], axis=1))
    second_2 = jnp.concatenate([piece(1), low], axis=1)
    second_3 = lax.ppermute(second_2, "tensor", third)
    right_2, left_2 = lax.optimization_barrier((second_2, right_2, left_2))[1:]
    last_3 = lax.ppermute(piece(2), "tensor", third)
    ups = (adapter_up_weight, across(after(adapter_up_weight, far_down), 1), far_up, across(after(far_up, first_2), 1))
    base = add_half(base, first_3, ended, started, output_weight)
    total, rows_of = prepare(facts, places, base, second_2, second_3, width - cuts[2], output_weight, ups, slot)
    total, rows_of, last_3 = lax.optimization_barrier((total, rows_of, last_3))
    return add_last(facts, total, rows_of, last_3)


def gather_pages(block, n_dp):
    return [block] + [
        lax.ppermute(block, "dp", [(i, i ^ j) for i in range(n_dp)]) for j in range(1, n_dp)
    ]


def plain(x, output_weight, down_weight, up_weight, places, one_hot, row_rank):
    n_dp = lax.axis_size("dp")
    rows = x.shape[0]
    rank, columns = up_weight.shape[1:]
    entries = one_hot.shape[1]

    def requested(block):
        blocks = jnp.concatenate(gather_pages(block, n_dp), axis=0)
        return jnp.concatenate(
            [lax.dynamic_slice_in_dim(blocks, places[e], 1, 0) for e in range(entries)], axis=0
        )

    down, up = requested(down_weight), requested(up_weight)
    x = lax.all_gather(x, "tensor", axis=1, tiled=True)
    base = jnp.dot(x, output_weight, preferred_element_type=F32)
    low = jnp.einsum("rd,ekd->rek", x, down, preferred_element_type=F32)
    low = jnp.sum(jnp.where(one_hot[:, :, None], low, 0.0), axis=1).astype(BF16)
    low = lax.all_gather(low, "tensor", axis=1, tiled=True)
    low = jnp.where(jnp.arange(rank)[None, :] < row_rank[:, None], low, jnp.zeros_like(low))
    spread = jnp.where(one_hot[:, :, None], low[:, None, :], jnp.zeros((), BF16))
    term = jnp.dot(
        spread.reshape(rows, entries * rank), up.reshape(entries * rank, columns), preferred_element_type=F32
    )
    return (base + term).astype(BF16)


def solution(mesh):
    in_specs = (
        P(("groups", "dp"), "tensor"),
        P(None, "tensor"),
        P("dp", "tensor", None),
        P("dp", None, "tensor"),
        P("groups"),
        P(("groups", "dp"), None),
        P(("groups", "dp")),
        P(),
    )
    out_specs = P(("groups", "dp"), "tensor")
    return jax.shard_map(local, mesh=mesh, in_specs=in_specs, out_specs=out_specs, check_vma=False)
```
